32 devices in a mesh: rows: 8 (over y, x, core), chan: 4 (over z).
Axes of the slice: x: 2, y: 2, z: 4, core: 2. Of those that a mesh axis runs over, the one named last changes fastest.
Arguments:
- pixels: float32 [64, 2, 64, 512], P('rows', None, None, 'chan')
- cotangent: bfloat16 [64, 2, 64, 512], P('rows', None, None, 'chan'), may hold values from -6 to 6
- loss_weight: float32 [2], replicated, may hold values from 0.5 to 2
- timesteps: int32 [2], replicated, may hold values from 0 to 999
- clip_embed: float32 [2, 2048], replicated, may hold values from -6 to 6
- context: bfloat16 [2, 81, 2048], replicated, may hold values from -6 to 6
- text_len: int32 [2], replicated, may hold values from 1 to 77
- conv_first: float32 [9, 512, 512], P(None, 'rows', 'chan'), may hold values from -0.09375 to 0.09375
- conv_first_moment: float32 [9, 512, 512], P(None, 'rows', 'chan')
- conv_first_square: float32 [9, 512, 512], P(None, 'rows', 'chan'), as said below
- conv_second: float32 [9, 512, 512], P(None, 'rows', 'chan'), may hold values from -0.09375 to 0.09375
- conv_second_moment: float32 [9, 512, 512], P(None, 'rows', 'chan')
- conv_second_square: float32 [9, 512, 512], P(None, 'rows', 'chan')
- qkv_weight: float32 [512, 3, 512], P('rows', None, 'chan'), may hold values from -0.25 to 0.25
- qkv_weight_moment: float32 [512, 3, 512], P('rows', None, 'chan')
- qkv_weight_square: float32 [512, 3, 512], P('rows', None, 'chan')
- out_weight: float32 [512, 512], P('rows', 'chan'), may hold values from -4 to 4
- out_weight_moment: float32 [512, 512], P('rows', 'chan')
- out_weight_square: float32 [512, 512], P('rows', 'chan')
- embed_weight: float32 [2048, 2, 512], P('rows', None, 'chan'), may hold values from -0.0625 to 0.0625
- embed_weight_moment: float32 [2048, 2, 512], P('rows', None, 'chan')
- embed_weight_square: float32 [2048, 2, 512], P('rows', None, 'chan')
- context_weight: float32 [2048, 2, 512], P('rows', None, 'chan'), may hold values from -0.125 to 0.125
- context_weight_moment: float32 [2048, 2, 512], P('rows', None, 'chan')
- context_weight_square: float32 [2048, 2, 512], P('rows', None, 'chan')
- vectors: float32 [14, 512], P(None, 'chan')
- vectors_moment: float32 [14, 512], P(None, 'chan')
- vectors_square: float32 [14, 512], P(None, 'chan')
Outputs:
- activations: bfloat16 [64, 2, 64, 512], P('rows', None, None, 'chan')
- pixel_grad: float32 [64, 2, 64, 512], P('rows', None, None, 'chan')
- grad_norm: float32 [], replicated
- conv_first_new: float32 [9, 512, 512], P(None, 'rows', 'chan')
- conv_first_moment_new: float32 [9, 512, 512], P(None, 'rows', 'chan')
- conv_first_square_new: float32 [9, 512, 512], P(None, 'rows', 'chan')
- conv_first_low: bfloat16 [9, 512, 512], P(None, 'rows', 'chan')
- conv_second_new: float32 [9, 512, 512], P(None, 'rows', 'chan')
- conv_second_moment_new: float32 [9, 512, 512], P(None, 'rows', 'chan')
- conv_second_square_new: float32 [9, 512, 512], P(None, 'rows', 'chan')
- conv_second_low: bfloat16 [9, 512, 512], P(None, 'rows', 'chan')
- qkv_weight_new: float32 [512, 3, 512], P('rows', None, 'chan')
- qkv_weight_moment_new: float32 [512, 3, 512], P('rows', None, 'chan')
- qkv_weight_square_new: float32 [512, 3, 512], P('rows', None, 'chan')
- qkv_weight_low: bfloat16 [512, 3, 512], P('rows', None, 'chan')
- out_weight_new: float32 [512, 512], P('rows', 'chan')
- out_weight_moment_new: float32 [512, 512], P('rows', 'chan')
- out_weight_square_new: float32 [512, 512], P('rows', 'chan')
- out_weight_low: bfloat16 [512, 512], P('rows', 'chan')
- embed_weight_new: float32 [2048, 2, 512], P('rows', None, 'chan')
- embed_weight_moment_new: float32 [2048, 2, 512], P('rows', None, 'chan')
- embed_weight_square_new: float32 [2048, 2, 512], P('rows', None, 'chan')
- embed_weight_low: bfloat16 [2048, 2, 512], P('rows', None, 'chan')
- context_weight_new: float32 [2048, 2, 512], P('rows', None, 'chan')
- context_weight_moment_new: float32 [2048, 2, 512], P('rows', None, 'chan')
- context_weight_square_new: float32 [2048, 2, 512], P('rows', None, 'chan')
- context_weight_low: bfloat16 [2048, 2, 512], P('rows', None, 'chan')
- vectors_new: float32 [14, 512], P(None, 'chan')
- vectors_moment_new: float32 [14, 512], P(None, 'chan')
- vectors_square_new: float32 [14, 512], P(None, 'chan')
The draws below stay inside these ranges and needn't reach their ends.
Inputs may be any that keep to these rules, and one draw needn't show every extreme that they name: `conv_first_square`: second moments are positive.
All inputs are finite; a program needn't handle non-finite values.
Results may differ from the reference program's by a relative error of at most 0.018.
The reference program's roundings to bfloat16 on the way count: a program that leaves them out, or rounds other values in their place, can miss the bound.
Values may be sent and summed in bfloat16 or wider, within the bound.
No kernel may reach another device: no remote copies, remote signals or barrier semaphores. Data moves between devices by JAX's collectives and lax.ppermute only.
A program may use at most 384 MiB of HBM per device.

```python
import math
import jax
import jax.numpy as jnp
import numpy as np
from jax import lax

C = 512
GROUPS = 32
HEADS = 8
HEAD_DIM = 64
EMB = 2048
DCTX = 2048
IMG_H = 64
IMG_W = 64
CLIP_TOK = 4
TEXT = 77
STEP = 10
IMAGES = 2
CTX = 81
NP = 9968640


def first_moment(key, shape, factor):
    spread = factor * 0.11 / math.sqrt(NP)
    return jax.random.normal(key, shape, jnp.float32) * spread


def second_moment(key, shape, factor):
    baseline = 0.001 * factor * factor / NP
    return baseline * jnp.exp(jax.random.uniform(key, shape, jnp.float32, 0.0, math.log(4.0)))


def draw_pixels(key, part):
    key = jax.random.fold_in(key, 3)
    row_ramp = jnp.arange(IMG_H, dtype=jnp.float32) / (IMG_H - 1)
    growth = 2.0
    base_values = jax.random.normal(key, (IMG_H, IMAGES, IMG_W, C), jnp.float32)
    return base_values * (1.0 + growth * row_ramp)[:, None, None, None] + 0.3


def draw_vectors(key, part):
    key = jax.random.fold_in(key, 5)
    jitter_key, bias_key = jax.random.split(key)
    channel_ramp = jnp.arange(C, dtype=jnp.float32) / (C - 1)
    growth = 2.0
    biases = 0.5 * jax.random.normal(bias_key, (14, C), jnp.float32)
    jitter_values = jax.random.uniform(jitter_key, (3, C), jnp.float32, 0.85, 1.15)
    rising = (1.0 + growth * channel_ramp)[None, :] * jitter_values[:2]
    third_gain = (0.8 + 0.6 * channel_ramp) * jitter_values[2]
    stacked = [rising[0], biases[1], biases[2], rising[1], biases[4], biases[5], third_gain, biases[7], biases[8], biases[9], biases[10], biases[11], biases[12], biases[13]]
    return jnp.stack(stacked)


def draw_conv_first_moment(key, part):
    key = jax.random.fold_in(key, 11)
    return first_moment(key, (9, C, C), 1.0)


def draw_conv_first_square(key, part):
    key = jax.random.fold_in(key, 12)
    return second_moment(key, (9, C, C), 1.0)


def draw_conv_second_moment(key, part):
    key = jax.random.fold_in(key, 13)
    return first_moment(key, (9, C, C), 1.0)


def draw_conv_second_square(key, part):
    key = jax.random.fold_in(key, 14)
    return second_moment(key, (9, C, C), 1.0)


def draw_qkv_weight_moment(key, part):
    key = jax.random.fold_in(key, 15)
    return first_moment(key, (C, 3, C), 1.0)


def draw_qkv_weight_square(key, part):
    key = jax.random.fold_in(key, 16)
    return second_moment(key, (C, 3, C), 1.0)


def draw_out_weight_moment(key, part):
    key = jax.random.fold_in(key, 17)
    return first_moment(key, (C, C), 0.25)


def draw_out_weight_square(key, part):
    key = jax.random.fold_in(key, 18)
    return second_moment(key, (C, C), 0.25)


def draw_embed_weight_moment(key, part):
    key = jax.random.fold_in(key, 19)
    return first_moment(key, (EMB, 2, C), 1.0)


def draw_embed_weight_square(key, part):
    key = jax.random.fold_in(key, 20)
    return second_moment(key, (EMB, 2, C), 1.0)


def draw_context_weight_moment(key, part):
    key = jax.random.fold_in(key, 21)
    return first_moment(key, (DCTX, 2, C), 0.35)


def draw_context_weight_square(key, part):
    key = jax.random.fold_in(key, 22)
    return second_moment(key, (DCTX, 2, C), 0.35)


def draw_vectors_moment(key, part):
    key = jax.random.fold_in(key, 23)
    return first_moment(key, (14, C), 3.0)


def draw_vectors_square(key, part):
    key = jax.random.fold_in(key, 24)
    return second_moment(key, (14, C), 3.0)


def shard_levels(rng, dims, cuts, least, top_value):
    loudness = 1.0
    for axis_at, parts in cuts:
        heights = jax.random.uniform(jax.random.fold_in(jax.random.fold_in(rng, 6), axis_at), (parts,), jnp.float32, least / len(cuts), top_value / len(cuts))
        loudness = loudness * jnp.repeat(jnp.exp(heights), dims[axis_at] // parts).reshape((-1,) + (1,) * (len(dims) - 1 - axis_at))
    return loudness


def rank_bounds(amount, slope):
    loads = [(1 << 20) // math.isqrt(rank ** slope) + 1 for rank in range(1, amount + 1)]
    deviation = 1 + sum(loads) // (1 << 30)
    return np.cumsum(np.array([max(1, weight // deviation) for weight in loads]))


def skewed_ids(stream_key, extent, count, skew):
    grid = rank_bounds(count, skew)
    ticket = jax.random.randint(jax.random.fold_in(stream_key, 1), extent, 0, int(grid[count - 1]))
    standing = jnp.searchsorted(jnp.asarray(grid, jnp.int32), ticket, side="right")
    return jax.random.permutation(jax.random.fold_in(stream_key, 2), count)[standing].astype(jnp.int32)


def noise(stream_key, dims, deviation, limit, cuts=(), kind=jnp.bfloat16):
    drawn = deviation * jax.random.normal(stream_key, dims, jnp.float32)
    if cuts:
        drawn = drawn * shard_levels(stream_key, dims, cuts, -0.22, 0.18)
    return jnp.clip(drawn, -limit, limit).astype(kind)


def setup_inputs(seed: int = 0) -> dict:
    arg_keys = jax.random.split(jax.random.key(seed), 29)
    pixels = draw_pixels(jax.random.fold_in(arg_keys[28], 71), 0)
    cotangent = noise(arg_keys[1], (IMG_H, IMAGES, IMG_W, C), 1.0, 6.0, ((0, 8), (3, 4)))
    loss_weight = jnp.clip(jnp.exp(jax.random.uniform(arg_keys[2], (IMAGES,), jnp.float32, math.log(0.5), math.log(2.0))), 0.5, 2.0)
    timesteps = skewed_ids(arg_keys[3], (IMAGES,), 1000, 2)
    clip_embed = noise(arg_keys[4], (IMAGES, EMB), 1.0, 6.0, (), jnp.float32)
    context = noise(arg_keys[5], (IMAGES, CTX, DCTX), 1.0, 6.0)
    text_len = jax.random.randint(arg_keys[6], (IMAGES,), 1, TEXT + 1).astype(jnp.int32)
    conv_first = noise(arg_keys[7], (9, C, C), (9 * C) ** -0.5, 0.09375, ((1, 8), (2, 4)), jnp.float32)
    conv_first_moment = draw_conv_first_moment(jax.random.fold_in(arg_keys[28], 71), 0)
    conv_first_square = draw_conv_first_square(jax.random.fold_in(arg_keys[28], 71), 0)
    conv_second = noise(arg_keys[10], (9, C, C), (9 * C) ** -0.5, 0.09375, ((1, 8), (2, 4)), jnp.float32)
    conv_second_moment = draw_conv_second_moment(jax.random.fold_in(arg_keys[28], 71), 0)
    conv_second_square = draw_conv_second_square(jax.random.fold_in(arg_keys[28], 71), 0)
    qkv_weight = noise(arg_keys[13], (C, 3, C), C ** -0.5, 0.25, ((0, 8), (2, 4)), jnp.float32)
    qkv_weight_moment = draw_qkv_weight_moment(jax.random.fold_in(arg_keys[28], 71), 0)
    qkv_weight_square = draw_qkv_weight_square(jax.random.fold_in(arg_keys[28], 71), 0)
    out_weight = noise(arg_keys[16], (C, C), 2 ** -0.5, 4.0, ((0, 8), (1, 4)), jnp.float32)
    out_weight_moment = draw_out_weight_moment(jax.random.fold_in(arg_keys[28], 71), 0)
    out_weight_square = draw_out_weight_square(jax.random.fold_in(arg_keys[28], 71), 0)
    embed_weight = noise(arg_keys[19], (EMB, 2, C), (4 * EMB) ** -0.5, 0.0625, ((0, 8), (2, 4)), jnp.float32)
    embed_weight_moment = draw_embed_weight_moment(jax.random.fold_in(arg_keys[28], 71), 0)
    embed_weight_square = draw_embed_weight_square(jax.random.fold_in(arg_keys[28], 71), 0)
    context_weight = noise(arg_keys[22], (DCTX, 2, C), DCTX ** -0.5, 0.125, ((0, 8), (2, 4)), jnp.float32)
    context_weight_moment = draw_context_weight_moment(jax.random.fold_in(arg_keys[28], 71), 0)
    context_weight_square = draw_context_weight_square(jax.random.fold_in(arg_keys[28], 71), 0)
    vectors = draw_vectors(jax.random.fold_in(arg_keys[28], 71), 0)
    vectors_moment = draw_vectors_moment(jax.random.fold_in(arg_keys[28], 71), 0)
    vectors_square = draw_vectors_square(jax.random.fold_in(arg_keys[28], 71), 0)
    return {"pixels": pixels, "cotangent": cotangent, "loss_weight": loss_weight, "timesteps": timesteps, "clip_embed": clip_embed, "context": context, "text_len": text_len, "conv_first": conv_first, "conv_first_moment": conv_first_moment, "conv_first_square": conv_first_square, "conv_second": conv_second, "conv_second_moment": conv_second_moment, "conv_second_square": conv_second_square, "qkv_weight": qkv_weight, "qkv_weight_moment": qkv_weight_moment, "qkv_weight_square": qkv_weight_square, "out_weight": out_weight, "out_weight_moment": out_weight_moment, "out_weight_square": out_weight_square, "embed_weight": embed_weight, "embed_weight_moment": embed_weight_moment, "embed_weight_square": embed_weight_square, "context_weight": context_weight, "context_weight_moment": context_weight_moment, "context_weight_square": context_weight_square, "vectors": vectors, "vectors_moment": vectors_moment, "vectors_square": vectors_square}


highest = lax.Precision.HIGHEST
clip_limit = 1.0

@jax.custom_vjp
def low(v):
    return lax.optimization_barrier(v.astype(jnp.bfloat16)).astype(jnp.float32)

@jax.custom_vjp
def low_back(v):
    return v

def low_keep(v):
    return (low(v), None)

def low_pass(kept, grad):
    return (grad,)

def back_keep(v):
    return (v, None)

def back_low(kept, grad):
    return (low(grad),)
low.defvjp(low_keep, low_pass)
low_back.defvjp(back_keep, back_low)

def time_features(timesteps):
    half_width = EMB // 2
    frequency = jnp.exp(-math.log(10000.0) * jnp.arange(half_width, dtype=jnp.float32) / half_width)
    phases = timesteps.astype(jnp.float32)[:, None] * frequency[None, :]
    return jnp.concatenate((jnp.cos(phases), jnp.sin(phases)), axis=1)

def group_norm(values, gain, offset):
    height, images, image_width, channels = values.shape
    grouped = values.reshape(height, images, image_width, GROUPS, channels // GROUPS)
    average = lax.optimization_barrier(jnp.mean(grouped, axis=(0, 2, 4), keepdims=True))
    squares = lax.optimization_barrier(jnp.mean(grouped * grouped, axis=(0, 2, 4), keepdims=True))
    inverse = lax.rsqrt(squares - average * average + 1e-05)
    return ((grouped - average) * inverse).reshape(values.shape) * gain + offset

def conv_layer(values, kernel):
    images_first = jnp.transpose(values, (1, 0, 2, 3))
    kernel_taps = kernel.reshape(3, 3, kernel.shape[1], kernel.shape[2])
    result = lax.conv_general_dilated(images_first, kernel_taps, (1, 1), ((1, 1), (1, 1)), dimension_numbers=('NHWC', 'HWIO', 'NHWC'), precision=highest)
    return jnp.transpose(result, (1, 0, 2, 3))

def attend_image(inputs):
    queries, keys_all, values_all, ctx_keys, ctx_values, allowed = inputs
    tokens = queries.shape[0]
    key_heads = keys_all.reshape(tokens, HEADS, HEAD_DIM)
    value_heads = values_all.reshape(tokens, HEADS, HEAD_DIM)
    ctx_key_heads = ctx_keys.reshape(CTX, HEADS, HEAD_DIM)
    ctx_value_heads = ctx_values.reshape(CTX, HEADS, HEAD_DIM)
    query_blocks = queries.reshape(tokens // 512, 512, HEADS, HEAD_DIM)

    def one_block(query_block):
        pixel_scores = low_back(jnp.einsum('qhd,khd->hqk', query_block, key_heads, precision=highest) * 0.125)
        ctx_scores = low_back(jnp.einsum('qhd,khd->hqk', query_block, ctx_key_heads, precision=highest) * 0.125)
        ctx_scores = jnp.where(allowed[None, None, :], ctx_scores, -1e+30)
        peak_score = jnp.maximum(lax.optimization_barrier(jnp.max(pixel_scores, axis=2)), lax.optimization_barrier(jnp.max(ctx_scores, axis=2)))[:, :, None]
        pixel_weights = jnp.exp(pixel_scores - peak_score)
        ctx_weights = jnp.exp(ctx_scores - peak_score)
        weight_sum = lax.optimization_barrier(jnp.sum(pixel_weights, axis=2)) + lax.optimization_barrier(jnp.sum(ctx_weights, axis=2))
        mixture = jnp.einsum('hqk,khd->qhd', pixel_weights, value_heads, precision=highest)
        mixture = mixture + jnp.einsum('hqk,khd->qhd', ctx_weights, ctx_value_heads, precision=highest)
        return (mixture / jnp.transpose(weight_sum)[:, :, None]).reshape(512, C)
    return lax.map(jax.checkpoint(one_block), query_blocks).reshape(tokens, C)

def attention(queries, keys_all, values_all, ctx_keys, ctx_values, allowed):
    height, images, image_width, channels = queries.shape

    def per_image(values):
        return jnp.transpose(values, (1, 0, 2, 3)).reshape(images, height * image_width, channels)
    mixture = lax.map(attend_image, (per_image(queries), per_image(keys_all), per_image(values_all), ctx_keys, ctx_values, allowed))
    return jnp.transpose(mixture.reshape(images, height, image_width, channels), (1, 0, 2, 3))

def adamw(weight, moment, square, gradient, step_rate, weight_decay):
    moment_new = 0.9 * moment + 0.1 * gradient
    square_new = 0.999 * square + 0.001 * gradient * gradient
    corrected = moment_new / (1.0 - 0.9 ** STEP)
    scaled = square_new / (1.0 - 0.999 ** STEP)
    weight_new = weight - step_rate * (corrected / (jnp.sqrt(scaled) + 1e-08) + weight_decay * weight)
    return (weight_new, moment_new, square_new)

def reference(pixels, cotangent, loss_weight, timesteps, clip_embed, context, text_len, conv_first, conv_first_moment, conv_first_square, conv_second, conv_second_moment, conv_second_square, qkv_weight, qkv_weight_moment, qkv_weight_square, out_weight, out_weight_moment, out_weight_square, embed_weight, embed_weight_moment, embed_weight_square, context_weight, context_weight_moment, context_weight_square, vectors, vectors_moment, vectors_square):
    embedding = low(jax.nn.silu(time_features(timesteps) + clip_embed))
    context_wide = context.astype(jnp.float32)
    allowed = jnp.arange(CTX, dtype=jnp.int32)[None, :] < (CLIP_TOK + text_len)[:, None]

    def forward(image_in, kernel_one, kernel_two, qkv_in, out_in, embed_in, context_in, vector_in):
        active_one = low(jax.nn.silu(group_norm(image_in, vector_in[0], vector_in[1])))
        hidden_one = low_back(conv_layer(active_one, kernel_one)) + vector_in[2]
        modulation = jnp.einsum('be,esc->bsc', embedding, embed_in, precision=highest)
        scale_rows = modulation[:, 0] + vector_in[12]
        shift_rows = modulation[:, 1] + vector_in[13]
        shaped = group_norm(hidden_one, vector_in[3], vector_in[4]) * (1.0 + scale_rows[None, :, None, :]) + shift_rows[None, :, None, :]
        active_two = low(jax.nn.silu(shaped))
        residual = image_in + (low_back(conv_layer(active_two, kernel_two)) + vector_in[5])
        normed = low(group_norm(residual, vector_in[6], vector_in[7]))
        projected = jnp.einsum('hbwc,csd->hbwsd', normed, qkv_in, precision=highest)
        queries = low_back(low(projected[:, :, :, 0] + vector_in[8]))
        keys_all = low_back(low(projected[:, :, :, 1]))
        values_all = low_back(low(projected[:, :, :, 2] + vector_in[9]))
        ctx_projected = jnp.einsum('bte,esc->btsc', context_wide, context_in, precision=highest)
        ctx_keys = low_back(low(ctx_projected[:, :, 0]))
        ctx_values = low_back(low(ctx_projected[:, :, 1] + vector_in[11]))
        attended = low_back(low(attention(queries, keys_all, values_all, ctx_keys, ctx_values, allowed)))
        channels = attended.shape[3]
        outward = jnp.dot(attended.reshape(-1, channels), out_in, precision=highest, preferred_element_type=jnp.float32)
        outward = low_back(outward).reshape(attended.shape)
        return residual + (outward + vector_in[10])
    output, pullback = jax.vjp(forward, pixels, low(conv_first), low(conv_second), low(qkv_weight), low(out_weight), low(embed_weight), low(context_weight), vectors)
    grad_out = cotangent.astype(jnp.float32) * loss_weight[None, :, None, None]
    gradients = pullback(grad_out)
    pixel_grad = gradients[0]
    squared = jnp.zeros((), jnp.float32)
    for member in gradients[1:]:
        squared = squared + jnp.sum(member * member)
    grad_norm = jnp.sqrt(squared)
    factor = jnp.minimum(1.0, clip_limit / grad_norm)
    conv_one = adamw(conv_first, conv_first_moment, conv_first_square, gradients[1] * factor, 0.02, 0.01)
    conv_two = adamw(conv_second, conv_second_moment, conv_second_square, gradients[2] * factor, 0.02, 0.01)
    qkv_new = adamw(qkv_weight, qkv_weight_moment, qkv_weight_square, gradients[3] * factor, 0.08, 0.01)
    out_new = adamw(out_weight, out_weight_moment, out_weight_square, gradients[4] * factor, 1.0, 0.01)
    embed_new = adamw(embed_weight, embed_weight_moment, embed_weight_square, gradients[5] * factor, 0.02, 0.01)
    context_new = adamw(context_weight, context_weight_moment, context_weight_square, gradients[6] * factor, 0.04, 0.01)
    vector_new = adamw(vectors, vectors_moment, vectors_square, gradients[7] * factor, 1.0, 0.0)
    return (output.astype(jnp.bfloat16), pixel_grad, grad_norm, conv_one[0], conv_one[1], conv_one[2], conv_one[0].astype(jnp.bfloat16), conv_two[0], conv_two[1], conv_two[2], conv_two[0].astype(jnp.bfloat16), qkv_new[0], qkv_new[1], qkv_new[2], qkv_new[0].astype(jnp.bfloat16), out_new[0], out_new[1], out_new[2], out_new[0].astype(jnp.bfloat16), embed_new[0], embed_new[1], embed_new[2], embed_new[0].astype(jnp.bfloat16), context_new[0], context_new[1], context_new[2], context_new[0].astype(jnp.bfloat16), vector_new[0], vector_new[1], vector_new[2])
```

```python
import functools
import math

import jax
import jax.numpy as jnp
from jax import lax
from jax.experimental import pallas as pl
from jax.experimental.pallas import tpu as pltpu
from jax.sharding import PartitionSpec as P

C = 512
GROUPS = 32
HEAD_DIM = 64
EMB = 2048
DCTX = 2048
IMG_H = 64
IMG_W = 64
CLIP_TOK = 4
STEP = 10
CTX = 81
CTX_PAD = 128
GROUP_SIZE = C // GROUPS
GROUP_COUNT = IMG_H * IMG_W * GROUP_SIZE
LOG2E = 1.4426950408889634
BF = jnp.bfloat16
F32 = jnp.float32
ORDER = (0, 1, 3, 2)

clip_limit = 1.0


def swap(x, axis, distance):
    size = lax.axis_size(axis)
    return lax.ppermute(x, axis, [(i, i ^ distance) for i in range(size)])


def rows_sum(x):
    size = lax.axis_size("rows")
    x = x + swap(x, "rows", 1)
    step = 2
    while step < size:
        if step * 4 <= size:
            one, two, three = (swap(x, "rows", step * k) for k in (1, 2, 3))
            x = (x + one) + (two + three)
            step *= 4
        else:
            x = x + swap(x, "rows", step)
            step *= 2
    return x


def chan_sum(x):
    one, two, three = (swap(x, "chan", k) for k in (1, 2, 3))
    return (x + one) + (two + three)


def chan_blocks(x):
    far = swap(x, "chan", 3)
    near = swap(x, "chan", 1)
    return (x, near, far, swap(far, "chan", 1))


def rims(x):
    size = lax.axis_size("rows")
    up = [(i, i + 1) for i in range(size - 1)]
    down = [(j, i) for i, j in up]
    before = lax.ppermute(x[-1:], "rows", up)
    after = lax.ppermute(x[:1], "rows", down)
    return jnp.concatenate([before, after], axis=0)


def chan_blocks_with_rims(x):
    edge = rims(x)
    return chan_blocks(x) + chan_blocks(edge)


def chan_scatter(parts):
    got = swap(parts[2:4], "chan", 1)
    middle = (parts[1].astype(F32) + got[1].astype(F32)).astype(BF)
    return parts[0], got[0], swap(middle, "chan", 3)


def pick(x, index, axis=0):
    return lax.dynamic_index_in_dim(x, index, axis, keepdims=False)


def pair_exchange(x, pair):
    count = x.shape[0]
    return [pick(x, pair)] + [swap(pick(x, pair ^ k), "rows", 2 * k) for k in range(1, count)]


def weight_scatter(x):
    size = lax.axis_size("rows")
    taps, height, width = x.shape
    share = height // size
    row = lax.axis_index("rows")
    core, pair = row % 2, row // 2
    count = size // 2
    split = x.reshape(taps, count, 2, share, width)
    mine = pick(split, core, 2)
    other = swap(pick(split, 1 - core, 2), "rows", 1)
    both = mine.astype(F32) + other.astype(F32)
    low = both.astype(BF)
    total = pick(both, pair, 1)
    for k in range(1, count):
        total = total + swap(pick(low, pair ^ k, 1), "rows", 2 * k).astype(F32)
    return total


def local_call(kernel, outs, *args, scratch=(), flops=0):
    def spec(a):
        return pl.BlockSpec(memory_space=pltpu.SMEM if a.dtype == jnp.int32 else pltpu.VMEM)

    size = sum(math.prod(a.shape) * a.dtype.itemsize for a in (*args, *outs))
    return pl.pallas_call(
        kernel,
        out_shape=tuple(outs),
        in_specs=[spec(a) for a in args],
        out_specs=tuple(pl.BlockSpec(memory_space=pltpu.VMEM) for _ in outs),
        scratch_shapes=list(scratch),
        compiler_params=pltpu.CompilerParams(vmem_limit_bytes=50 * 1024 * 1024),
        cost_estimate=pl.CostEstimate(flops=flops, bytes_accessed=size, transcendentals=0),
    )(*args)


def out(shape, dtype):
    return jax.ShapeDtypeStruct(shape, dtype)


def nn(a, b):
    return lax.dot_general(a, b, (((1,), (0,)), ((), ())), preferred_element_type=F32)


def nt(a, b):
    return lax.dot_general(a, b, (((1,), (1,)), ((), ())), preferred_element_type=F32)


def group_mean(x):
    width = x.shape[1]
    left = lax.broadcasted_iota(jnp.int32, (width, width), 0) // GROUP_SIZE
    right = lax.broadcasted_iota(jnp.int32, (width, width), 1) // GROUP_SIZE
    same = (left == right).astype(F32)
    total = lax.dot_general(
        x, same, (((1,), (0,)), ((), ())), precision=lax.Precision.HIGHEST, preferred_element_type=F32
    )
    return total * (1.0 / GROUP_COUNT)


def moments(sums, images):
    means = group_mean(sums)
    average = means[:images]
    return average, lax.rsqrt(means[images:] - average * average + 1e-05)


def image_of(ref, b):
    rows, _, width, channels = ref.shape
    return ref[:, b].reshape(rows * width, channels)


def put_image(ref, b, value):
    rows, _, width, channels = ref.shape
    ref[:, b] = value.reshape(rows, width, channels).astype(ref.dtype)


def column_sum(x):
    return jnp.sum(x, axis=0, keepdims=True)


def silu(z):
    return z * jax.nn.sigmoid(z)


def silu_slope(z):
    s = jax.nn.sigmoid(z)
    return s * (1.0 + z * (1.0 - s))


def norm_kernel(x, sums, vec, o, *, gain, offset, active):
    images = x.shape[1]
    average, inverse = moments(sums[...], images)
    for b in range(images):
        z = (image_of(x, b) - average[b : b + 1]) * inverse[b : b + 1]
        z = z * vec[gain : gain + 1] + vec[offset : offset + 1]
        put_image(o, b, silu(z) if active else z)


def modulated(x, average, inverse, mod, vec, b, images):
    xhat = (x - average[b : b + 1]) * inverse[b : b + 1]
    scale = mod[b : b + 1] + vec[12:13]
    shift = mod[images + b : images + b + 1] + vec[13:14]
    return xhat, (xhat * vec[3:4] + vec[4:5]) * (1.0 + scale) + shift


def act_two_kernel(x, sums, mod, vec, o):
    images = x.shape[1]
    average, inverse = moments(sums[...], images)
    for b in range(images):
        _, shaped = modulated(image_of(x, b), average, inverse, mod, vec, b, images)
        put_image(o, b, silu(shaped))


def fill(xs, blocks, edges):
    rows, images, width, channels = blocks[0].shape
    span = images * width
    for j in range(4):
        lanes = slice(j * channels, (j + 1) * channels)
        if edges is None:
            xs[:, lanes] = blocks[j][...].reshape(rows * span, channels)
        else:
            xs[0:span, lanes] = edges[j][0].reshape(span, channels)
            xs[span : span + rows * span, lanes] = blocks[j][...].reshape(rows * span, channels)
            xs[span + rows * span :, lanes] = edges[j][1].reshape(span, channels)


def rows_of(z, j, width):
    return pl.ds(pl.multiple_of((z ^ ORDER[j]) * width, width), width)


def shifted(x, by, width):
    length = x.shape[0]
    column = lax.broadcasted_iota(jnp.int32, x.shape, 0) % width
    moved = pltpu.roll(x, by % length, 0)
    return jnp.where(column == (0 if by == 1 else width - 1), 0.0, moved)


def conv_taps(xs, w, z, rows, span, width, flipped):
    channels = w.shape[2]
    parts = []
    for dx in range(3):
        total = None
        for dy in range(3):
            at = (2 - dy if flipped else dy) * span
            a = xs[at : at + rows * span, :]
            taps = [w[3 * dy + dx, rows_of(z, j, channels), :] for j in range(4)]
            if flipped:
                term = nt(a, jnp.concatenate(taps, axis=1))
            else:
                term = nn(a, jnp.concatenate(taps, axis=0))
            total = term if total is None else total + term
        parts.append(total)
    if flipped:
        parts = parts[::-1]
    return parts[1] + shifted(parts[0], 1, width) + shifted(parts[2], -1, width)


def conv_one_kernel(zi, x0, x1, x2, x3, e0, e1, e2, e3, w, vec, hidden, sums, xs):
    rows, images, width, channels = x0.shape
    fill(xs, (x0, x1, x2, x3), (e0, e1, e2, e3))
    result = conv_taps(xs, w, zi[0], rows, images * width, width, False) + vec[2:3]
    hidden[...] = result.reshape(hidden.shape)
    for b in range(images):
        v = image_of(hidden, b)
        sums[b : b + 1] = column_sum(v)
        sums[images + b : images + b + 1] = column_sum(v * v)


def conv_two_kernel(zi, x0, x1, x2, x3, e0, e1, e2, e3, w, vec, pixels, residual, sums, xs):
    rows, images, width, channels = x0.shape
    fill(xs, (x0, x1, x2, x3), (e0, e1, e2, e3))
    result = conv_taps(xs, w, zi[0], rows, images * width, width, False) + vec[5:6]
    residual[...] = pixels[...] + result.reshape(residual.shape)
    for b in range(images):
        v = image_of(residual, b)
        sums[b : b + 1] = column_sum(v)
        sums[images + b : images + b + 1] = column_sum(v * v)


def conv_two_back_kernel(
    zi, x0, x1, x2, x3, e0, e1, e2, e3, w, vec, hidden, stats, mod, shaped_grad, sums, xs
):
    rows, images, width, channels = x0.shape
    fill(xs, (x0, x1, x2, x3), (e0, e1, e2, e3))
    result = conv_taps(xs, w, zi[0], rows, images * width, width, True)
    shaped_grad[...] = result.reshape(shaped_grad.shape)
    average, inverse = moments(stats[...], images)
    for b in range(images):
        xhat, shaped = modulated(image_of(hidden, b), average, inverse, mod, vec, b, images)
        g = image_of(shaped_grad, b) * silu_slope(shaped)
        put_image(shaped_grad, b, g)
        sums[b : b + 1] = column_sum(g)
        sums[images + b : images + b + 1] = column_sum(g * xhat)


def conv_one_back_kernel(
    zi, x0, x1, x2, x3, e0, e1, e2, e3, w, vec, pixels, stats, normed_grad, sums, xs
):
    rows, images, width, channels = x0.shape
    fill(xs, (x0, x1, x2, x3), (e0, e1, e2, e3))
    result = conv_taps(xs, w, zi[0], rows, images * width, width, True)
    normed_grad[...] = result.reshape(normed_grad.shape)
    average, inverse = moments(stats[...], images)
    for b in range(images):
        xhat = (image_of(pixels, b) - average[b : b + 1]) * inverse[b : b + 1]
        g = image_of(normed_grad, b) * silu_slope(xhat * vec[0:1] + vec[1:2])
        put_image(normed_grad, b, g)
        sums[b : b + 1] = column_sum(g)
        sums[images + b : images + b + 1] = column_sum(g * xhat)


def conv_weight_kernel(zi, x0, x1, x2, x3, e0, e1, e2, e3, r, o, xs):
    rows, images, width, channels = x0.shape
    span = images * width
    fill(xs, (x0, x1, x2, x3), (e0, e1, e2, e3))
    turned = xs[...].T
    wide = r[...].reshape(rows * span, channels).astype(F32)
    three = jnp.concatenate(
        [shifted(wide, -1, width).astype(BF), wide.astype(BF), shifted(wide, 1, width).astype(BF)],
        axis=1,
    )
    for dy in range(3):
        grad = nn(turned[:, dy * span : (dy + rows) * span], three)
        for dx in range(3):
            for j in range(4):
                o[3 * dy + dx, rows_of(zi[0], j, channels), :] = grad[
                    j * channels : (j + 1) * channels, dx * channels : (dx + 1) * channels
                ].astype(BF)


def heads_out(o, leading, value, b, heads):
    turned = value.T.astype(o.dtype)
    for h in range(heads):
        o[b * heads + h, leading] = turned[h * HEAD_DIM : (h + 1) * HEAD_DIM]


def project_kernel(zi, x0, x1, x2, x3, w, vec, o, *, base):
    rows, images, width, channels = x0.shape
    heads = channels // HEAD_DIM
    pixels = rows * images * width
    a = jnp.concatenate([x[...].reshape(pixels, channels) for x in (x0, x1, x2, x3)], axis=1)
    for s in range(3):
        taps = [w[base + s, rows_of(zi[0], j, channels), :] for j in range(4)]
        value = nn(a, jnp.concatenate(taps, axis=0))
        if s != 1:
            at = 8 if s == 0 else 9
            value = value + vec[at : at + 1]
        split = value.reshape(rows, images, width, channels)
        for b in range(images):
            heads_out(o, s, split[:, b].reshape(rows * width, channels), b, heads)


def output_grad_kernel(zi, x0, x1, x2, x3, w, o, *, tap):
    rows, images, width, channels = x0.shape
    heads = channels // HEAD_DIM
    pixels = rows * images * width
    a = jnp.concatenate([x[...].reshape(pixels, channels) for x in (x0, x1, x2, x3)], axis=1)
    taps = [w[tap, rows_of(zi[0], j, channels), :] for j in range(4)]
    split = nt(a, jnp.concatenate(taps, axis=1)).reshape(rows, images, width, channels)
    for b in range(images):
        turned = split[:, b].reshape(rows * width, channels).T.astype(BF)
        for h in range(heads):
            o[b * heads + h] = turned[h * HEAD_DIM : (h + 1) * HEAD_DIM]


def attention_kernel(
    live, q_ref, do_ref, kv_ref, sib_ref, ctx_ref, oq_ref, own_ref, other_ref, ctx_grad_ref, kt_s, k_s, v_s, s_s, p_s, acc_s, *, chunk
):
    step = pl.program_id(0)
    last = pl.num_programs(0) - 1
    depth, queries = q_ref.shape
    half = kv_ref.shape[2]
    keys = 2 * half
    extra = ctx_ref.shape[2]

    @pl.when(step == 0)
    def _():
        kt_s[:, :, 0:half] = kv_ref[...]
        kt_s[:, :, half:keys] = sib_ref[...]
        kt_s[:, :, keys:] = ctx_ref[...]
        k_s[...] = kt_s[0].T
        v_s[...] = kt_s[1].T
        acc_s[...] = jnp.zeros_like(acc_s)

    q = q_ref[...]
    do = do_ref[...]
    spans = [(i * chunk, chunk) for i in range(keys // chunk)] + [(keys, extra)]
    highest = None
    for at, size in spans:
        s = nn(k_s[at : at + size], q)
        if at == keys:
            position = lax.broadcasted_iota(jnp.int32, s.shape, 0)
            s = jnp.where(position < live[0], s, -1e30)
        s_s[at : at + size] = s
        top = jnp.max(s.reshape(size // 8, 8, queries), axis=0)
        highest = top if highest is None else jnp.maximum(highest, top)
    factor = 0.125 * LOG2E
    peak = jnp.max(highest, axis=0, keepdims=True) * factor
    weight_sum = jnp.zeros((8, queries), F32)
    mixture = jnp.zeros((depth, queries), F32)
    for at, size in spans:
        p = jnp.exp2(s_s[at : at + size] * factor - peak)
        weight_sum = weight_sum + jnp.sum(p.reshape(size // 8, 8, queries), axis=0)
        low = p.astype(BF)
        p_s[at : at + size] = low
        mixture = mixture + nn(kt_s[1, :, at : at + size], low)
    inverse = 1.0 / jnp.sum(weight_sum, axis=0, keepdims=True)
    attended = mixture * inverse
    oq_ref[0] = attended.astype(BF)
    delta = jnp.sum(do.astype(F32) * attended, axis=0, keepdims=True)
    do_scaled = (do.astype(F32) * inverse).astype(BF)
    q_scaled = (q.astype(F32) * (inverse * 0.125)).astype(BF)
    query_grad = jnp.zeros((depth, queries), F32)
    for at, size in spans:
        dprob = nn(v_s[at : at + size], do)
        low = p_s[at : at + size]
        dscore = (low.astype(F32) * (dprob - delta)).astype(BF)
        query_grad = query_grad + nn(kt_s[0, :, at : at + size], dscore)
        acc_s[0, :, at : at + size] += nt(q_scaled, dscore)
        acc_s[1, :, at : at + size] += nt(do_scaled, low)
    oq_ref[1] = (query_grad * (inverse * 0.125)).astype(BF)

    @pl.when(step == last)
    def _():
        own_ref[...] = acc_s[:, :, 0:half]
        other_ref[...] = acc_s[:, :, half:keys].astype(BF)
        ctx_grad_ref[...] = acc_s[:, :, keys:]


def attention(live, q, do, kv, sib, ctx):
    depth, queries = q.shape
    half = kv.shape[2]
    total = 2 * half + ctx.shape[2]
    block = min(512, queries)
    chunk = min(1024, 2 * half)

    def whole(a):
        return pl.BlockSpec(a.shape, lambda i: (0,) * len(a.shape))

    columns = pl.BlockSpec((depth, block), lambda i: (0, i))
    outs = (
        out((2, depth, queries), BF),
        out((2, depth, half), F32),
        out((2, depth, half), BF),
        out(ctx.shape, F32),
    )
    return pl.pallas_call(
        functools.partial(attention_kernel, chunk=chunk),
        grid=(queries // block,),
        in_specs=[pl.BlockSpec(memory_space=pltpu.SMEM), columns, columns, whole(kv), whole(sib), whole(ctx)],
        out_specs=(
            pl.BlockSpec((2, depth, block), lambda i: (0, 0, i)),
            whole(outs[1]),
            whole(outs[2]),
            whole(outs[3]),
        ),
        out_shape=outs,
        scratch_shapes=[
            pltpu.VMEM((2, depth, total), BF),
            pltpu.VMEM((total, depth), BF),
            pltpu.VMEM((total, depth), BF),
            pltpu.VMEM((total, block), F32),
            pltpu.VMEM((total, block), BF),
            pltpu.VMEM((2, depth, total), F32),
        ],
        compiler_params=pltpu.CompilerParams(
            vmem_limit_bytes=56 * 1024 * 1024, dimension_semantics=("arbitrary",)
        ),
        cost_estimate=pl.CostEstimate(
            flops=12 * depth * queries * total, bytes_accessed=8 * depth * total, transcendentals=queries * total
        ),
    )(live, q, do, kv, sib, ctx)


def back_project_kernel(zi, rec, w, attended, grads, parts, biases, *, base):
    rows, images, width, channels = attended.shape
    heads = channels // HEAD_DIM
    for b in range(images):
        for s in range(4):
            blocks = [rec[(b * heads + h) ^ zi[1], s] for h in range(heads)]
            value = jnp.concatenate(blocks, axis=0).T.reshape(rows, width, channels)
            if s == 0:
                attended[:, b] = value
            else:
                grads[:, b, :, (s - 1) * channels : s * channels] = value
    flat = grads[...].reshape(rows * images * width, 3 * channels)
    for place, j in enumerate((0, 2, 1, 3)):
        at = rows_of(zi[0], j, channels)
        taps = jnp.concatenate([w[base + s, at, :] for s in range(3)], axis=1)
        parts[place] = nt(flat, taps).astype(BF).reshape(parts.shape[1:])
    wide = flat.astype(F32)
    biases[0:1] = column_sum(wide[:, 0:channels])
    biases[1:2] = column_sum(wide[:, 2 * channels :])


def product_weight_kernel(zi, x0, x1, x2, x3, g, o):
    rows, images, width, channels = x0.shape
    pixels = rows * images * width
    a = jnp.concatenate([x[...].reshape(pixels, channels) for x in (x0, x1, x2, x3)], axis=1)
    columns = g.shape[3]
    grad = nn(a.T, g[...].reshape(pixels, columns))
    for s in range(columns // channels):
        for j in range(4):
            o[s, rows_of(zi[0], j, channels), :] = grad[
                j * channels : (j + 1) * channels, s * channels : (s + 1) * channels
            ].astype(BF)


def out_project_kernel(zi, x0, x1, x2, x3, w, vec, residual, o, *, tap):
    rows, images, width, channels = x0.shape
    pixels = rows * images * width
    a = jnp.concatenate([x[...].reshape(pixels, channels) for x in (x0, x1, x2, x3)], axis=1)
    taps = [w[tap, rows_of(zi[0], j, channels), :] for j in range(4)]
    value = nn(a, jnp.concatenate(taps, axis=0)) + vec[10:11]
    o[...] = (residual[...] + value.reshape(o.shape)).astype(BF)


def back_three_sum_kernel(t0, t1, t2, residual, stats, g_out, sums):
    images = residual.shape[1]
    average, inverse = moments(stats[...], images)
    for b in range(images):
        g = image_of(t0, b).astype(F32) + image_of(t1, b).astype(F32) + image_of(t2, b).astype(F32)
        xhat = (image_of(residual, b) - average[b : b + 1]) * inverse[b : b + 1]
        put_image(g_out, b, g)
        sums[b : b + 1] = column_sum(g)
        sums[images + b : images + b + 1] = column_sum(g * xhat)


def back_three_kernel(g_in, residual, stats, sums, vec, grad_out, residual_grad, low, bias):
    images = residual.shape[1]
    average, inverse = moments(stats[...], images)
    means = group_mean(sums[...] * vec[6:7])
    total = None
    for b in range(images):
        xhat = (image_of(residual, b) - average[b : b + 1]) * inverse[b : b + 1]
        scaled = image_of(g_in, b) * vec[6:7]
        g = inverse[b : b + 1] * (scaled - means[b : b + 1] - xhat * means[images + b : images + b + 1])
        g = image_of(grad_out, b) + g
        put_image(residual_grad, b, g)
        put_image(low, b, g)
        part = column_sum(g)
        total = part if total is None else total + part
    bias[...] = total


def back_two_kernel(g_in, hidden, stats, sums, mod, vec, low, bias):
    images = hidden.shape[1]
    average, inverse = moments(stats[...], images)
    scale = 1.0 + (mod[0:images] + vec[12:13])
    both = jnp.concatenate([scale, scale], axis=0)
    means = group_mean(sums[...] * both * vec[3:4])
    total = None
    for b in range(images):
        xhat = (image_of(hidden, b) - average[b : b + 1]) * inverse[b : b + 1]
        scaled = image_of(g_in, b) * scale[b : b + 1] * vec[3:4]
        g = inverse[b : b + 1] * (scaled - means[b : b + 1] - xhat * means[images + b : images + b + 1])
        put_image(low, b, g)
        part = column_sum(g)
        total = part if total is None else total + part
    bias[...] = total


def back_one_kernel(g_in, pixels, stats, sums, vec, residual_grad, pixel_grad):
    images = pixels.shape[1]
    average, inverse = moments(stats[...], images)
    means = group_mean(sums[...] * vec[0:1])
    for b in range(images):
        xhat = (image_of(pixels, b) - average[b : b + 1]) * inverse[b : b + 1]
        scaled = image_of(g_in, b) * vec[0:1]
        g = inverse[b : b + 1] * (scaled - means[b : b + 1] - xhat * means[images + b : images + b + 1])
        put_image(pixel_grad, b, image_of(residual_grad, b) + g)


def adamw(weight, moment, square, gradient, step_rate, weight_decay):
    moment_new = 0.9 * moment + 0.1 * gradient
    square_new = 0.999 * square + 0.001 * gradient * gradient
    corrected = moment_new / (1.0 - 0.9**STEP)
    scaled = square_new / (1.0 - 0.999**STEP)
    weight_new = weight - step_rate * (
        corrected / (jnp.sqrt(scaled) + 1e-08) + weight_decay * weight
    )
    return (weight_new, moment_new, square_new)


def turn_weights(x, row_count, chan_count):
    share = row_count // chan_count
    moves = []
    for r in range(row_count):
        for z in range(chan_count):
            moves.append((r * chan_count + z, (z * share + r % share) * chan_count + r // share))
    return lax.ppermute(x, ("rows", "chan"), moves)


def body(
    pixels,
    cotangent,
    loss_weight,
    timesteps,
    clip_embed,
    context,
    text_len,
    conv_first,
    conv_first_moment,
    conv_first_square,
    conv_second,
    conv_second_moment,
    conv_second_square,
    qkv_weight,
    qkv_weight_moment,
    qkv_weight_square,
    out_weight,
    out_weight_moment,
    out_weight_square,
    embed_weight,
    embed_weight_moment,
    embed_weight_square,
    context_weight,
    context_weight_moment,
    context_weight_square,
    vectors,
    vectors_moment,
    vectors_square,
):
    row_count = lax.axis_size("rows")
    chan_count = lax.axis_size("chan")
    row = lax.axis_index("rows")
    chan = lax.axis_index("chan")
    local_rows, images, width, channels = pixels.shape
    heads = channels // HEAD_DIM
    pairs = images * heads
    assert chan_count == 4 and row_count == 2 * pairs
    pair = row // 2
    zi = jnp.stack([chan, pair]).astype(jnp.int32)
    act = (local_rows, images, width, channels)
    edge_rows = (local_rows + 2) * images * width
    xs = pltpu.VMEM((edge_rows, C), BF)
    conv_flops = 2 * local_rows * images * width * 9 * C * channels

    one_low = conv_first.astype(BF)
    two_low = conv_second.astype(BF)
    qkv_low = jnp.transpose(qkv_weight, (1, 0, 2)).astype(BF)
    out_low = out_weight.astype(BF)[None]
    one_full = lax.all_gather(one_low, "rows", axis=1, tiled=True)
    out_turned = turn_weights(out_low, row_count, chan_count)
    two_full = lax.all_gather(
        jnp.concatenate([two_low, qkv_low, out_low, out_turned], axis=0), "rows", axis=1, tiled=True
    )
    ctx_full = lax.all_gather(context_weight.astype(BF), "rows", axis=0, tiled=True)
    back_full = lax.all_gather(
        turn_weights(jnp.concatenate([two_low, one_low], axis=0), row_count, chan_count),
        "rows",
        axis=1,
        tiled=True,
    )

    share = EMB // row_count
    index = row * share + jnp.arange(share, dtype=jnp.int32)
    half_width = EMB // 2
    frequency = jnp.exp(-math.log(10000.0) * (index % half_width).astype(F32) / half_width)
    phases = timesteps.astype(F32)[:, None] * frequency[None, :]
    features = jnp.where(index[None, :] < half_width, jnp.cos(phases), jnp.sin(phases))
    clip_share = lax.dynamic_slice_in_dim(clip_embed, row * share, share, 1)
    embedding = jax.nn.silu(features + clip_share).astype(BF)
    modulation = jnp.einsum(
        "be,esc->sbc", embedding, embed_weight.astype(BF), preferred_element_type=F32
    ).reshape(2 * images, channels)

    first = jnp.concatenate(
        [jnp.sum(pixels, axis=(0, 2)), jnp.sum(pixels * pixels, axis=(0, 2)), modulation], axis=0
    )
    first = rows_sum(first)
    stats_one, mod = first[: 2 * images], first[2 * images :]
    (active_one,) = local_call(
        functools.partial(norm_kernel, gain=0, offset=1, active=True),
        [out(act, BF)],
        pixels,
        stats_one,
        vectors,
    )
    blocks_one = chan_blocks_with_rims(active_one)
    sums_shape = out((2 * images, channels), F32)
    hidden, stats_two = local_call(
        conv_one_kernel,
        [out(act, F32), sums_shape],
        zi,
        *blocks_one,
        one_full,
        vectors,
        scratch=[xs],
        flops=conv_flops,
    )
    stats_two = rows_sum(stats_two)
    (active_two,) = local_call(act_two_kernel, [out(act, BF)], hidden, stats_two, mod, vectors)
    blocks_two = chan_blocks_with_rims(active_two)
    residual, stats_three = local_call(
        conv_two_kernel,
        [out(act, F32), sums_shape],
        zi,
        *blocks_two,
        two_full,
        vectors,
        pixels,
        scratch=[xs],
        flops=conv_flops,
    )
    stats_three = rows_sum(stats_three)
    (normed,) = local_call(
        functools.partial(norm_kernel, gain=6, offset=7, active=False),
        [out(act, BF)],
        residual,
        stats_three,
        vectors,
    )
    blocks_three = chan_blocks(normed)
    tokens = local_rows * width
    (projected,) = local_call(
        functools.partial(project_kernel, base=9),
        [out((pairs, 3, HEAD_DIM, tokens), BF)],
        zi,
        *blocks_three,
        two_full,
        vectors,
        flops=conv_flops // 3,
    )
    mine = jnp.concatenate(pair_exchange(projected, pair), axis=2)
    query, key_value = mine[0], mine[1:]
    sibling = swap(key_value, "rows", 1)

    grad_out = cotangent.astype(F32) * loss_weight[None, :, None, None]
    grad_low = grad_out.astype(BF)
    out_bias = jnp.sum(grad_out, axis=(0, 1, 2))[None]
    (attended_grad,) = local_call(
        functools.partial(output_grad_kernel, tap=13),
        [out((pairs, HEAD_DIM, tokens), BF)],
        zi,
        *chan_blocks(grad_low),
        two_full,
    )
    attended_grad = jnp.concatenate(pair_exchange(attended_grad, pair), axis=1)

    image, head = pair // heads, pair % heads
    ctx_low = pick(context, image)
    ctx_projected = jnp.einsum("te,esc->sct", ctx_low, ctx_full, preferred_element_type=F32)
    ctx_bias = jnp.stack([jnp.zeros_like(vectors[11]), vectors[11]])[:, :, None]
    ctx_heads = lax.dynamic_slice_in_dim(ctx_projected + ctx_bias, head * HEAD_DIM, HEAD_DIM, 1)
    ctx_heads = jnp.pad(ctx_heads.astype(BF), ((0, 0), (0, 0), (0, CTX_PAD - CTX)))
    live = (CLIP_TOK + pick(text_len, image))[None].astype(jnp.int32)

    out_query, own, other, ctx_grad = attention(
        live, query, attended_grad, key_value, sibling, ctx_heads
    )
    own = (own + swap(other, "rows", 1).astype(F32)).astype(BF)
    back = jnp.concatenate([out_query, own], axis=0)
    returned = [back[:, :, k * tokens : (k + 1) * tokens] for k in range(pairs)]
    received = jnp.stack(
        [returned[0]] + [swap(returned[k], "rows", 2 * k) for k in range(1, pairs)]
    )
    ctx_low_grad = (ctx_grad + swap(ctx_grad, "rows", 1)).astype(BF)
    ctx_all = jnp.stack(
        [ctx_low_grad] + [swap(ctx_low_grad, "rows", 2 * k) for k in range(1, pairs)]
    )

    attended, grads, parts, qv_bias = local_call(
        functools.partial(back_project_kernel, base=9),
        [
            out(act, BF),
            out((local_rows, images, width, 3 * channels), BF),
            out((4,) + act, BF),
            out((2, channels), F32),
        ],
        zi,
        received,
        two_full,
        flops=conv_flops // 3,
    )
    terms = chan_scatter(parts)
    normed_grad, sums_three = local_call(
        back_three_sum_kernel, [out(act, F32), sums_shape], *terms, residual, stats_three
    )
    sums_three = rows_sum(sums_three)
    residual_grad, residual_low, conv_two_bias = local_call(
        back_three_kernel,
        [out(act, F32), out(act, BF), out((1, channels), F32)],
        normed_grad,
        residual,
        stats_three,
        sums_three,
        vectors,
        grad_out,
    )
    shaped_grad, sums_two = local_call(
        conv_two_back_kernel,
        [out(act, F32), sums_shape],
        zi,
        *chan_blocks_with_rims(residual_low),
        back_full[:9],
        vectors,
        hidden,
        stats_two,
        mod,
        scratch=[xs],
        flops=conv_flops,
    )
    second = rows_sum(jnp.concatenate([sums_two, conv_two_bias, qv_bias, out_bias], axis=0))
    sums_two = second[: 2 * images]
    hidden_low, conv_one_bias = local_call(
        back_two_kernel,
        [out(act, BF), out((1, channels), F32)],
        shaped_grad,
        hidden,
        stats_two,
        sums_two,
        mod,
        vectors,
    )
    normed_one_grad, sums_one = local_call(
        conv_one_back_kernel,
        [out(act, F32), sums_shape],
        zi,
        *chan_blocks_with_rims(hidden_low),
        back_full[9:],
        vectors,
        pixels,
        stats_one,
        scratch=[xs],
        flops=conv_flops,
    )
    third = rows_sum(jnp.concatenate([sums_one, conv_one_bias], axis=0))
    sums_one = third[: 2 * images]
    (pixel_grad,) = local_call(
        back_one_kernel,
        [out(act, F32)],
        normed_one_grad,
        pixels,
        stats_one,
        sums_one,
        vectors,
        residual_grad,
    )

    attended_blocks = chan_blocks(attended)
    (activations,) = local_call(
        functools.partial(out_project_kernel, tap=12),
        [out(act, BF)],
        zi,
        *attended_blocks,
        two_full,
        vectors,
        residual,
    )

    taps = (9, C, channels)
    (two_grad,) = local_call(
        conv_weight_kernel,
        [out(taps, BF)],
        zi,
        *blocks_two,
        residual_low,
        scratch=[xs],
        flops=conv_flops,
    )
    (qkv_grad,) = local_call(
        product_weight_kernel, [out((3, C, channels), BF)], zi, *blocks_three, grads
    )
    (out_grad,) = local_call(
        product_weight_kernel, [out((1, C, channels), BF)], zi, *attended_blocks, grad_low
    )
    two_sum = weight_scatter(jnp.concatenate([two_grad, qkv_grad, out_grad], axis=0))
    qkv_sum = jnp.transpose(two_sum[9:12], (1, 0, 2))
    out_sum = two_sum[12]
    two_sum = two_sum[:9]
    (one_grad,) = local_call(
        conv_weight_kernel,
        [out(taps, BF)],
        zi,
        *blocks_one,
        hidden_low,
        scratch=[xs],
        flops=conv_flops,
    )
    one_sum = weight_scatter(one_grad)

    shift_grad, crossed = sums_two[:images], sums_two[images:]
    scale_grad = crossed * vectors[3] + shift_grad * vectors[4]
    embed_grad = jnp.einsum(
        "be,sbc->esc",
        embedding.astype(F32),
        jnp.stack((scale_grad, shift_grad)),
        precision=lax.Precision.HIGHEST,
    )
    order = jnp.arange(pairs, dtype=jnp.int32) ^ pair
    ctx_all = jnp.take(ctx_all, order, axis=0)[:, :, :, :CTX]
    ctx_all = ctx_all.reshape(images, heads, 2, HEAD_DIM, CTX)
    ctx_share = DCTX // row_count
    ctx_rows = lax.dynamic_slice_in_dim(context, row * ctx_share, ctx_share, 2)
    context_grad = jnp.einsum(
        "bte,bhsdt->eshd", ctx_rows, ctx_all, preferred_element_type=F32
    ).reshape(ctx_share, 2, channels)
    ctx_value_bias = jnp.sum(ctx_all[:, :, 1].astype(F32), axis=(0, 3)).reshape(1, channels)

    modulated_scale = 1.0 + mod[:images] + vectors[12]
    vector_grad = jnp.concatenate(
        (
            jnp.sum(sums_one[images:], axis=0, keepdims=True),
            jnp.sum(sums_one[:images], axis=0, keepdims=True),
            third[2 * images :],
            jnp.sum(modulated_scale * crossed, axis=0, keepdims=True),
            jnp.sum(modulated_scale * shift_grad, axis=0, keepdims=True),
            second[2 * images : 2 * images + 1],
            jnp.sum(sums_three[images:], axis=0, keepdims=True),
            jnp.sum(sums_three[:images], axis=0, keepdims=True),
            second[2 * images + 1 : 2 * images + 4],
            ctx_value_bias,
            jnp.sum(scale_grad, axis=0, keepdims=True),
            jnp.sum(shift_grad, axis=0, keepdims=True),
        ),
        axis=0,
    )

    squared = jnp.zeros((), F32)
    for member in (two_sum, qkv_sum, out_sum, embed_grad, context_grad, one_sum):
        squared = squared + jnp.sum(member * member)
    squared = squared + jnp.where(row == 0, jnp.sum(vector_grad * vector_grad), 0.0)
    squared = chan_sum(rows_sum(jnp.broadcast_to(squared, (8, 128))))[0, 0]
    grad_norm = jnp.sqrt(squared)
    factor = jnp.minimum(1.0, clip_limit / grad_norm)
    conv_one = adamw(
        conv_first, conv_first_moment, conv_first_square, one_sum * factor, 0.02, 0.01
    )
    conv_two = adamw(
        conv_second, conv_second_moment, conv_second_square, two_sum * factor, 0.02, 0.01
    )
    qkv_new = adamw(qkv_weight, qkv_weight_moment, qkv_weight_square, qkv_sum * factor, 0.08, 0.01)
    out_new = adamw(out_weight, out_weight_moment, out_weight_square, out_sum * factor, 1.0, 0.01)
    embed_new = adamw(
        embed_weight, embed_weight_moment, embed_weight_square, embed_grad * factor, 0.02, 0.01
    )
    context_new = adamw(
        context_weight,
        context_weight_moment,
        context_weight_square,
        context_grad * factor,
        0.04,
        0.01,
    )
    vector_new = adamw(vectors, vectors_moment, vectors_square, vector_grad * factor, 1.0, 0.0)
    result = [activations, pixel_grad, grad_norm]
    for new in (conv_one, conv_two, qkv_new, out_new, embed_new, context_new):
        result += [new[0], new[1], new[2], new[0].astype(BF)]
    return (*result, *vector_new)


def solution(mesh):
    act = P("rows", None, None, "chan")
    conv = P(None, "rows", "chan")
    wide = P("rows", None, "chan")
    flat = P("rows", "chan")
    vec = P(None, "chan")
    weights = (conv, conv, wide, flat, wide, wide)
    in_specs = (act, act) + (P(),) * 5 + tuple(s for w in weights for s in (w,) * 3) + (vec,) * 3
    out_specs = (act, act, P()) + tuple(s for w in weights for s in (w,) * 4) + (vec,) * 3
    return jax.shard_map(body, mesh=mesh, in_specs=in_specs, out_specs=out_specs, check_vma=False)
```

```python
import functools
import math

import jax
import jax.numpy as jnp
from jax import lax
from jax.experimental import pallas as pl
from jax.experimental.pallas import tpu as pltpu
from jax.sharding import PartitionSpec as P

C = 512
GROUPS = 32
HEAD_DIM = 64
EMB = 2048
DCTX = 2048
IMG_H = 64
IMG_W = 64
CLIP_TOK = 4
STEP = 10
CTX = 81
CTX_PAD = 128
GROUP_SIZE = C // GROUPS
GROUP_COUNT = IMG_H * IMG_W * GROUP_SIZE
LOG2E = 1.4426950408889634
BF = jnp.bfloat16
F32 = jnp.float32
ORDER = (0, 1, 3, 2)

clip_limit = 1.0


def swap(x, axis, distance):
    size = lax.axis_size(axis)
    return lax.ppermute(x, axis, [(i, i ^ distance) for i in range(size)])


def rows_sum(x, first=None):
    size = lax.axis_size("rows")
    x = x + swap(x, "rows", 1) if first is None else first
    step = 2
    while step < size:
        if step * 4 <= size:
            one, two, three = (swap(x, "rows", step * k) for k in (1, 2, 3))
            x = (x + one) + (two + three)
            step *= 4
        else:
            x = x + swap(x, "rows", step)
            step *= 2
    return x


def chan_blocks(x, *beside):
    far = swap(x, "chan", 3)
    near = swap(x, "chan", 1)
    return (x, near, far, swap(after(far, *beside), "chan", 1))


def rims(top, bottom):
    size = lax.axis_size("rows")
    up = [(i, i + 1) for i in range(size - 1)]
    down = [(j, i) for i, j in up]
    return lax.ppermute(bottom, "rows", up), lax.ppermute(top, "rows", down)


def after(x, *earlier):
    return lax.optimization_barrier((x, *earlier))[0]


def pick(x, index, axis=0):
    return lax.dynamic_index_in_dim(x, index, axis, keepdims=False)


def weight_scatter(mine, other):
    count, _, *rest = mine[0].shape
    shape = (sum(a.shape[1] for a in mine), *rest)
    total, *low = local_call(
        scatter_kernel,
        [out(shape, F32)] + [out(shape, BF)] * (count - 1),
        *mine,
        *other,
    )
    return [total] + [swap(low[k - 1], "rows", 2 * k) for k in range(1, count)]


class Far:
    def __init__(self, array):
        self.array = array


def near_rows(*arrays):
    return tuple(a.reshape(math.prod(a.shape[:-1]), a.shape[-1]) for a in arrays)


def far_rows(*arrays):
    return tuple(Far(a.reshape(math.prod(a.shape[:-1]), a.shape[-1])) for a in arrays)


def local_call(kernel, outs, *args, scratch=(), copies=0, flops=0, limit=50):
    arrays = [a.array if isinstance(a, Far) else a for a in args]

    def spec(a):
        if isinstance(a, Far):
            return pl.BlockSpec(memory_space=pl.ANY)
        return pl.BlockSpec(memory_space=pltpu.SMEM if a.dtype == jnp.int32 else pltpu.VMEM)

    size = sum(math.prod(a.shape) * a.dtype.itemsize for a in (*arrays, *outs))
    scratch = list(scratch)
    if copies:
        scratch.append(pltpu.SemaphoreType.DMA((copies,)))
    return pl.pallas_call(
        kernel,
        out_shape=tuple(outs),
        in_specs=[spec(a) for a in args],
        out_specs=tuple(pl.BlockSpec(memory_space=pltpu.VMEM) for _ in outs),
        scratch_shapes=scratch,
        compiler_params=pltpu.CompilerParams(vmem_limit_bytes=(56 if copies else limit) * 1024 * 1024),
        cost_estimate=pl.CostEstimate(flops=1, bytes_accessed=1, transcendentals=0),
    )(*arrays)


def begin(sems, *moves):
    started = []
    for i, (source, place) in enumerate(moves):
        copy = pltpu.make_async_copy(source, place, sems.at[i])
        copy.start()
        started.append(copy)
    return started


def fetch(sems, *moves):
    for copy in begin(sems, *moves):
        copy.wait()


def lanes_of(xs, j):
    width = xs.shape[1] // 4
    return xs.at[:, j * width : (j + 1) * width]


def block_moves(xs, blocks):
    return [(x, lanes_of(xs, j)) for j, x in enumerate(blocks)]


def out(shape, dtype):
    return jax.ShapeDtypeStruct(shape, dtype)


def nn(a, b):
    return lax.dot_general(a, b, (((1,), (0,)), ((), ())), preferred_element_type=F32)


def nt(a, b):
    return lax.dot_general(a, b, (((1,), (1,)), ((), ())), preferred_element_type=F32)


def group_mean(x):
    width = x.shape[1]
    left = lax.broadcasted_iota(jnp.int32, (width, width), 0) // GROUP_SIZE
    right = lax.broadcasted_iota(jnp.int32, (width, width), 1) // GROUP_SIZE
    same = (left == right).astype(F32)
    total = lax.dot_general(
        x, same, (((1,), (0,)), ((), ())), precision=lax.Precision.HIGHEST, preferred_element_type=F32
    )
    return total * (1.0 / GROUP_COUNT)


def moments(sums, images):
    means = group_mean(sums)
    average = means[:images]
    return average, lax.rsqrt(means[images:] - average * average + 1e-05)


def image_of(ref, b):
    rows, _, width, channels = ref.shape
    return ref[:, b].reshape(rows * width, channels)


def put_image(ref, b, value):
    rows, _, width, channels = ref.shape
    ref[:, b] = value.reshape(rows, width, channels).astype(ref.dtype)


def column_sum(x):
    return jnp.sum(x, axis=0, keepdims=True)


def silu(z):
    return z * jax.nn.sigmoid(z)


def silu_slope(z):
    s = jax.nn.sigmoid(z)
    return s * (1.0 + z * (1.0 - s))


def put_sums(sums, b, images, v, w):
    sums[b : b + 1] = column_sum(v)
    sums[images + b : images + b + 1] = column_sum(v * w)


def start_kernel(pixels, sums):
    images = pixels.shape[1]
    for b in range(images):
        v = image_of(pixels, b)
        put_sums(sums, b, images, v, v)


def edge_of(ref, b):
    return ref[0, b]


def put_wide(o, b, zi, before, value, behind):
    rows, _, width, channels = o.shape
    top = (zi[2] > 0).astype(F32)
    bottom = (zi[3] > 0).astype(F32)
    o[0, b] = (before * top).astype(o.dtype)
    o[1 : rows - 1, b] = value.reshape(rows - 2, width, channels).astype(o.dtype)
    o[rows - 1, b] = (behind * bottom).astype(o.dtype)


def act_one_kernel(zi, x, before, behind, sums, vec, o):
    images = x.shape[1]
    average, inverse = moments(sums[0 : 2 * images], images)
    for b in range(images):

        def active(v):
            xhat = (v - average[b : b + 1]) * inverse[b : b + 1]
            return silu(xhat * vec[0:1] + vec[1:2])

        put_wide(
            o, b, zi, active(edge_of(before, b)), active(image_of(x, b)), active(edge_of(behind, b))
        )


def shaped_of(xhat, mod, vec, b, images):
    scale = 1.0 + (mod[b : b + 1] + vec[12:13])
    shift = mod[images + b : images + b + 1] + vec[13:14]
    return (xhat * vec[3:4] + vec[4:5]) * scale + shift


def act_two_kernel(zi, x, before, behind, sums, mod, vec, o):
    images = x.shape[1]
    average, inverse = moments(sums[...], images)
    for b in range(images):

        def active(v):
            xhat = (v - average[b : b + 1]) * inverse[b : b + 1]
            return silu(shaped_of(xhat, mod, vec, b, images))

        put_wide(
            o, b, zi, active(edge_of(before, b)), active(image_of(x, b)), active(edge_of(behind, b))
        )


def norm_three_kernel(x, sums, vec, o):
    images = x.shape[1]
    average, inverse = moments(sums[...], images)
    for b in range(images):
        xhat = (image_of(x, b) - average[b : b + 1]) * inverse[b : b + 1]
        put_image(o, b, xhat * vec[6:7] + vec[7:8])


def rows_of(z, j, width):
    return pl.ds(pl.multiple_of((z ^ ORDER[j]) * width, width), width)


def shifted(x, by, width):
    length = x.shape[0]
    column = lax.broadcasted_iota(jnp.int32, x.shape, 0) % width
    moved = pltpu.roll(x, by % length, 0)
    return jnp.where(column == (0 if by == 1 else width - 1), 0.0, moved)


def conv_taps(blocks, w, extra, zi, xs, rows, span, width, flipped):
    z = zi[0]
    if extra:
        w_far, (w, sems) = w, extra
        fetch(sems, (w_far.at[0:9], w), *block_moves(xs, blocks))
    else:
        for j, x in enumerate(blocks):
            lanes_of(xs, j)[...] = x[...]
    channels = w.shape[2]
    parts = []
    for dx in range(3):
        total = None
        for dy in range(3):
            at = (2 - dy if flipped else dy) * span
            a = xs[at : at + rows * span, :]
            taps = [w[3 * dy + dx, rows_of(z, j, channels), :] for j in range(4)]
            if flipped:
                term = nt(a, jnp.concatenate(taps, axis=1))
            else:
                term = nn(a, jnp.concatenate(taps, axis=0))
            total = term if total is None else total + term
        parts.append(total)
    if flipped:
        parts = parts[::-1]
    return parts[1] + shifted(parts[0], 1, width) + shifted(parts[2], -1, width)


def conv_one_kernel(zi, x0, x1, x2, x3, w_far, vec, hidden, sums, top, bottom, xs, *extra):
    rows, images, width, channels = hidden.shape
    blocks = (x0, x1, x2, x3)
    result = conv_taps(
        blocks, w_far, extra, zi, xs, rows, images * width, width, False
    ) + vec[2:3]
    hidden[...] = result.reshape(hidden.shape)
    for b in range(images):
        v = image_of(hidden, b)
        put_sums(sums, b, images, v, v)
    top[...] = hidden[0:1]
    bottom[...] = hidden[rows - 1 : rows]


def conv_two_kernel(zi, x0, x1, x2, x3, w_far, vec, pixels, residual, sums, xs, *extra):
    rows, images, width, channels = residual.shape
    blocks = (x0, x1, x2, x3)
    result = conv_taps(
        blocks, w_far, extra, zi, xs, rows, images * width, width, False
    ) + vec[5:6]
    residual[...] = pixels[...] + result.reshape(residual.shape)
    for b in range(images):
        v = image_of(residual, b)
        put_sums(sums, b, images, v, v)


def conv_two_back_kernel(
    zi, x0, x1, x2, x3, w_far, vec, hidden, stats, mod, shaped_grad, sums, top, bottom, xs, *extra
):
    rows, images, width, channels = hidden.shape
    blocks = (x0, x1, x2, x3)
    result = conv_taps(
        blocks, w_far, extra, zi, xs, rows, images * width, width, True
    )
    shaped_grad[...] = result.reshape(shaped_grad.shape)
    average, inverse = moments(stats[...], images)
    for b in range(images):
        xhat = (image_of(hidden, b) - average[b : b + 1]) * inverse[b : b + 1]
        g = image_of(shaped_grad, b) * silu_slope(shaped_of(xhat, mod, vec, b, images))
        put_image(shaped_grad, b, g)
        put_sums(sums, b, images, g, xhat)
    top[...] = shaped_grad[0:1]
    bottom[...] = shaped_grad[rows - 1 : rows]


def conv_one_back_kernel(
    zi, x0, x1, x2, x3, w_far, vec, pixels, stats, normed_grad, sums, xs, *extra
):
    rows, images, width, channels = pixels.shape
    blocks = (x0, x1, x2, x3)
    result = conv_taps(
        blocks, w_far, extra, zi, xs, rows, images * width, width, True
    )
    normed_grad[...] = result.reshape(normed_grad.shape)
    average, inverse = moments(stats[0 : 2 * images], images)
    for b in range(images):
        xhat = (image_of(pixels, b) - average[b : b + 1]) * inverse[b : b + 1]
        g = image_of(normed_grad, b) * silu_slope(xhat * vec[0:1] + vec[1:2])
        put_image(normed_grad, b, g)
        put_sums(sums, b, images, g, xhat)


def put_shares(box, zi, tap, grad):
    share, channels = box.shape[3:]
    each = channels // share
    for j in range(4):
        for i in range(each):
            at = j * channels + i * share
            row = (zi[0] ^ ORDER[j]) * each + i
            box[(row & 1) ^ zi[4], (row >> 1) ^ zi[1], tap] = grad[at : at + share].astype(box.dtype)


def conv_weights(zi, xs, r, box):
    rows, images, width, channels = r.shape
    rows = rows - 2
    span = images * width
    turned = xs[...].T
    wide = r[1 : rows + 1].reshape(rows * span, channels).astype(F32)
    three = jnp.concatenate(
        [shifted(wide, -1, width).astype(BF), wide.astype(BF), shifted(wide, 1, width).astype(BF)],
        axis=1,
    )
    for dy in range(3):
        grad = nn(turned[:, dy * span : (dy + rows) * span], three)
        for dx in range(3):
            put_shares(box, zi, 3 * dy + dx, grad[:, dx * channels : (dx + 1) * channels])


def weights_two_kernel(
    zi, x0, x1, x2, x3, r, n0, n1, n2, n3, grads, att, c0, c1, c2, c3, loss, mine, other, xs, ns, cs, box, sems
):
    blocks = begin(
        sems,
        *block_moves(xs, (x0, x1, x2, x3)),
        *block_moves(ns, (n0, n1, n2, n3)),
        *block_moves(cs, (c0, c1, c2, c3)),
    )
    for copy in blocks[:4]:
        copy.wait()
    conv_weights(zi, xs, r, box)
    for copy in blocks[4:]:
        copy.wait()
    rows, images, width, columns = grads.shape
    channels = att.shape[3]
    pixels = rows * images * width
    grad = nn(ns[...].T, grads[...].reshape(pixels, columns))
    for s in range(3):
        put_shares(box, zi, 9 + s, grad[:, s * channels : (s + 1) * channels])
    scale = jnp.concatenate([loss[b : b + 1] for b in range(images)], axis=0)
    scale = jnp.concatenate([scale] * 4, axis=1)[None, :, None, :]
    low = (cs[...].reshape(rows, images, width, 4 * channels).astype(F32) * scale).astype(BF)
    grad = nn(att[...].reshape(pixels, channels).T, low.reshape(pixels, 4 * channels))
    by_output = [grad[:, j * channels : (j + 1) * channels] for j in range(4)]
    put_shares(box, zi, 12, jnp.concatenate(by_output, axis=0))
    mine[...] = box[0]
    other[...] = box[1]


def weights_one_kernel(zi, x0, x1, x2, x3, r, mine, other, xs, box, sems):
    fetch(sems, *block_moves(xs, (x0, x1, x2, x3)))
    conv_weights(zi, xs, r, box)
    mine[...] = box[0]
    other[...] = box[1]


def scatter_kernel(mine_two, mine_one, other_two, other_one, total, *low):
    at = 0
    for mine, other in ((mine_two, other_two), (mine_one, other_one)):
        taps = slice(at, at + mine.shape[1])
        at += mine.shape[1]
        total[taps] = mine[0].astype(F32) + other[0].astype(F32)
        for k, o in enumerate(low):
            o[taps] = (mine[k + 1].astype(F32) + other[k + 1].astype(F32)).astype(BF)


def put_heads(scratch, leading, value, b, heads):
    turned = value.T.astype(scratch.dtype)
    for h in range(heads):
        scratch[b * heads + h, leading] = turned[h * HEAD_DIM : (h + 1) * HEAD_DIM]


def project_kernel(*refs, base):
    zi, w_far, vec, blocks = refs[0], refs[1], refs[2], refs[3:7]
    outs, (xs, w, scratch, sems) = refs[7:-4], refs[-4:]
    fetch(sems, (w_far.at[base : base + 3], w), *block_moves(xs, blocks))
    tokens = outs[0].shape[2]
    channels = w.shape[2]
    heads = channels // HEAD_DIM
    images = len(outs) // heads
    rows = xs.shape[0] // (images * IMG_W)
    a = xs[...]
    for s in range(3):
        rows_in = [w[s, rows_of(zi[0], j, channels), :] for j in range(4)]
        value = nn(a, jnp.concatenate(rows_in, axis=0))
        if s != 1:
            at = 8 if s == 0 else 9
            value = value + vec[at : at + 1]
        split = value.reshape(rows, images, IMG_W, channels)
        for b in range(images):
            put_heads(scratch, s, split[:, b].reshape(tokens, channels), b, heads)
    for k, o in enumerate(outs):
        o[...] = scratch[zi[1] ^ k]


def output_grad_kernel(*refs, tap):
    zi, w_far, cots, loss = refs[0], refs[1], refs[2:6], refs[6]
    outs, (xs, w, scratch, sems) = refs[7:-4], refs[-4:]
    fetch(sems, (w_far.at[tap : tap + 1], w), *block_moves(xs, cots))
    tokens = outs[0].shape[1]
    channels = w.shape[2]
    heads = channels // HEAD_DIM
    images = len(outs) // heads
    rows = xs.shape[0] // (images * IMG_W)
    lanes = [w[0, rows_of(zi[0], j, channels), :] for j in range(4)]
    turned = jnp.concatenate(lanes, axis=1)
    wide = xs[...].reshape(rows, images, IMG_W, 4 * channels)
    for b in range(images):
        scale = jnp.concatenate([loss[b : b + 1]] * 4, axis=1)
        low = (wide[:, b].reshape(tokens, 4 * channels).astype(F32) * scale).astype(BF)
        put_heads(scratch, 0, nt(low, turned), b, heads)
    for k, o in enumerate(outs):
        o[...] = scratch[zi[1] ^ k, 0]


def attention_kernel(*refs, chunk, count, block):
    live, ctx_ref = refs[0], refs[1]
    mine, grads, sibs = (refs[2 + i * count : 2 + (i + 1) * count] for i in range(3))
    oq_ref, own_ref, other_ref = refs[2 + 3 * count : 5 + 3 * count]
    q_s, do_s, kt_s, k_s, v_s, s_s, p_s, acc_s = refs[5 + 3 * count :]
    step = pl.program_id(0)
    last = pl.num_programs(0) - 1
    tokens = mine[0].shape[2]
    depth = HEAD_DIM
    queries = block
    half = count * tokens
    keys = 2 * half
    extra = ctx_ref.shape[2]

    @pl.when(step == 0)
    def _():
        for k in range(count):
            lanes = slice(k * tokens, (k + 1) * tokens)
            q_s[:, lanes] = mine[k][0]
            do_s[:, lanes] = grads[k][...]
            kt_s[:, :, lanes] = mine[k][1:3]
            kt_s[:, :, half + k * tokens : half + (k + 1) * tokens] = sibs[k][1:3]
        kt_s[:, :, keys:] = ctx_ref[...]
        k_s[...] = kt_s[0].T
        v_s[...] = kt_s[1].T
        acc_s[...] = jnp.zeros_like(acc_s)

    here = pl.ds(pl.multiple_of(step * block, block), block)
    q = q_s[:, here]
    do = do_s[:, here]
    spans = [(i * chunk, chunk) for i in range(keys // chunk)] + [(keys, extra)]
    highest = None
    for at, size in spans:
        s = nn(k_s[at : at + size], q)
        if at == keys:
            position = lax.broadcasted_iota(jnp.int32, s.shape, 0)
            s = jnp.where(position < live[0], s, -1e30)
        s_s[at : at + size] = s
        top = jnp.max(s.reshape(size // 8, 8, queries), axis=0)
        highest = top if highest is None else jnp.maximum(highest, top)
    factor = 0.125 * LOG2E
    peak = jnp.max(highest, axis=0, keepdims=True) * factor
    weight_sum = jnp.zeros((8, queries), F32)
    mixture = jnp.zeros((depth, queries), F32)
    for at, size in spans:
        p = jnp.exp2(s_s[at : at + size] * factor - peak)
        weight_sum = weight_sum + jnp.sum(p.reshape(size // 8, 8, queries), axis=0)
        low = p.astype(BF)
        p_s[at : at + size] = low
        mixture = mixture + nn(kt_s[1, :, at : at + size], low)
    inverse = 1.0 / jnp.sum(weight_sum, axis=0, keepdims=True)
    attended = mixture * inverse
    oq_ref[0] = attended.astype(BF)
    delta = jnp.sum(do.astype(F32) * attended, axis=0, keepdims=True)
    do_scaled = (do.astype(F32) * inverse).astype(BF)
    q_scaled = (q.astype(F32) * (inverse * 0.125)).astype(BF)
    query_grad = jnp.zeros((depth, queries), F32)
    for at, size in spans:
        dprob = nn(v_s[at : at + size], do)
        low = p_s[at : at + size]
        dscore = (low.astype(F32) * (dprob - delta)).astype(BF)
        query_grad = query_grad + nn(kt_s[0, :, at : at + size], dscore)
        acc_s[0, :, at : at + size] += nt(q_scaled, dscore)
        acc_s[1, :, at : at + size] += nt(do_scaled, low)
    oq_ref[1] = (query_grad * (inverse * 0.125)).astype(BF)

    @pl.when(step == last)
    def _():
        own_ref[:, :, 0:half] = acc_s[:, :, 0:half].astype(BF)
        own_ref[:, :, half:] = acc_s[:, :, keys:].astype(BF)
        other_ref[...] = acc_s[:, :, half:].astype(BF)


def attention(live, ctx, mine, grads, sibs):
    count = len(mine)
    depth, tokens = grads[0].shape
    queries = count * tokens
    total = 2 * queries + ctx.shape[2]
    block = min(512, queries)
    chunk = min(1024, 2 * queries)

    def whole(a):
        return pl.BlockSpec(a.shape, lambda i: (0,) * len(a.shape))

    outs = (
        out((2, depth, queries), BF),
        out((2, depth, queries + ctx.shape[2]), BF),
        out((2, depth, queries + ctx.shape[2]), BF),
    )
    arrays = (ctx, *mine, *grads, *sibs)
    return pl.pallas_call(
        functools.partial(attention_kernel, chunk=chunk, count=count, block=block),
        grid=(queries // block,),
        in_specs=[pl.BlockSpec(memory_space=pltpu.SMEM)] + [whole(a) for a in arrays],
        out_specs=(
            pl.BlockSpec((2, depth, block), lambda i: (0, 0, i)),
            whole(outs[1]),
            whole(outs[2]),
        ),
        out_shape=outs,
        scratch_shapes=[
            pltpu.VMEM((depth, queries), BF),
            pltpu.VMEM((depth, queries), BF),
            pltpu.VMEM((2, depth, total), BF),
            pltpu.VMEM((total, depth), BF),
            pltpu.VMEM((total, depth), BF),
            pltpu.VMEM((total, block), F32),
            pltpu.VMEM((total, block), BF),
            pltpu.VMEM((2, depth, total), F32),
        ],
        compiler_params=pltpu.CompilerParams(
            vmem_limit_bytes=56 * 1024 * 1024, dimension_semantics=("arbitrary",)
        ),
        cost_estimate=pl.CostEstimate(
            flops=12 * depth * queries * total, bytes_accessed=8 * depth * total, transcendentals=queries * total
        ),
    )(live, *arrays)


def merge_kernel(oq_far, own_far, other_far, *refs):
    oq, own, other, sems = refs[-4:]
    outs = refs[:-4]
    count = len(outs) // 2
    fetch(sems, (oq_far, oq), (own_far, own), (other_far, other))
    tokens = oq.shape[2] // count
    both = (own[...].astype(F32) + other[...].astype(F32)).astype(BF)
    for k in range(count):
        lanes = slice(k * tokens, (k + 1) * tokens)
        outs[k][0] = oq[1, :, lanes]
        outs[k][1:3] = both[:, :, lanes]
        outs[count + k][:, 0:tokens] = oq[0, :, lanes]
        for s in range(2):
            at = tokens + s * CTX_PAD
            outs[count + k][:, at : at + CTX_PAD] = both[s, :, count * tokens :]


def back_project_kernel(*refs, base, count):
    zi, w_far, pieces = refs[0], refs[1], refs[2 : 2 + count]
    grads, part_own, part_near, part_cross, part_far, biases = refs[2 + count : -3]
    rec, w, sems = refs[-3:]
    fetch(sems, (w_far.at[base : base + 3], w))
    rows, images, width, channels = part_own.shape
    heads = channels // HEAD_DIM
    for k in range(count):
        rec[zi[1] ^ k] = pieces[k][...]
    for b in range(images):
        for s in range(3):
            blocks = [rec[b * heads + h, s] for h in range(heads)]
            value = jnp.concatenate(blocks, axis=0).T.reshape(rows, width, channels)
            grads[:, b, :, s * channels : (s + 1) * channels] = value
    flat = grads[...].reshape(rows * images * width, 3 * channels)
    for j, part in enumerate((part_own, part_near, part_far, part_cross)):
        at = rows_of(zi[0], j, channels)
        taps = jnp.concatenate([w[s, at, :] for s in range(3)], axis=1)
        part[...] = nt(flat, taps).astype(part.dtype).reshape(part.shape)
    wide = flat.astype(F32)
    biases[0:1] = column_sum(wide[:, 0:channels])
    biases[1:2] = column_sum(wide[:, 2 * channels :])


def attended_kernel(*refs):
    zi, pieces = refs[0], refs[1:-3]
    attended, ctx, rec = refs[-3:]
    rows, images, width, channels = attended.shape
    heads = channels // HEAD_DIM
    tokens = rows * width
    for k, piece in enumerate(pieces):
        rec[zi[1] ^ k] = piece[...]
    for b in range(images):
        blocks = [rec[b * heads + h, :, 0:tokens] for h in range(heads)]
        attended[:, b] = jnp.concatenate(blocks, axis=0).T.reshape(rows, width, channels)
    for q in range(len(pieces)):
        for s in range(2):
            at = tokens + s * CTX_PAD
            ctx[q, s] = rec[q, :, at : at + CTX_PAD]


def out_project_kernel(zi, x0, x1, x2, x3, w_far, vec, residual, o, xs, w, sems, *, tap):
    fetch(sems, (w_far.at[tap : tap + 1], w), *block_moves(xs, (x0, x1, x2, x3)))
    channels = w.shape[2]
    rows_in = [w[0, rows_of(zi[0], j, channels), :] for j in range(4)]
    value = nn(xs[...], jnp.concatenate(rows_in, axis=0)) + vec[10:11]
    o[...] = (residual[...] + value.reshape(o.shape)).astype(BF)


def back_three_sum_kernel(t0, t1, t2, residual, cotangent, loss, stats, g_out, sums, top, bottom):
    rows, images, width, channels = residual.shape
    average, inverse = moments(stats[...], images)
    for b in range(images):
        g = image_of(t0, b).astype(F32) + image_of(t1, b).astype(F32) + image_of(t2, b).astype(F32)
        xhat = (image_of(residual, b) - average[b : b + 1]) * inverse[b : b + 1]
        put_image(g_out, b, g)
        put_sums(sums, b, images, g, xhat)
        for edge, at in ((top, 0), (bottom, rows - 1)):
            edge[0, b, :, 0:channels] = g_out[at, b]
            edge[0, b, :, channels : 2 * channels] = residual[at, b]
            edge[0, b, :, 2 * channels :] = cotangent[at, b].astype(F32) * loss[b : b + 1]


def back_three_kernel(
    zi, g0, x0, c0, before, behind, stats, sums, vec, loss, residual_grad, low, bias
):
    images, channels = x0.shape[1], x0.shape[3]
    average, inverse = moments(stats[...], images)
    means = group_mean(sums[...] * vec[6:7])
    total = None
    for b in range(images):

        def back(g, x, c):
            xhat = (x - average[b : b + 1]) * inverse[b : b + 1]
            part = g * vec[6:7] - means[b : b + 1] - xhat * means[images + b : images + b + 1]
            return c + inverse[b : b + 1] * part

        def back_edge(edge):
            return back(*(edge[0, b, :, i * channels : (i + 1) * channels] for i in range(3)))

        cot = image_of(c0, b).astype(F32) * loss[b : b + 1]
        g = back(image_of(g0, b), image_of(x0, b), cot)
        put_image(residual_grad, b, g)
        put_wide(low, b, zi, back_edge(before), g, back_edge(behind))
        part = column_sum(g)
        total = part if total is None else total + part
    bias[...] = total


def back_two_kernel(zi, g0, g1, g2, x0, x1, x2, stats, sums, mod, vec, low, bias):
    images = x0.shape[1]
    average, inverse = moments(stats[...], images)
    gains = [vec[3:4] * (1.0 + (mod[b : b + 1] + vec[12:13])) for b in range(images)]
    means = group_mean(sums[0 : 2 * images] * jnp.concatenate(gains + gains, axis=0))
    total = None
    for b in range(images):

        def back(g, x):
            xhat = (x - average[b : b + 1]) * inverse[b : b + 1]
            part = g * gains[b] - means[b : b + 1] - xhat * means[images + b : images + b + 1]
            return inverse[b : b + 1] * part

        g = back(image_of(g0, b), image_of(x0, b))
        before = back(edge_of(g1, b), edge_of(x1, b))
        behind = back(edge_of(g2, b), edge_of(x2, b))
        put_wide(low, b, zi, before, g, behind)
        part = column_sum(g)
        total = part if total is None else total + part
    bias[...] = total


def back_one_kernel(g_in, pixels, stats, sums, vec, residual_grad, pixel_grad):
    images = pixels.shape[1]
    average, inverse = moments(stats[0 : 2 * images], images)
    means = group_mean(sums[0 : 2 * images] * vec[0:1])
    for b in range(images):
        xhat = (image_of(pixels, b) - average[b : b + 1]) * inverse[b : b + 1]
        scaled = image_of(g_in, b) * vec[0:1]
        g = inverse[b : b + 1] * (scaled - means[b : b + 1] - xhat * means[images + b : images + b + 1])
        put_image(pixel_grad, b, image_of(residual_grad, b) + g)


RATES = (0.02, 0.02, 0.08, 1.0, 0.02, 0.04, 1.0)


def finish_kernel(*refs):
    terms, (squares, sums, bias, two_sum, qkv_sum, out_sum, one_sum, payload) = refs[:-8], refs[-8:]
    squared = squares[...]
    at = 0
    for o in (two_sum, qkv_sum, out_sum, one_sum):
        taps = slice(at, at + o.shape[0])
        at += o.shape[0]
        total = terms[0][taps]
        for term in terms[1:]:
            total = total + term[taps].astype(F32)
        o[...] = total
        squared = squared + column_sum((total * total).reshape(-1, total.shape[-1]))
    count = sums.shape[0]
    payload[0:count] = sums[...]
    payload[count : count + 1] = bias[...]
    payload[count + 1 : count + 2] = squared
    payload[count + 2 :] = jnp.zeros((payload.shape[0] - count - 2, payload.shape[1]), F32)


def vector_kernel(third, second, sums_three, mod, vec, ctx, grad, squares):
    images = sums_three.shape[0] // 2

    def total(ref, at):
        return column_sum(ref[at : at + images])

    scale = 1.0 + (mod[0:images] + vec[12:13])
    shift_grad = second[0:images]
    crossed = second[images : 2 * images]
    scale_grad = crossed * vec[3:4] + shift_grad * vec[4:5]
    at = 2 * images
    rows = (
        total(third, images),
        total(third, 0),
        third[at : at + 1],
        column_sum(scale * crossed),
        column_sum(scale * shift_grad),
        second[at : at + 1],
        total(sums_three, images),
        total(sums_three, 0),
        second[at + 1 : at + 2],
        second[at + 2 : at + 3],
        second[at + 3 : at + 4],
        ctx[...],
        column_sum(scale_grad),
        column_sum(shift_grad),
    )
    squared = third[at + 1 : at + 2]
    for i, row in enumerate(rows):
        grad[i : i + 1] = row
        squared = squared + row * row
    squares[...] = jnp.broadcast_to(squared, squares.shape)


def update_kernel(*refs):
    count = len(RATES)
    squares, given = refs[0:4], refs[4 : 4 + 4 * count]
    made, held, sems = refs[4 + 4 * count : -4 * count - 1], refs[-4 * count - 1 : -1], refs[-1]
    arriving = begin(sems, *zip(given, held))
    near = squares[0][0:1] + squares[1][0:1]
    total = jnp.sum(near + (squares[2][0:1] + squares[3][0:1]), axis=1, keepdims=True)
    norm = jnp.sqrt(total)
    made[0][...] = jnp.broadcast_to(norm, made[0].shape)
    factor = jnp.minimum(1.0, clip_limit / norm)
    at = 1
    for i, rate in enumerate(RATES):
        for copy in arriving[4 * i : 4 * i + 4]:
            copy.wait()
        weight, moment, square, gradient = held[4 * i : 4 * i + 4]
        decay = 0.0 if i == count - 1 else 0.01
        scale = factor.reshape((1,) * (len(weight.shape) - 2) + factor.shape)
        new = adamw(weight[...], moment[...], square[...], gradient[...] * scale, rate, decay)
        for value in new:
            made[at][...] = value
            at += 1
        if i < count - 1:
            made[at][...] = new[0].astype(BF)
            at += 1


def adamw(weight, moment, square, gradient, step_rate, weight_decay):
    moment_new = 0.9 * moment + 0.1 * gradient
    square_new = 0.999 * square + 0.001 * gradient * gradient
    corrected = moment_new / (1.0 - 0.9**STEP)
    scaled = square_new / (1.0 - 0.999**STEP)
    weight_new = weight - step_rate * (
        corrected / (jnp.sqrt(scaled) + 1e-08) + weight_decay * weight
    )
    return (weight_new, moment_new, square_new)


def turn_moves(row_count, chan_count):
    share = row_count // chan_count
    return [
        (r * chan_count + z, (z * share + r % share) * chan_count + r // share)
        for r in range(row_count)
        for z in range(chan_count)
    ]


def turn_weights(x, row_count, chan_count):
    return lax.ppermute(x, ("rows", "chan"), turn_moves(row_count, chan_count))


def turn_back(x, row_count, chan_count):
    moves = [(j, i) for i, j in turn_moves(row_count, chan_count)]
    return lax.ppermute(x, ("rows", "chan"), moves)


def body(
    pixels,
    cotangent,
    loss_weight,
    timesteps,
    clip_embed,
    context,
    text_len,
    conv_first,
    conv_first_moment,
    conv_first_square,
    conv_second,
    conv_second_moment,
    conv_second_square,
    qkv_weight,
    qkv_weight_moment,
    qkv_weight_square,
    out_weight,
    out_weight_moment,
    out_weight_square,
    embed_weight,
    embed_weight_moment,
    embed_weight_square,
    context_weight,
    context_weight_moment,
    context_weight_square,
    vectors,
    vectors_moment,
    vectors_square,
):
    row_count = lax.axis_size("rows")
    chan_count = lax.axis_size("chan")
    row = lax.axis_index("rows")
    chan = lax.axis_index("chan")
    local_rows, images, width, channels = pixels.shape
    heads = channels // HEAD_DIM
    pairs = images * heads
    assert chan_count == 4 and row_count == 2 * pairs
    pair = row // 2
    zi = jnp.stack(
        [chan, pair, row, row_count - 1 - row, row % 2]
    ).astype(jnp.int32)
    act = (local_rows, images, width, channels)
    edge_rows = (local_rows + 2) * images * width
    xs = pltpu.VMEM((edge_rows, C), BF)
    flat = pltpu.VMEM((local_rows * images * width, C), BF)
    taps = pltpu.VMEM((9, C, channels), BF)
    conv_flops = 2 * local_rows * images * width * 9 * C * channels

    (sums,) = local_call(start_kernel, [out((2 * images, channels), F32)], pixels)
    loss = jnp.broadcast_to(loss_weight[:, None], (images, channels))
    cot = after(cotangent, sums)
    cot_near, cot_far = swap(cot, "chan", 1), swap(cot, "chan", 3)

    sums_shape = out((2 * images, channels), F32)
    tall = (local_rows + 2, images, width, channels)
    by_chip = sums + swap(sums, "rows", 1)
    stats_one = rows_sum(sums, by_chip)

    one_full = lax.all_gather(after(conv_first, by_chip).astype(BF), "rows", axis=1, tiled=True)
    two_low = after(conv_second, by_chip).astype(BF)
    qkv_low = jnp.transpose(after(qkv_weight, by_chip), (1, 0, 2)).astype(BF)
    out_low = out_weight.astype(BF)[None]
    pixel_rims = rims(pixels[:1], pixels[-1:])
    (active_one,) = local_call(
        act_one_kernel, [out(tall, BF)], zi, pixels, *pixel_rims, after(stats_one, cot_near, cot_far), vectors
    )
    out_turned = turn_weights(after(out_low, active_one), row_count, chan_count)
    blocks_one = chan_blocks(active_one)
    ctx_full = lax.all_gather(
        after(context_weight, blocks_one[2]).astype(BF), "rows", axis=0, tiled=True
    )

    share = EMB // row_count
    index = row * share + jnp.arange(share, dtype=jnp.int32)
    half_width = EMB // 2
    frequency = jnp.exp(-math.log(10000.0) * (index % half_width).astype(F32) / half_width)
    phases = after(timesteps, active_one).astype(F32)[:, None] * frequency[None, :]
    features = jnp.where(index[None, :] < half_width, jnp.cos(phases), jnp.sin(phases))
    clip_share = lax.dynamic_slice_in_dim(clip_embed, row * share, share, 1)
    embedding = jax.nn.silu(features + clip_share).astype(BF)
    both = jnp.eye(2, dtype=F32)[None, :, :, None]
    embed_rows = (embedding.astype(F32).T[:, None, None, :] * both).reshape(2 * share, 2 * images)
    modulation = jnp.einsum(
        "be,esc->sbc",
        embedding,
        after(embed_weight, active_one).astype(BF),
        preferred_element_type=F32,
    ).reshape(2 * images, channels)

    two_full = lax.all_gather(
        jnp.concatenate([two_low, qkv_low, out_low, after(out_turned, blocks_one[2])], axis=0),
        "rows",
        axis=1,
        tiled=True,
    )
    cot_cross = swap(after(cot_far, *blocks_one), "chan", 1)
    edge = out((1,) + act[1:], F32)
    hidden, sums, *edges = local_call(
        conv_one_kernel,
        [out(act, F32), sums_shape, edge, edge],
        zi,
        *near_rows(*blocks_one),
        one_full,
        vectors,
        scratch=[xs],
        flops=conv_flops,
    )
    hidden_rims = rims(*edges)
    stats_two = rows_sum(jnp.concatenate([after(sums, cot_cross), modulation], axis=0))
    stats_two, mod = stats_two[: 2 * images], stats_two[2 * images :]
    (active_two,) = local_call(
        act_two_kernel, [out(tall, BF)], zi, hidden, *hidden_rims, stats_two, mod, vectors
    )

    tokens = local_rows * width
    cots = (cotangent, cot_near, cot_far, after(cot_cross, active_two))
    grad_pieces = local_call(
        functools.partial(output_grad_kernel, tap=13),
        [out((HEAD_DIM, tokens), BF)] * pairs,
        zi,
        Far(two_full),
        *far_rows(*cots),
        loss,
        scratch=[
            flat,
            pltpu.VMEM((1, C, channels), BF),
            pltpu.VMEM((pairs, 1, HEAD_DIM, tokens), BF),
        ],
        copies=5,
    )
    blocks_two = chan_blocks(active_two, *grad_pieces)
    grad_pieces = [grad_pieces[0]] + [
        swap(grad_pieces[k], "rows", 2 * k) for k in range(1, pairs)
    ]

    residual, sums = local_call(
        conv_two_kernel,
        [out(act, F32), sums_shape],
        zi,
        *far_rows(*blocks_two),
        Far(two_full),
        after(vectors, *grad_pieces),
        pixels,
        scratch=[xs, taps],
        copies=5,
        flops=conv_flops,
    )
    stats_three = rows_sum(sums)
    (normed,) = local_call(norm_three_kernel, [out(act, BF)], residual, stats_three, vectors)
    blocks_three = chan_blocks(normed)

    image, head = pair // heads, pair % heads
    ctx_low = pick(context, image)
    ctx_projected = jnp.einsum("te,esc->sct", ctx_low, ctx_full, preferred_element_type=F32)
    ctx_bias = jnp.stack([jnp.zeros_like(vectors[11]), vectors[11]])[:, :, None]
    ctx_heads = lax.dynamic_slice_in_dim(ctx_projected + ctx_bias, head * HEAD_DIM, HEAD_DIM, 1)
    ctx_heads = jnp.pad(ctx_heads.astype(BF), ((0, 0), (0, 0), (0, CTX_PAD - CTX)))
    live = (CLIP_TOK + pick(text_len, image))[None].astype(jnp.int32)

    pieces = local_call(
        functools.partial(project_kernel, base=9),
        [out((3, HEAD_DIM, tokens), BF)] * pairs,
        zi,
        Far(two_full),
        after(vectors, ctx_heads),
        *far_rows(*blocks_three),
        scratch=[
            flat,
            pltpu.VMEM((3, C, channels), BF),
            pltpu.VMEM((pairs, 3, HEAD_DIM, tokens), BF),
        ],
        copies=5,
        flops=conv_flops // 3,
    )
    pieces = [pieces[0]] + [swap(pieces[k], "rows", 2 * k) for k in range(1, pairs)]
    siblings = [swap(piece, "rows", 1) for piece in pieces]

    turned = turn_weights(
        after(jnp.concatenate([two_low, conv_first.astype(BF)], axis=0), *siblings),
        row_count,
        chan_count,
    )

    out_query, own, other = attention(
        live, ctx_heads, pieces, grad_pieces, siblings
    )
    merged = local_call(
        merge_kernel,
        [out((3, HEAD_DIM, tokens), BF)] * pairs
        + [out((HEAD_DIM, tokens + 2 * CTX_PAD), BF)] * pairs,
        Far(out_query),
        Far(own),
        Far(swap(after(other, turned), "rows", 1)),
        scratch=[
            pltpu.VMEM(out_query.shape, BF),
            pltpu.VMEM(own.shape, BF),
            pltpu.VMEM(own.shape, BF),
        ],
        copies=3,
    )
    received = [merged[0]] + [swap(merged[k], "rows", 2 * k) for k in range(1, pairs)]

    grads, part_own, part_near, part_cross, part_far, qv_bias = local_call(
        functools.partial(back_project_kernel, base=9, count=pairs),
        [
            out((local_rows, images, width, 3 * channels), BF),
            out(act, F32),
            out(act, BF),
            out(act, BF),
            out(act, F32),
            out((2, channels), F32),
        ],
        zi,
        Far(two_full),
        *received,
        scratch=[
            pltpu.VMEM((pairs, 3, HEAD_DIM, tokens), BF),
            pltpu.VMEM((3, C, channels), BF),
        ],
        copies=1,
        flops=conv_flops // 3,
    )
    turned = after(turned, part_cross)
    two_turned = lax.all_gather(turned[:9], "rows", axis=1, tiled=True)
    one_turned = lax.all_gather(after(turned[9:], two_turned), "rows", axis=1, tiled=True)
    cross = swap(part_cross, "chan", 1)
    near = swap(part_near, "chan", 1)
    far = swap((part_far + cross.astype(F32)).astype(BF), "chan", 3)
    long_edge = out((1, images, width, 3 * channels), F32)
    late = [after(piece, part_cross) for piece in merged[pairs:]]
    late = [late[0]] + [swap(late[k], "rows", 2 * k) for k in range(1, pairs)]
    normed_grad, sums, *edges = local_call(
        back_three_sum_kernel,
        [out(act, F32), sums_shape, long_edge, long_edge],
        part_own,
        near,
        far,
        residual,
        cotangent,
        after(loss, *late),
        stats_three,
    )
    normed_rims = rims(*edges)
    sums_three = rows_sum(sums)
    residual_grad, residual_low, conv_two_bias = local_call(
        back_three_kernel,
        [out(act, F32), out(tall, BF), out((1, channels), F32)],
        zi,
        normed_grad,
        residual,
        cotangent,
        *normed_rims,
        stats_three,
        sums_three,
        vectors,
        loss,
    )
    attended, ctx_all = local_call(
        attended_kernel,
        [out(act, BF), out((pairs, 2, HEAD_DIM, CTX_PAD), BF)],
        zi,
        *late,
        scratch=[pltpu.VMEM((pairs, HEAD_DIM, tokens + 2 * CTX_PAD), BF)],
    )
    weights_scratch = [
        xs,
        flat,
        flat,
        pltpu.VMEM((2, pairs, 13, C // row_count, channels), BF),
    ]
    two_grads = local_call(
        weights_two_kernel,
        [out((pairs, 13, C // row_count, channels), BF)] * 2,
        zi,
        *far_rows(*blocks_two),
        residual_low,
        *far_rows(*blocks_three),
        grads,
        attended,
        *far_rows(*cots),
        loss,
        scratch=weights_scratch,
        copies=12,
        flops=conv_flops,
    )
    blocks = chan_blocks(residual_low, *two_grads)
    two_other = swap(two_grads[1], "rows", 1)
    shaped_grad, sums, *edges = local_call(
        conv_two_back_kernel,
        [out(act, F32), sums_shape, edge, edge],
        zi,
        *far_rows(*blocks),
        Far(two_turned),
        vectors,
        hidden,
        stats_two,
        mod,
        scratch=[xs, taps],
        copies=5,
        flops=conv_flops,
    )
    shaped_rims = rims(*edges)
    out_bias = jnp.sum(
        cotangent.astype(F32) * loss_weight[None, :, None, None], axis=(0, 1, 2)
    )[None]
    second = rows_sum(jnp.concatenate([sums, conv_two_bias, qv_bias, out_bias], axis=0))
    sums_two = second[: 2 * images]
    hidden_low, conv_one_bias = local_call(
        back_two_kernel,
        [out(tall, BF), out((1, channels), F32)],
        zi,
        shaped_grad,
        *shaped_rims,
        hidden,
        *hidden_rims,
        stats_two,
        sums_two,
        mod,
        vectors,
    )
    one_grads = local_call(
        weights_one_kernel,
        [out((pairs, 9, C // row_count, channels), BF)] * 2,
        zi,
        *far_rows(*blocks_one),
        hidden_low,
        scratch=[xs, pltpu.VMEM((2, pairs, 9, C // row_count, channels), BF)],
        copies=4,
        flops=conv_flops,
    )
    blocks = chan_blocks(hidden_low, *one_grads)
    terms = weight_scatter(
        (two_grads[0], one_grads[0]), (two_other, swap(one_grads[1], "rows", 1))
    )
    normed_one_grad, sums = local_call(
        conv_one_back_kernel,
        [out(act, F32), sums_shape],
        zi,
        *far_rows(*blocks),
        Far(one_turned),
        vectors,
        pixels,
        stats_one,
        scratch=[xs, taps],
        copies=5,
        flops=conv_flops,
    )
    attended_blocks = chan_blocks(after(attended, sums))
    (activations,) = local_call(
        functools.partial(out_project_kernel, tap=12),
        [out(act, BF)],
        zi,
        *far_rows(*attended_blocks),
        Far(two_full),
        vectors,
        residual,
        scratch=[flat, pltpu.VMEM((1, C, channels), BF)],
        copies=5,
    )

    shift_grad, crossed = sums_two[:images], sums_two[images : 2 * images]
    scale_grad = crossed * vectors[3] + shift_grad * vectors[4]
    embed_grad = jnp.dot(
        embed_rows,
        jnp.concatenate((scale_grad, shift_grad), axis=0),
        precision=lax.Precision.HIGHEST,
    )
    ctx_all = ctx_all[:, :, :, :CTX].reshape(images, heads, 2, HEAD_DIM, CTX)
    ctx_share = DCTX // row_count
    ctx_rows = lax.dynamic_slice_in_dim(context, row * ctx_share, ctx_share, 2)
    context_grad = jnp.einsum(
        "bte,bhsdt->eshd", ctx_rows, ctx_all, preferred_element_type=F32
    ).reshape(2 * ctx_share, channels)
    ctx_value_bias = jnp.sum(ctx_all[:, :, 1].astype(F32), axis=(0, 3)).reshape(1, channels)

    squared = jnp.zeros((1, channels), F32)
    for member in (embed_grad, context_grad):
        squared = squared + jnp.sum((member * member).reshape(-1, channels), axis=0)[None]
    conv_share = (9, C // row_count, channels)
    two_sum, qkv_sum, out_sum, one_sum, payload = local_call(
        finish_kernel,
        [
            out(conv_share, F32),
            out((3,) + conv_share[1:], F32),
            out((1,) + conv_share[1:], F32),
            out(conv_share, F32),
            out((-(-(2 * images + 2) // 8) * 8, channels), F32),
        ],
        *terms,
        squared,
        sums,
        conv_one_bias,
    )
    out_sum = turn_back(out_sum, row_count, chan_count)[0]
    third = rows_sum(payload)
    (pixel_grad,) = local_call(
        back_one_kernel,
        [out(act, F32)],
        normed_one_grad,
        pixels,
        stats_one,
        third,
        vectors,
        residual_grad,
    )
    vector_grad, squares = local_call(
        vector_kernel,
        [out((14, channels), F32), out((8, channels), F32)],
        third,
        second,
        sums_three,
        mod,
        vectors,
        ctx_value_bias,
    )
    squares = [squares] + [swap(squares, "chan", k) for k in (1, 2, 3)]
    squares[0] = after(squares[0], activations, pixel_grad)

    def turn(x):
        return jnp.transpose(x, (1, 0, 2))

    def flat_rows(x):
        return x.reshape(-1, x.shape[2])

    weights = (
        (conv_first, conv_first_moment, conv_first_square, one_sum),
        (conv_second, conv_second_moment, conv_second_square, two_sum),
        (turn(qkv_weight), turn(qkv_weight_moment), turn(qkv_weight_square), qkv_sum),
        (out_weight, out_weight_moment, out_weight_square, out_sum),
        (flat_rows(embed_weight), flat_rows(embed_weight_moment), flat_rows(embed_weight_square), embed_grad),
        (
            flat_rows(context_weight),
            flat_rows(context_weight_moment),
            flat_rows(context_weight_square),
            context_grad,
        ),
        (vectors, vectors_moment, vectors_square, vector_grad),
    )
    outs = [out((1, channels), F32)]
    for weight, *_ in weights:
        outs += [out(weight.shape, F32)] * 3 + [out(weight.shape, BF)]
    operands = [a for group in weights for a in group]
    norm, *updated = local_call(
        update_kernel,
        outs[:-1],
        *squares,
        *(Far(a) for a in operands),
        scratch=[pltpu.VMEM(a.shape, F32) for a in operands],
        copies=len(operands),
    )
    for i in (8, 9, 10, 11):
        updated[i] = turn(updated[i])
    for i in range(16, 24):
        updated[i] = updated[i].reshape(-1, 2, channels)
    return (activations, pixel_grad, norm[0, 0], *updated)


def solution(mesh):
    act = P("rows", None, None, "chan")
    conv = P(None, "rows", "chan")
    wide = P("rows", None, "chan")
    flat = P("rows", "chan")
    vec = P(None, "chan")
    weights = (conv, conv, wide, flat, wide, wide)
    in_specs = (act, act) + (P(),) * 5 + tuple(s for w in weights for s in (w,) * 3) + (vec,) * 3
    out_specs = (act, act, P()) + tuple(s for w in weights for s in (w,) * 4) + (vec,) * 3
    return jax.shard_map(body, mesh=mesh, in_specs=in_specs, out_specs=out_specs, check_vma=False)
```

```python
import functools
import math

import jax
import jax.numpy as jnp
from jax import lax
from jax.experimental import pallas as pl
from jax.experimental.pallas import tpu as pltpu
from jax.sharding import PartitionSpec as P

C = 512
GROUPS = 32
HEAD_DIM = 64
EMB = 2048
DCTX = 2048
IMG_H = 64
IMG_W = 64
CLIP_TOK = 4
STEP = 10
CTX = 81
CTX_PAD = 128
GROUP_SIZE = C // GROUPS
GROUP_COUNT = IMG_H * IMG_W * GROUP_SIZE
LOG2E = 1.4426950408889634
BF = jnp.bfloat16
F32 = jnp.float32
ORDER = (0, 1, 3, 2)

clip_limit = 1.0


def swap(x, axis, distance):
    size = lax.axis_size(axis)
    return lax.ppermute(x, axis, [(i, i ^ distance) for i in range(size)])


def rows_sum(x, first=None):
    size = lax.axis_size("rows")
    x = x + swap(x, "rows", 1) if first is None else first
    step = 2
    while step < size:
        if step * 4 <= size:
            one, two, three = (swap(x, "rows", step * k) for k in (1, 2, 3))
            x = (x + one) + (two + three)
            step *= 4
        else:
            x = x + swap(x, "rows", step)
            step *= 2
    return x


def chan_blocks(x, *beside):
    far = swap(x, "chan", 3)
    near = swap(x, "chan", 1)
    return (x, near, far, swap(after(far, *beside), "chan", 1))


def chan_scatter(own, near, cross, far):
    cross = swap(cross, "chan", 1)
    near = swap(near, "chan", 1)
    return own, near, swap((far + cross.astype(F32)).astype(BF), "chan", 3)


def rims(blocks):
    size = lax.axis_size("rows")
    even = lax.axis_index("rows") % 2 == 0
    top = jnp.stack([x[0] for x in blocks])
    bottom = jnp.stack([x[-1] for x in blocks])
    inside = swap(jnp.where(even, bottom, top), "rows", 1)
    pairs = [(i, i + 1) for i in range(1, size - 1, 2)]
    outside = jnp.where(even, top, bottom)
    outside = lax.ppermute(outside, "rows", pairs + [(j, i) for i, j in pairs])
    shape = (len(blocks), -1, inside.shape[-1])
    return inside.reshape(shape), outside.reshape(shape)


def after(x, *earlier):
    return lax.optimization_barrier((x, *earlier))[0]


def pick(x, index, axis=0):
    return lax.dynamic_index_in_dim(x, index, axis, keepdims=False)


def weight_scatter(mine, other):
    count = mine.shape[0]
    shape = mine.shape[1:]
    total, *low = local_call(
        scatter_kernel, [out(shape, F32)] + [out(shape, BF)] * (count - 1), mine, other
    )
    return [total] + [swap(low[k - 1], "rows", 2 * k) for k in range(1, count)]


class Far:
    def __init__(self, array):
        self.array = array


def near_rows(*arrays):
    return tuple(a.reshape(math.prod(a.shape[:-1]), a.shape[-1]) for a in arrays)


def far_rows(*arrays):
    return tuple(Far(a.reshape(math.prod(a.shape[:-1]), a.shape[-1])) for a in arrays)


def local_call(kernel, outs, *args, scratch=(), copies=0, flops=0, limit=0):
    arrays = [a.array if isinstance(a, Far) else a for a in args]

    def spec(a):
        if isinstance(a, Far):
            return pl.BlockSpec(memory_space=pl.ANY)
        return pl.BlockSpec(memory_space=pltpu.SMEM if a.dtype == jnp.int32 else pltpu.VMEM)

    size = sum(math.prod(a.shape) * a.dtype.itemsize for a in (*arrays, *outs))
    scratch = list(scratch)
    if copies:
        scratch.append(pltpu.SemaphoreType.DMA((copies,)))
    return pl.pallas_call(
        kernel,
        out_shape=tuple(outs),
        in_specs=[spec(a) for a in args],
        out_specs=tuple(pl.BlockSpec(memory_space=pltpu.VMEM) for _ in outs),
        scratch_shapes=scratch,
        compiler_params=pltpu.CompilerParams(vmem_limit_bytes=(limit or (56 if copies else 50)) * 1024 * 1024),
        cost_estimate=pl.CostEstimate(flops=1, bytes_accessed=1, transcendentals=0),
    )(*arrays)


def begin(sems, *moves):
    started = []
    for i, (source, place) in enumerate(moves):
        copy = pltpu.make_async_copy(source, place, sems.at[i])
        copy.start()
        started.append(copy)
    return started


def fetch(sems, *moves):
    for copy in begin(sems, *moves):
        copy.wait()


def lanes_of(xs, j, start=0, size=None):
    width = xs.shape[1] // 4
    size = xs.shape[0] if size is None else size
    return xs.at[start : start + size, j * width : (j + 1) * width]


def block_moves(xs, blocks, start=0):
    return [(x, lanes_of(xs, j, start, x.shape[0])) for j, x in enumerate(blocks)]


def put_rims(xs, zi, inside, outside):
    count, span, width = inside.shape
    last = xs.shape[0] - span
    for j in range(count):
        lanes = slice(j * width, (j + 1) * width)
        xs[pl.ds(pl.multiple_of((1 - zi[4]) * last, span), span), lanes] = inside[j]
        xs[pl.ds(pl.multiple_of(zi[4] * last, span), span), lanes] = outside[j]


def out(shape, dtype):
    return jax.ShapeDtypeStruct(shape, dtype)


def nn(a, b):
    return lax.dot_general(a, b, (((1,), (0,)), ((), ())), preferred_element_type=F32)


def nt(a, b):
    return lax.dot_general(a, b, (((1,), (1,)), ((), ())), preferred_element_type=F32)


def group_mean(x):
    width = x.shape[1]
    left = lax.broadcasted_iota(jnp.int32, (width, width), 0) // GROUP_SIZE
    right = lax.broadcasted_iota(jnp.int32, (width, width), 1) // GROUP_SIZE
    same = (left == right).astype(F32)
    total = lax.dot_general(
        x, same, (((1,), (0,)), ((), ())), precision=lax.Precision.HIGHEST, preferred_element_type=F32
    )
    return total * (1.0 / GROUP_COUNT)


def moments(sums, images):
    means = group_mean(sums)
    average = means[:images]
    return average, lax.rsqrt(means[images:] - average * average + 1e-05)


def image_of(ref, b):
    rows, _, width, channels = ref.shape
    return ref[:, b].reshape(rows * width, channels)


def put_image(ref, b, value):
    rows, _, width, channels = ref.shape
    ref[:, b] = value.reshape(rows, width, channels).astype(ref.dtype)


def column_sum(x):
    return jnp.sum(x, axis=0, keepdims=True)


def silu(z):
    return z * jax.nn.sigmoid(z)


def silu_slope(z):
    s = jax.nn.sigmoid(z)
    return s * (1.0 + z * (1.0 - s))


def put_sums(sums, b, images, v, w):
    sums[b : b + 1] = column_sum(v)
    sums[images + b : images + b + 1] = column_sum(v * w)


def start_kernel(pixels, sums):
    images = pixels.shape[1]
    for b in range(images):
        v = image_of(pixels, b)
        put_sums(sums, b, images, v, v)


def act_one_kernel(x, sums, vec, o):
    images = x.shape[1]
    average, inverse = moments(sums[...], images)
    for b in range(images):
        xhat = (image_of(x, b) - average[b : b + 1]) * inverse[b : b + 1]
        put_image(o, b, silu(xhat * vec[0:1] + vec[1:2]))


def shaped_of(xhat, mod, vec, b, images):
    scale = 1.0 + (mod[b : b + 1] + vec[12:13])
    shift = mod[images + b : images + b + 1] + vec[13:14]
    return (xhat * vec[3:4] + vec[4:5]) * scale + shift


def act_two_kernel(x, sums, mod, vec, o):
    images = x.shape[1]
    average, inverse = moments(sums[...], images)
    for b in range(images):
        xhat = (image_of(x, b) - average[b : b + 1]) * inverse[b : b + 1]
        put_image(o, b, silu(shaped_of(xhat, mod, vec, b, images)))


def norm_three_kernel(x, sums, vec, o):
    images = x.shape[1]
    average, inverse = moments(sums[...], images)
    for b in range(images):
        xhat = (image_of(x, b) - average[b : b + 1]) * inverse[b : b + 1]
        put_image(o, b, xhat * vec[6:7] + vec[7:8])


def rows_of(z, j, width):
    return pl.ds(pl.multiple_of((z ^ ORDER[j]) * width, width), width)


def shifted(x, by, width):
    length = x.shape[0]
    column = lax.broadcasted_iota(jnp.int32, x.shape, 0) % width
    moved = pltpu.roll(x, by % length, 0)
    return jnp.where(column == (0 if by == 1 else width - 1), 0.0, moved)


def conv_taps(blocks, edges, w, extra, zi, xs, rows, span, width):
    z = zi[0]
    if extra:
        w_far, (w, sems) = w, extra
        copies = begin(sems, (w_far.at[0:9], w), *block_moves(xs, blocks, span))
        put_rims(xs, zi, *edges)
        for copy in copies:
            copy.wait()
    else:
        put_rims(xs, zi, *edges)
        for j, x in enumerate(blocks):
            lanes_of(xs, j, span, x.shape[0])[...] = x[...]
    channels = w.shape[2]
    parts = []
    for dx in range(3):
        total = None
        for dy in range(3):
            at = dy * span
            a = xs[at : at + rows * span, :]
            taps = [w[3 * dy + dx, rows_of(z, j, channels), :] for j in range(4)]
            term = nn(a, jnp.concatenate(taps, axis=0))
            total = term if total is None else total + term
        parts.append(total)
    return parts[1] + shifted(parts[0], 1, width) + shifted(parts[2], -1, width)


def conv_one_kernel(zi, x0, x1, x2, x3, e0, e1, w_far, vec, hidden, sums, xs, *extra):
    rows, images, width, channels = hidden.shape
    blocks = (x0, x1, x2, x3)
    result = conv_taps(
        blocks, (e0, e1), w_far, extra, zi, xs, rows, images * width, width
    ) + vec[2:3]
    hidden[...] = result.reshape(hidden.shape)
    for b in range(images):
        v = image_of(hidden, b)
        put_sums(sums, b, images, v, v)


def conv_two_kernel(zi, x0, x1, x2, x3, e0, e1, w_far, vec, pixels, residual, sums, xs, *extra):
    rows, images, width, channels = residual.shape
    blocks = (x0, x1, x2, x3)
    result = conv_taps(
        blocks, (e0, e1), w_far, extra, zi, xs, rows, images * width, width
    ) + vec[5:6]
    residual[...] = pixels[...] + result.reshape(residual.shape)
    for b in range(images):
        v = image_of(residual, b)
        put_sums(sums, b, images, v, v)


def conv_back_kernel(zi, r, e0, e1, w, own, near, cross, far, xs, *, first):
    rows, images, width, channels = r.shape
    span = images * width
    put_rims(xs, zi, e0, e1)
    xs[span : span + rows * span] = r[...].reshape(rows * span, channels)
    wide = xs[...].astype(F32)
    turned = [shifted(wide, -1, width).astype(BF), xs[...], shifted(wide, 1, width).astype(BF)]
    taps = [(dy, dx) for dy in range(3) for dx in range(3)]
    a = jnp.concatenate(
        [turned[dx][(2 - dy) * span : (2 - dy + rows) * span] for dy, dx in taps], axis=1
    )
    for j, part in enumerate((own, near, far, cross)):
        at = rows_of(zi[0], j, channels)
        b = jnp.concatenate([w[first + 3 * dy + dx, at, :] for dy, dx in taps], axis=1)
        part[...] = nt(a, b).astype(part.dtype).reshape(part.shape)


def total_image(terms, b):
    total = image_of(terms[0], b)
    for term in terms[1:]:
        total = total + image_of(term, b).astype(F32)
    return total


def back_two_sum_kernel(t0, t1, t2, vec, hidden, stats, mod, shaped_grad, sums):
    images = hidden.shape[1]
    average, inverse = moments(stats[...], images)
    for b in range(images):
        xhat = (image_of(hidden, b) - average[b : b + 1]) * inverse[b : b + 1]
        g = total_image((t0, t1, t2), b) * silu_slope(shaped_of(xhat, mod, vec, b, images))
        put_image(shaped_grad, b, g)
        put_sums(sums, b, images, g, xhat)


def back_one_sum_kernel(t0, t1, t2, vec, pixels, stats, residual_grad, partial, sums):
    images = pixels.shape[1]
    average, inverse = moments(stats[0 : 2 * images], images)
    for b in range(images):
        xhat = (image_of(pixels, b) - average[b : b + 1]) * inverse[b : b + 1]
        g = total_image((t0, t1, t2), b) * silu_slope(xhat * vec[0:1] + vec[1:2])
        put_image(partial, b, image_of(residual_grad, b) + g * (inverse[b : b + 1] * vec[0:1]))
        put_sums(sums, b, images, g, xhat)


def put_shares(box, zi, tap, grad, base=0):
    share, channels = box.shape[3:]
    each = channels // share
    for j in range(4):
        for i in range(each):
            at = j * channels + i * share
            row = (zi[0] ^ ORDER[j]) * each + i
            box[(row & 1) ^ zi[4], (row >> 1) ^ base, tap] = grad[at : at + share].astype(box.dtype)


def conv_weights(zi, xs, r, box, base=0):
    rows, images, width, channels = r.shape
    span = images * width
    turned = xs[...].T
    wide = r[...].reshape(rows * span, channels).astype(F32)
    three = jnp.concatenate(
        [shifted(wide, -1, width).astype(BF), wide.astype(BF), shifted(wide, 1, width).astype(BF)],
        axis=1,
    )
    for dy in range(3):
        grad = nn(turned[:, dy * span : (dy + rows) * span], three)
        for dx in range(3):
            put_shares(box, zi, 3 * dy + dx, grad[:, dx * channels : (dx + 1) * channels], base)


def weights_two_kernel(
    zi, x0, x1, x2, x3, e0, e1, r, n0, n1, n2, n3, grads, att, c0, c1, c2, c3, loss, mine, other, xs, ns, cs, box, sems
):
    blocks = begin(
        sems,
        *block_moves(xs, (x0, x1, x2, x3), e0.shape[1]),
        *block_moves(ns, (n0, n1, n2, n3)),
        *block_moves(cs, (c0, c1, c2, c3)),
    )
    put_rims(xs, zi, e0, e1)
    for copy in blocks[:4]:
        copy.wait()
    conv_weights(zi, xs, r, box)
    for copy in blocks[4:]:
        copy.wait()
    rows, images, width, columns = grads.shape
    channels = att.shape[3]
    pixels = rows * images * width
    grad = nn(ns[...].T, grads[...].reshape(pixels, columns))
    for s in range(3):
        put_shares(box, zi, 9 + s, grad[:, s * channels : (s + 1) * channels])
    scale = jnp.concatenate([loss[b : b + 1] for b in range(images)], axis=0)
    scale = jnp.concatenate([scale] * 4, axis=1)[None, :, None, :]
    low = (cs[...].reshape(rows, images, width, 4 * channels).astype(F32) * scale).astype(BF)
    grad = nn(att[...].reshape(pixels, channels).T, low.reshape(pixels, 4 * channels))
    by_output = [grad[:, j * channels : (j + 1) * channels] for j in range(4)]
    put_shares(box, zi, 12, jnp.concatenate(by_output, axis=0))
    mine[...] = box[0]
    other[...] = box[1]


def weights_one_kernel(zi, x0, x1, x2, x3, e0, e1, r, mine, other, xs, box, sems):
    copies = begin(sems, *block_moves(xs, (x0, x1, x2, x3), e0.shape[1]))
    put_rims(xs, zi, e0, e1)
    for copy in copies:
        copy.wait()
    conv_weights(zi, xs, r, box, zi[1])
    mine[...] = box[0]
    other[...] = box[1]


def pair_sum_kernel(mine, other, o):
    o[...] = (mine[...].astype(F32) + other[...].astype(F32)).astype(BF)


def scatter_kernel(mine, other, total, *low):
    total[...] = mine[0].astype(F32) + other[0].astype(F32)
    for k, o in enumerate(low):
        o[...] = (mine[k + 1].astype(F32) + other[k + 1].astype(F32)).astype(BF)


def put_heads(scratch, leading, value, b, heads):
    turned = value.T.astype(scratch.dtype)
    for h in range(heads):
        scratch[b * heads + h, leading] = turned[h * HEAD_DIM : (h + 1) * HEAD_DIM]


def project_kernel(*refs, base):
    zi, w_far, vec, grads, blocks = refs[0], refs[1], refs[2], refs[3], refs[4:8]
    outs, (xs, w, scratch, sems) = refs[8:-4], refs[-4:]
    fetch(sems, (w_far.at[base : base + 3], w), *block_moves(xs, blocks))
    tokens = outs[0].shape[2]
    channels = w.shape[2]
    heads = channels // HEAD_DIM
    images = len(outs) // heads
    rows = xs.shape[0] // (images * IMG_W)
    a = xs[...]
    for s in range(3):
        rows_in = [w[s, rows_of(zi[0], j, channels), :] for j in range(4)]
        value = nn(a, jnp.concatenate(rows_in, axis=0))
        if s != 1:
            at = 8 if s == 0 else 9
            value = value + vec[at : at + 1]
        split = value.reshape(rows, images, IMG_W, channels)
        for b in range(images):
            put_heads(scratch, s, split[:, b].reshape(tokens, channels), b, heads)
    for k, o in enumerate(outs):
        o[0:3] = scratch[zi[1] ^ k]
        o[3] = grads[zi[1] ^ k, 0]


def output_grad_kernel(c0, c1, c2, c3, w0, w1, w2, w3, loss, o, xs, sems):
    fetch(sems, *block_moves(xs, (c0, c1, c2, c3)))
    images, channels = loss.shape
    heads = channels // HEAD_DIM
    tokens = o.shape[3]
    turned = jnp.concatenate([w[...] for w in (w0, w1, w2, w3)], axis=1)
    wide = xs[...].reshape(tokens // IMG_W, images, IMG_W, 4 * channels)
    for b in range(images):
        scale = jnp.concatenate([loss[b : b + 1]] * 4, axis=1)
        low = (wide[:, b].reshape(tokens, 4 * channels).astype(F32) * scale).astype(BF)
        put_heads(o, 0, nt(low, turned), b, heads)


def attention_kernel(*refs, chunk, count, block):
    live, ctx_ref = refs[0], refs[1]
    mine, sibs = (refs[2 + i * count : 2 + (i + 1) * count] for i in range(2))
    oq_ref, own_ref, other_ref = refs[2 + 2 * count : 5 + 2 * count]
    q_s, do_s, kt_s, k_s, v_s, s_s, p_s, acc_s = refs[5 + 2 * count :]
    step = pl.program_id(0)
    last = pl.num_programs(0) - 1
    tokens = mine[0].shape[2]
    depth = HEAD_DIM
    queries = block
    half = count * tokens
    keys = 2 * half
    extra = ctx_ref.shape[2]

    @pl.when(step == 0)
    def _():
        for k in range(count):
            lanes = slice(k * tokens, (k + 1) * tokens)
            q_s[:, lanes] = mine[k][0]
            do_s[:, lanes] = mine[k][3]
            kt_s[:, :, lanes] = mine[k][1:3]
            kt_s[:, :, half + k * tokens : half + (k + 1) * tokens] = sibs[k][1:3]
        kt_s[:, :, keys:] = ctx_ref[...]
        k_s[...] = kt_s[0].T
        v_s[...] = kt_s[1].T
        acc_s[...] = jnp.zeros_like(acc_s)

    here = pl.ds(pl.multiple_of(step * block, block), block)
    q = q_s[:, here]
    do = do_s[:, here]
    spans = [(i * chunk, chunk) for i in range(keys // chunk)] + [(keys, extra)]
    highest = None
    for at, size in spans:
        s = nn(k_s[at : at + size], q)
        if at == keys:
            position = lax.broadcasted_iota(jnp.int32, s.shape, 0)
            s = jnp.where(position < live[0], s, -1e30)
        s_s[at : at + size] = s
        top = jnp.max(s.reshape(size // 8, 8, queries), axis=0)
        highest = top if highest is None else jnp.maximum(highest, top)
    factor = 0.125 * LOG2E
    peak = jnp.max(highest, axis=0, keepdims=True) * factor
    weight_sum = jnp.zeros((8, queries), F32)
    mixture = jnp.zeros((depth, queries), F32)
    for at, size in spans:
        p = jnp.exp2(s_s[at : at + size] * factor - peak)
        weight_sum = weight_sum + jnp.sum(p.reshape(size // 8, 8, queries), axis=0)
        low = p.astype(BF)
        p_s[at : at + size] = low
        mixture = mixture + nn(kt_s[1, :, at : at + size], low)
    inverse = 1.0 / jnp.sum(weight_sum, axis=0, keepdims=True)
    attended = mixture * inverse
    oq_ref[0] = attended.astype(BF)
    delta = jnp.sum(do.astype(F32) * attended, axis=0, keepdims=True)
    do_scaled = (do.astype(F32) * inverse).astype(BF)
    q_scaled = (q.astype(F32) * (inverse * 0.125)).astype(BF)
    query_grad = jnp.zeros((depth, queries), F32)
    for at, size in spans:
        dprob = nn(v_s[at : at + size], do)
        low = p_s[at : at + size]
        dscore = (low.astype(F32) * (dprob - delta)).astype(BF)
        query_grad = query_grad + nn(kt_s[0, :, at : at + size], dscore)
        acc_s[0, :, at : at + size] += nt(q_scaled, dscore)
        acc_s[1, :, at : at + size] += nt(do_scaled, low)
    oq_ref[1] = (query_grad * (inverse * 0.125)).astype(BF)

    @pl.when(step == last)
    def _():
        own_ref[:, :, 0:half] = acc_s[:, :, 0:half].astype(BF)
        own_ref[:, :, half:] = acc_s[:, :, keys:].astype(BF)
        other_ref[...] = acc_s[:, :, half:].astype(BF)


def attention(live, ctx, mine, sibs):
    count = len(mine)
    _, depth, tokens = mine[0].shape
    queries = count * tokens
    total = 2 * queries + ctx.shape[2]
    block = min(512, queries)
    chunk = min(1024, 2 * queries)

    def whole(a):
        return pl.BlockSpec(a.shape, lambda i: (0,) * len(a.shape))

    outs = (
        out((2, depth, queries), BF),
        out((2, depth, queries + ctx.shape[2]), BF),
        out((2, depth, queries + ctx.shape[2]), BF),
    )
    arrays = (ctx, *mine, *sibs)
    return pl.pallas_call(
        functools.partial(attention_kernel, chunk=chunk, count=count, block=block),
        grid=(queries // block,),
        in_specs=[pl.BlockSpec(memory_space=pltpu.SMEM)] + [whole(a) for a in arrays],
        out_specs=(
            pl.BlockSpec((2, depth, block), lambda i: (0, 0, i)),
            whole(outs[1]),
            whole(outs[2]),
        ),
        out_shape=outs,
        scratch_shapes=[
            pltpu.VMEM((depth, queries), BF),
            pltpu.VMEM((depth, queries), BF),
            pltpu.VMEM((2, depth, total), BF),
            pltpu.VMEM((total, depth), BF),
            pltpu.VMEM((total, depth), BF),
            pltpu.VMEM((total, block), F32),
            pltpu.VMEM((total, block), BF),
            pltpu.VMEM((2, depth, total), F32),
        ],
        compiler_params=pltpu.CompilerParams(
            vmem_limit_bytes=56 * 1024 * 1024, dimension_semantics=("arbitrary",)
        ),
        cost_estimate=pl.CostEstimate(
            flops=12 * depth * queries * total, bytes_accessed=8 * depth * total, transcendentals=queries * total
        ),
    )(live, *arrays)


def merge_kernel(oq_far, own_far, other_far, *refs):
    oq, own, other, sems = refs[-4:]
    outs = refs[:-4]
    count = len(outs) // 2
    fetch(sems, (oq_far, oq), (own_far, own), (other_far, other))
    tokens = oq.shape[2] // count
    both = (own[...].astype(F32) + other[...].astype(F32)).astype(BF)
    for k in range(count):
        lanes = slice(k * tokens, (k + 1) * tokens)
        outs[k][0] = oq[1, :, lanes]
        outs[k][1:3] = both[:, :, lanes]
        outs[count + k][:, 0:tokens] = oq[0, :, lanes]
        for s in range(2):
            at = tokens + s * CTX_PAD
            outs[count + k][:, at : at + CTX_PAD] = both[s, :, count * tokens :]


def back_project_kernel(*refs, base, count):
    zi, w_far, pieces = refs[0], refs[1], refs[2 : 2 + count]
    grads, part_own, part_near, part_cross, part_far, biases = refs[2 + count : -3]
    rec, w, sems = refs[-3:]
    fetch(sems, (w_far.at[base : base + 3], w))
    rows, images, width, channels = part_own.shape
    heads = channels // HEAD_DIM
    for k in range(count):
        rec[zi[1] ^ k] = pieces[k][...]
    for b in range(images):
        for s in range(3):
            blocks = [rec[b * heads + h, s] for h in range(heads)]
            value = jnp.concatenate(blocks, axis=0).T.reshape(rows, width, channels)
            grads[:, b, :, s * channels : (s + 1) * channels] = value
    flat = grads[...].reshape(rows * images * width, 3 * channels)
    for j, part in enumerate((part_own, part_near, part_far, part_cross)):
        at = rows_of(zi[0], j, channels)
        taps = jnp.concatenate([w[s, at, :] for s in range(3)], axis=1)
        part[...] = nt(flat, taps).astype(part.dtype).reshape(part.shape)
    wide = flat.astype(F32)
    biases[0:1] = column_sum(wide[:, 0:channels])
    biases[1:2] = column_sum(wide[:, 2 * channels :])


def attended_kernel(*refs):
    zi, pieces = refs[0], refs[1:-3]
    attended, ctx, rec = refs[-3:]
    rows, images, width, channels = attended.shape
    heads = channels // HEAD_DIM
    tokens = rows * width
    for k, piece in enumerate(pieces):
        rec[zi[1] ^ k] = piece[...]
    for b in range(images):
        blocks = [rec[b * heads + h, :, 0:tokens] for h in range(heads)]
        attended[:, b] = jnp.concatenate(blocks, axis=0).T.reshape(rows, width, channels)
    for q in range(len(pieces)):
        for s in range(2):
            at = tokens + s * CTX_PAD
            ctx[q, s] = rec[q, :, at : at + CTX_PAD]


def out_project_kernel(zi, x0, x1, x2, x3, w_far, vec, residual, o, xs, w, sems, *, tap):
    fetch(sems, (w_far.at[tap : tap + 1], w), *block_moves(xs, (x0, x1, x2, x3)))
    channels = w.shape[2]
    rows_in = [w[0, rows_of(zi[0], j, channels), :] for j in range(4)]
    value = nn(xs[...], jnp.concatenate(rows_in, axis=0)) + vec[10:11]
    o[...] = (residual[...] + value.reshape(o.shape)).astype(BF)


def back_three_sum_kernel(t0, t1, t2, residual, stats, g_out, sums):
    images = residual.shape[1]
    average, inverse = moments(stats[...], images)
    for b in range(images):
        g = image_of(t0, b).astype(F32) + image_of(t1, b).astype(F32) + image_of(t2, b).astype(F32)
        xhat = (image_of(residual, b) - average[b : b + 1]) * inverse[b : b + 1]
        put_image(g_out, b, g)
        put_sums(sums, b, images, g, xhat)


def back_three_kernel(g0, x0, c0, stats, sums, vec, loss, residual_grad, low, bias):
    images = x0.shape[1]
    average, inverse = moments(stats[...], images)
    means = group_mean(sums[...] * vec[6:7])
    total = None
    for b in range(images):
        xhat = (image_of(x0, b) - average[b : b + 1]) * inverse[b : b + 1]
        g = image_of(g0, b) * vec[6:7] - means[b : b + 1] - xhat * means[images + b : images + b + 1]
        g = image_of(c0, b).astype(F32) * loss[b : b + 1] + inverse[b : b + 1] * g
        put_image(residual_grad, b, g)
        put_image(low, b, g)
        part = column_sum(g)
        total = part if total is None else total + part
    bias[...] = total


def back_two_kernel(g0, x0, stats, sums, mod, vec, low, bias):
    images = x0.shape[1]
    average, inverse = moments(stats[...], images)
    gains = [vec[3:4] * (1.0 + (mod[b : b + 1] + vec[12:13])) for b in range(images)]
    means = group_mean(sums[0 : 2 * images] * jnp.concatenate(gains + gains, axis=0))
    total = None
    for b in range(images):
        xhat = (image_of(x0, b) - average[b : b + 1]) * inverse[b : b + 1]
        g = image_of(g0, b) * gains[b]
        g = g - means[b : b + 1] - xhat * means[images + b : images + b + 1]
        g = inverse[b : b + 1] * g
        put_image(low, b, g)
        part = column_sum(g)
        total = part if total is None else total + part
    bias[...] = total


def back_one_kernel(partial, pixels, stats, sums, vec, pixel_grad):
    images = pixels.shape[1]
    average, inverse = moments(stats[0 : 2 * images], images)
    means = group_mean(sums[0 : 2 * images] * vec[0:1])
    for b in range(images):
        slope = inverse[b : b + 1] * inverse[b : b + 1] * means[images + b : images + b + 1]
        level = inverse[b : b + 1] * means[b : b + 1] - average[b : b + 1] * slope
        put_image(pixel_grad, b, image_of(partial, b) - (image_of(pixels, b) * slope + level))


RATES = (0.02, 0.02, 0.08, 1.0, 0.02, 0.04, 1.0)


def finish_kernel(*refs):
    terms, (squares, sums, bias, two_sum, qkv_sum, out_sum, one_sum, payload) = refs[:-8], refs[-8:]
    squared = squares[...]
    at = 0
    for o in (two_sum, qkv_sum, out_sum, one_sum):
        if o is one_sum:
            total = terms[1][...]
            for term in terms[2:]:
                total = total + term[...].astype(F32)
        else:
            total = terms[0][at : at + o.shape[0]].astype(F32)
            at += o.shape[0]
        o[...] = total
        squared = squared + column_sum((total * total).reshape(-1, total.shape[-1]))
    count = sums.shape[0]
    payload[0:count] = sums[...]
    payload[count : count + 1] = bias[...]
    payload[count + 1 : count + 2] = squared
    payload[count + 2 :] = jnp.zeros((payload.shape[0] - count - 2, payload.shape[1]), F32)


def vector_kernel(third, second, sums_three, mod, vec, ctx, grad, squares):
    images = sums_three.shape[0] // 2

    def total(ref, at):
        return column_sum(ref[at : at + images])

    scale = 1.0 + (mod[0:images] + vec[12:13])
    shift_grad = second[0:images]
    crossed = second[images : 2 * images]
    scale_grad = crossed * vec[3:4] + shift_grad * vec[4:5]
    at = 2 * images
    rows = (
        total(third, images),
        total(third, 0),
        third[at : at + 1],
        column_sum(scale * crossed),
        column_sum(scale * shift_grad),
        second[at : at + 1],
        total(sums_three, images),
        total(sums_three, 0),
        second[at + 1 : at + 2],
        second[at + 2 : at + 3],
        second[at + 3 : at + 4],
        ctx[...],
        column_sum(scale_grad),
        column_sum(shift_grad),
    )
    squared = third[at + 1 : at + 2]
    for i, row in enumerate(rows):
        grad[i : i + 1] = row
        squared = squared + row * row
    squares[...] = jnp.broadcast_to(squared, squares.shape)


def update_kernel(*refs):
    count = len(RATES)
    squares, given = refs[0:4], refs[4 : 4 + 4 * count]
    made, held, sems = refs[4 + 4 * count : -3 * count - 1], refs[-3 * count - 1 : -1], refs[-1]
    far = [a for i, a in enumerate(given) if i % 4 < 3]
    arriving = begin(sems, *zip(far, held))
    near = squares[0][0:1] + squares[1][0:1]
    total = jnp.sum(near + (squares[2][0:1] + squares[3][0:1]), axis=1, keepdims=True)
    norm = jnp.sqrt(total)
    made[0][...] = jnp.broadcast_to(norm, made[0].shape)
    factor = jnp.minimum(1.0, clip_limit / norm)
    at = 1
    for i, rate in enumerate(RATES):
        for copy in arriving[3 * i : 3 * i + 3]:
            copy.wait()
        weight, moment, square = held[3 * i : 3 * i + 3]
        gradient = given[4 * i + 3]
        decay = 0.0 if i == count - 1 else 0.01
        scale = factor.reshape((1,) * (len(weight.shape) - 2) + factor.shape)
        new = adamw(weight[...], moment[...], square[...], gradient[...] * scale, rate, decay)
        for value in new:
            made[at][...] = value
            at += 1
        if i < count - 1:
            made[at][...] = new[0].astype(BF)
            at += 1


def adamw(weight, moment, square, gradient, step_rate, weight_decay):
    moment_new = 0.9 * moment + 0.1 * gradient
    square_new = 0.999 * square + 0.001 * gradient * gradient
    corrected = moment_new / (1.0 - 0.9**STEP)
    scaled = square_new / (1.0 - 0.999**STEP)
    weight_new = weight - step_rate * (
        corrected / (jnp.sqrt(scaled) + 1e-08) + weight_decay * weight
    )
    return (weight_new, moment_new, square_new)


def turn_moves(row_count, chan_count):
    share = row_count // chan_count
    return [
        (r * chan_count + z, (z * share + r % share) * chan_count + r // share)
        for r in range(row_count)
        for z in range(chan_count)
    ]


def turn_back(x, row_count, chan_count):
    moves = [(j, i) for i, j in turn_moves(row_count, chan_count)]
    return lax.ppermute(x, ("rows", "chan"), moves)


def body(
    pixels,
    cotangent,
    loss_weight,
    timesteps,
    clip_embed,
    context,
    text_len,
    conv_first,
    conv_first_moment,
    conv_first_square,
    conv_second,
    conv_second_moment,
    conv_second_square,
    qkv_weight,
    qkv_weight_moment,
    qkv_weight_square,
    out_weight,
    out_weight_moment,
    out_weight_square,
    embed_weight,
    embed_weight_moment,
    embed_weight_square,
    context_weight,
    context_weight_moment,
    context_weight_square,
    vectors,
    vectors_moment,
    vectors_square,
):
    row_count = lax.axis_size("rows")
    chan_count = lax.axis_size("chan")
    row = lax.axis_index("rows")
    chan = lax.axis_index("chan")
    local_rows, images, width, channels = pixels.shape
    heads = channels // HEAD_DIM
    pairs = images * heads
    assert chan_count == 4 and row_count == 2 * pairs
    pair = row // 2
    zi = jnp.stack(
        [chan, pair, row, row_count - 1 - row, row % 2]
    ).astype(jnp.int32)
    act = (local_rows, images, width, channels)
    edge_rows = (local_rows + 2) * images * width
    xs = pltpu.VMEM((edge_rows, C), BF)
    flat = pltpu.VMEM((local_rows * images * width, C), BF)
    taps = pltpu.VMEM((9, C, channels), BF)
    conv_flops = 2 * local_rows * images * width * 9 * C * channels

    (sums,) = local_call(start_kernel, [out((2 * images, channels), F32)], pixels)
    loss = jnp.broadcast_to(loss_weight[:, None], (images, channels))
    cot = after(cotangent, sums)
    cot_near, cot_far = swap(cot, "chan", 1), swap(cot, "chan", 3)

    sums_shape = out((2 * images, channels), F32)
    by_chip = sums + swap(sums, "rows", 1)
    stats_one = rows_sum(sums, by_chip)

    one_full = lax.all_gather(after(conv_first, by_chip).astype(BF), "rows", axis=1, tiled=True)
    (active_one,) = local_call(
        act_one_kernel, [out(act, BF)], pixels, after(stats_one, cot_near, cot_far), vectors
    )
    blocks_one = chan_blocks(active_one)
    arrived = blocks_one[1:3]
    two_low = after(conv_second, *arrived).astype(BF)
    qkv_low = jnp.transpose(after(qkv_weight, *arrived), (1, 0, 2)).astype(BF)
    out_low = after(out_weight, *arrived).astype(BF)[None]
    two_full = lax.all_gather(
        jnp.concatenate([two_low, qkv_low, out_low], axis=0), "rows", axis=1, tiled=True
    )
    ctx_full = lax.all_gather(
        after(context_weight, *arrived).astype(BF), "rows", axis=0, tiled=True
    )

    share = EMB // row_count
    index = row * share + jnp.arange(share, dtype=jnp.int32)
    half_width = EMB // 2
    frequency = jnp.exp(-math.log(10000.0) * (index % half_width).astype(F32) / half_width)
    phases = after(timesteps, active_one).astype(F32)[:, None] * frequency[None, :]
    features = jnp.where(index[None, :] < half_width, jnp.cos(phases), jnp.sin(phases))
    clip_share = lax.dynamic_slice_in_dim(clip_embed, row * share, share, 1)
    embedding = jax.nn.silu(features + clip_share).astype(BF)
    both = jnp.eye(2, dtype=F32)[None, :, :, None]
    embed_rows = (embedding.astype(F32).T[:, None, None, :] * both).reshape(2 * share, 2 * images)
    modulation = jnp.einsum(
        "be,esc->sbc",
        embedding,
        after(embed_weight, active_one).astype(BF),
        preferred_element_type=F32,
    ).reshape(2 * images, channels)

    cot_cross = swap(after(cot_far, *blocks_one), "chan", 1)
    rims_one = rims(blocks_one)
    hidden, sums = local_call(
        conv_one_kernel,
        [out(act, F32), sums_shape],
        zi,
        *near_rows(*blocks_one),
        *rims_one,
        one_full,
        vectors,
        scratch=[xs],
        flops=conv_flops,
    )
    stats_two = rows_sum(jnp.concatenate([after(sums, cot_cross), modulation], axis=0))
    stats_two, mod = stats_two[: 2 * images], stats_two[2 * images :]
    (active_two,) = local_call(
        act_two_kernel, [out(act, BF)], hidden, stats_two, mod, vectors
    )

    blocks_two = chan_blocks(active_two)

    def out_rows(owner):
        return lax.dynamic_slice_in_dim(two_full[12], owner * channels, channels, 0)

    out_part = [out_rows(chan)] + [swap(out_rows(chan ^ k), "chan", k) for k in ORDER[1:]]
    tokens = local_rows * width
    cots = (cotangent, cot_near, cot_far, cot_cross)
    (attended_grad,) = local_call(
        output_grad_kernel,
        [out((pairs, 1, HEAD_DIM, tokens), BF)],
        *far_rows(*(after(a, active_two) for a in cots)),
        *out_part,
        loss,
        scratch=[flat],
        copies=4,
    )
    ctx_share = DCTX // row_count
    ctx_rows = lax.dynamic_slice_in_dim(context, row * ctx_share, ctx_share, 2)
    ctx_rows = jnp.transpose(ctx_rows, (2, 0, 1)).reshape(ctx_share, 1, 1, -1)
    ctx_rows = (ctx_rows * jnp.eye(2, dtype=BF)[None, :, :, None]).reshape(2 * ctx_share, -1)
    rims_two = rims((after(blocks_two[0], attended_grad), *blocks_two[1:]))
    residual, sums = local_call(
        conv_two_kernel,
        [out(act, F32), sums_shape],
        zi,
        *far_rows(*blocks_two),
        *rims_two,
        Far(two_full),
        after(vectors, ctx_rows, embed_rows),
        pixels,
        scratch=[xs, taps],
        copies=5,
        flops=conv_flops,
    )
    stats_three = rows_sum(sums)
    (normed,) = local_call(norm_three_kernel, [out(act, BF)], residual, stats_three, vectors)
    blocks_three = chan_blocks(normed)

    image, head = pair // heads, pair % heads
    ctx_low = pick(context, image)
    ctx_projected = jnp.einsum("te,esc->sct", ctx_low, ctx_full, preferred_element_type=F32)
    ctx_bias = jnp.stack([jnp.zeros_like(vectors[11]), vectors[11]])[:, :, None]
    ctx_heads = lax.dynamic_slice_in_dim(ctx_projected + ctx_bias, head * HEAD_DIM, HEAD_DIM, 1)
    ctx_heads = jnp.pad(ctx_heads.astype(BF), ((0, 0), (0, 0), (0, CTX_PAD - CTX)))
    live = (CLIP_TOK + pick(text_len, image))[None].astype(jnp.int32)

    pieces = local_call(
        functools.partial(project_kernel, base=9),
        [out((4, HEAD_DIM, tokens), BF)] * pairs,
        zi,
        Far(two_full),
        after(vectors, ctx_heads),
        attended_grad,
        *far_rows(*blocks_three),
        scratch=[
            flat,
            pltpu.VMEM((3, C, channels), BF),
            pltpu.VMEM((pairs, 3, HEAD_DIM, tokens), BF),
        ],
        copies=5,
        flops=conv_flops // 3,
    )
    pieces = [pieces[0]] + [swap(pieces[k], "rows", 2 * k) for k in range(1, pairs)]
    siblings = [swap(piece, "rows", 1) for piece in pieces]

    out_query, own, other = attention(live, ctx_heads, pieces, siblings)
    merged = local_call(
        merge_kernel,
        [out((3, HEAD_DIM, tokens), BF)] * pairs
        + [out((HEAD_DIM, tokens + 2 * CTX_PAD), BF)] * pairs,
        Far(out_query),
        Far(own),
        Far(swap(other, "rows", 1)),
        scratch=[
            pltpu.VMEM(out_query.shape, BF),
            pltpu.VMEM(own.shape, BF),
            pltpu.VMEM(own.shape, BF),
        ],
        copies=3,
    )
    received = [merged[0]] + [swap(merged[k], "rows", 2 * k) for k in range(1, pairs)]

    grads, part_own, part_near, part_cross, part_far, qv_bias = local_call(
        functools.partial(back_project_kernel, base=9, count=pairs),
        [
            out((local_rows, images, width, 3 * channels), BF),
            out(act, F32),
            out(act, BF),
            out(act, BF),
            out(act, F32),
            out((2, channels), F32),
        ],
        zi,
        Far(two_full),
        *received,
        scratch=[
            pltpu.VMEM((pairs, 3, HEAD_DIM, tokens), BF),
            pltpu.VMEM((3, C, channels), BF),
        ],
        copies=1,
        flops=conv_flops // 3,
    )
    normed_terms = chan_scatter(part_own, part_near, part_cross, part_far)
    late = [after(piece, part_cross) for piece in merged[pairs:]]
    late = [late[0]] + [swap(late[k], "rows", 2 * k) for k in range(1, pairs)]
    normed_grad, sums = local_call(
        back_three_sum_kernel,
        [out(act, F32), sums_shape],
        *normed_terms,
        residual,
        after(stats_three, *late),
    )
    sums_three = rows_sum(sums)
    residual_grad, residual_low, conv_two_bias = local_call(
        back_three_kernel,
        [out(act, F32), out(act, BF), out((1, channels), F32)],
        normed_grad,
        residual,
        cotangent,
        stats_three,
        sums_three,
        vectors,
        loss,
    )
    attended, ctx_all = local_call(
        attended_kernel,
        [out(act, BF), out((pairs, 2, HEAD_DIM, CTX_PAD), BF)],
        zi,
        *late,
        scratch=[pltpu.VMEM((pairs, HEAD_DIM, tokens + 2 * CTX_PAD), BF)],
    )
    weights_scratch = [
        xs,
        flat,
        flat,
        pltpu.VMEM((2, pairs, 13, C // row_count, channels), BF),
    ]
    two_grads = local_call(
        weights_two_kernel,
        [out((pairs, 13, C // row_count, channels), BF)] * 2,
        zi,
        *far_rows(*blocks_two),
        *rims_two,
        residual_low,
        *far_rows(*blocks_three),
        grads,
        attended,
        *far_rows(*cots),
        loss,
        scratch=weights_scratch,
        copies=12,
        flops=conv_flops,
    )
    one_edge = pltpu.VMEM((edge_rows, channels), BF)
    back_parts = [out(act, F32), out(act, BF), out(act, BF), out(act, F32)]
    (two_pairs,) = local_call(
        pair_sum_kernel,
        [out((pairs, 13, C // row_count, channels), BF)],
        two_grads[0],
        swap(two_grads[1], "rows", 1),
    )
    groups = [[2 * p + c for p in range(pairs)] for c in range(2)]
    two_total = lax.psum_scatter(two_pairs, "rows", axis_index_groups=groups)
    parts = local_call(
        functools.partial(conv_back_kernel, first=0),
        back_parts,
        zi,
        residual_low,
        *rims((residual_low,)),
        two_full,
        scratch=[one_edge],
    )
    shaped_grad, sums = local_call(
        back_two_sum_kernel,
        [out(act, F32), sums_shape],
        *chan_scatter(*parts),
        vectors,
        hidden,
        stats_two,
        mod,
    )
    out_bias = jnp.sum(
        cotangent.astype(F32) * loss_weight[None, :, None, None], axis=(0, 1, 2)
    )[None]
    second = rows_sum(jnp.concatenate([sums, conv_two_bias, qv_bias, out_bias], axis=0))
    sums_two = second[: 2 * images]
    hidden_low, conv_one_bias = local_call(
        back_two_kernel,
        [out(act, BF), out((1, channels), F32)],
        shaped_grad,
        hidden,
        after(stats_two, two_pairs),
        sums_two,
        mod,
        vectors,
    )
    one_grads = local_call(
        weights_one_kernel,
        [out((pairs, 9, C // row_count, channels), BF)] * 2,
        zi,
        *far_rows(*blocks_one),
        *rims_one,
        hidden_low,
        scratch=[xs, pltpu.VMEM((2, pairs, 9, C // row_count, channels), BF)],
        copies=4,
        flops=conv_flops,
    )
    one_terms = weight_scatter(one_grads[0], swap(one_grads[1], "rows", 1))
    parts = local_call(
        functools.partial(conv_back_kernel, first=0),
        back_parts,
        zi,
        hidden_low,
        *rims((hidden_low,)),
        one_full,
        scratch=[one_edge],
    )
    partial, sums = local_call(
        back_one_sum_kernel,
        [out(act, F32), sums_shape],
        *chan_scatter(*parts),
        after(vectors, *one_terms),
        pixels,
        stats_one,
        residual_grad,
    )

    attended_blocks = chan_blocks(after(attended, sums))
    (activations,) = local_call(
        functools.partial(out_project_kernel, tap=12),
        [out(act, BF)],
        zi,
        *far_rows(*attended_blocks),
        Far(two_full),
        vectors,
        residual,
        scratch=[flat, pltpu.VMEM((1, C, channels), BF)],
        copies=5,
    )

    shift_grad, crossed = sums_two[:images], sums_two[images : 2 * images]
    scale_grad = crossed * vectors[3] + shift_grad * vectors[4]
    embed_grad = jnp.dot(
        embed_rows,
        jnp.concatenate((scale_grad, shift_grad), axis=0),
        precision=lax.Precision.HIGHEST,
    )
    ctx_all = ctx_all[:, :, :, :CTX].reshape(images, heads, 2, HEAD_DIM, CTX)
    context_grad = jnp.dot(
        ctx_rows,
        jnp.transpose(ctx_all, (2, 0, 4, 1, 3)).reshape(-1, channels),
        preferred_element_type=F32,
    )
    ctx_value_bias = jnp.sum(ctx_all[:, :, 1].astype(F32), axis=(0, 3)).reshape(1, channels)

    squared = jnp.zeros((1, channels), F32)
    for member in (embed_grad, context_grad):
        squared = squared + jnp.sum((member * member).reshape(-1, channels), axis=0)[None]
    conv_share = (9, C // row_count, channels)
    two_sum, qkv_sum, out_sum, one_sum, payload = local_call(
        finish_kernel,
        [
            out(conv_share, F32),
            out((3,) + conv_share[1:], F32),
            out((1,) + conv_share[1:], F32),
            out(conv_share, F32),
            out((-(-(2 * images + 2) // 8) * 8, channels), F32),
        ],
        two_total,
        *one_terms,
        squared,
        sums,
        conv_one_bias,
    )
    out_sum = turn_back(out_sum, row_count, chan_count)[0]
    third = rows_sum(payload)
    (pixel_grad,) = local_call(
        back_one_kernel,
        [out(act, F32)],
        partial,
        pixels,
        stats_one,
        third,
        vectors,
    )
    vector_grad, squares = local_call(
        vector_kernel,
        [out((14, channels), F32), out((8, channels), F32)],
        third,
        second,
        sums_three,
        mod,
        vectors,
        ctx_value_bias,
    )
    squares = [squares] + [swap(squares, "chan", k) for k in (1, 2, 3)]
    squares[0] = after(squares[0], activations, pixel_grad)

    def turn(x):
        return jnp.transpose(x, (1, 0, 2))

    def flat_rows(x):
        return x.reshape(-1, x.shape[2])

    weights = (
        (conv_first, conv_first_moment, conv_first_square, one_sum),
        (conv_second, conv_second_moment, conv_second_square, two_sum),
        (turn(qkv_weight), turn(qkv_weight_moment), turn(qkv_weight_square), qkv_sum),
        (out_weight, out_weight_moment, out_weight_square, out_sum),
        (flat_rows(embed_weight), flat_rows(embed_weight_moment), flat_rows(embed_weight_square), embed_grad),
        (
            flat_rows(context_weight),
            flat_rows(context_weight_moment),
            flat_rows(context_weight_square),
            context_grad,
        ),
        (vectors, vectors_moment, vectors_square, vector_grad),
    )
    outs = [out((1, channels), F32)]
    for weight, *_ in weights:
        outs += [out(weight.shape, F32)] * 3 + [out(weight.shape, BF)]
    operands = [a for group in weights for a in group]
    norm, *updated = local_call(
        update_kernel,
        outs[:-1],
        *squares,
        *(a if i % 4 == 3 else Far(a) for i, a in enumerate(operands)),
        scratch=[pltpu.VMEM(a.shape, F32) for i, a in enumerate(operands) if i % 4 < 3],
        copies=3 * len(weights),
        limit=24,
    )
    for i in (8, 9, 10, 11):
        updated[i] = turn(updated[i])
    for i in range(16, 24):
        updated[i] = updated[i].reshape(-1, 2, channels)
    return (activations, pixel_grad, norm[0, 0], *updated)


def solution(mesh):
    act = P("rows", None, None, "chan")
    conv = P(None, "rows", "chan")
    wide = P("rows", None, "chan")
    flat = P("rows", "chan")
    vec = P(None, "chan")
    weights = (conv, conv, wide, flat, wide, wide)
    in_specs = (act, act) + (P(),) * 5 + tuple(s for w in weights for s in (w,) * 3) + (vec,) * 3
    out_specs = (act, act, P()) + tuple(s for w in weights for s in (w,) * 4) + (vec,) * 3
    return jax.shard_map(body, mesh=mesh, in_specs=in_specs, out_specs=out_specs, check_vma=False)
```

```python
import functools
import math

import jax
import jax.numpy as jnp
from jax import lax
from jax.experimental import pallas as pl
from jax.experimental.pallas import tpu as pltpu
from jax.sharding import PartitionSpec as P

C = 512
GROUPS = 32
HEAD_DIM = 64
EMB = 2048
DCTX = 2048
IMG_H = 64
IMG_W = 64
CLIP_TOK = 4
STEP = 10
CTX = 81
CTX_PAD = 128
GROUP_SIZE = C // GROUPS
GROUP_COUNT = IMG_H * IMG_W * GROUP_SIZE
LOG2E = 1.4426950408889634
BF = jnp.bfloat16
F32 = jnp.float32
ORDER = (0, 1, 3, 2)

clip_limit = 1.0


def swap(x, axis, distance):
    size = lax.axis_size(axis)
    return lax.ppermute(x, axis, [(i, i ^ distance) for i in range(size)])


def rows_sum(x, first=None):
    size = lax.axis_size("rows")
    x = x + swap(x, "rows", 1) if first is None else first
    step = 2
    while step < size:
        if step * 4 <= size:
            one, two, three = (swap(x, "rows", step * k) for k in (1, 2, 3))
            x = (x + one) + (two + three)
            step *= 4
        else:
            x = x + swap(x, "rows", step)
            step *= 2
    return x


def chan_blocks(x, *beside):
    far = swap(x, "chan", 3)
    near = swap(x, "chan", 1)
    return (x, near, far, swap(after(far, *beside), "chan", 1))


def chan_scatter(own, near, cross, far):
    cross = swap(cross, "chan", 1)
    near = swap(near, "chan", 1)
    return own, near, swap((far + cross.astype(F32)).astype(BF), "chan", 3)


def rims(blocks):
    size = lax.axis_size("rows")
    even = lax.axis_index("rows") % 2 == 0
    top = jnp.stack([x[0] for x in blocks])
    bottom = jnp.stack([x[-1] for x in blocks])
    inside = swap(jnp.where(even, bottom, top), "rows", 1)
    pairs = [(i, i + 1) for i in range(1, size - 1, 2)]
    outside = jnp.where(even, top, bottom)
    outside = lax.ppermute(outside, "rows", pairs + [(j, i) for i, j in pairs])
    shape = (len(blocks), -1, inside.shape[-1])
    return inside.reshape(shape), outside.reshape(shape)


def after(x, *earlier):
    return lax.optimization_barrier((x, *earlier))[0]


def pick(x, index, axis=0):
    return lax.dynamic_index_in_dim(x, index, axis, keepdims=False)


def weight_scatter(mine, other):
    count = mine.shape[0]
    shape = mine.shape[1:]
    total, *low = local_call(
        scatter_kernel, [out(shape, F32)] + [out(shape, BF)] * (count - 1), mine, other
    )
    return [total] + [swap(low[k - 1], "rows", 2 * k) for k in range(1, count)]


class Far:
    def __init__(self, array):
        self.array = array


def near_rows(*arrays):
    return tuple(a.reshape(math.prod(a.shape[:-1]), a.shape[-1]) for a in arrays)


def far_rows(*arrays):
    return tuple(Far(a.reshape(math.prod(a.shape[:-1]), a.shape[-1])) for a in arrays)


def local_call(kernel, outs, *args, scratch=(), copies=0, flops=0, limit=0):
    arrays = [a.array if isinstance(a, Far) else a for a in args]

    def spec(a):
        if isinstance(a, Far):
            return pl.BlockSpec(memory_space=pl.ANY)
        return pl.BlockSpec(memory_space=pltpu.SMEM if a.dtype == jnp.int32 else pltpu.VMEM)

    size = sum(math.prod(a.shape) * a.dtype.itemsize for a in (*arrays, *outs))
    scratch = list(scratch)
    if copies:
        scratch.append(pltpu.SemaphoreType.DMA((copies,)))
    return pl.pallas_call(
        kernel,
        out_shape=tuple(outs),
        in_specs=[spec(a) for a in args],
        out_specs=tuple(pl.BlockSpec(memory_space=pltpu.VMEM) for _ in outs),
        scratch_shapes=scratch,
        compiler_params=pltpu.CompilerParams(vmem_limit_bytes=(limit or (56 if copies else 50)) * 1024 * 1024),
        cost_estimate=pl.CostEstimate(flops=1, bytes_accessed=1, transcendentals=0),
    )(*arrays)


def begin(sems, *moves):
    started = []
    for i, (source, place) in enumerate(moves):
        copy = pltpu.make_async_copy(source, place, sems.at[i])
        copy.start()
        started.append(copy)
    return started


def fetch(sems, *moves):
    for copy in begin(sems, *moves):
        copy.wait()


def lanes_of(xs, j, start=0, size=None):
    width = xs.shape[1] // 4
    size = xs.shape[0] if size is None else size
    return xs.at[start : start + size, j * width : (j + 1) * width]


def block_moves(xs, blocks, start=0):
    return [(x, lanes_of(xs, j, start, x.shape[0])) for j, x in enumerate(blocks)]


def put_rims(xs, zi, inside, outside):
    count, span, width = inside.shape
    last = xs.shape[0] - span
    for j in range(count):
        lanes = slice(j * width, (j + 1) * width)
        xs[pl.ds(pl.multiple_of((1 - zi[4]) * last, span), span), lanes] = inside[j]
        xs[pl.ds(pl.multiple_of(zi[4] * last, span), span), lanes] = outside[j]


def out(shape, dtype):
    return jax.ShapeDtypeStruct(shape, dtype)


def nn(a, b):
    return lax.dot_general(a, b, (((1,), (0,)), ((), ())), preferred_element_type=F32)


def nt(a, b):
    return lax.dot_general(a, b, (((1,), (1,)), ((), ())), preferred_element_type=F32)


def group_mean(x):
    width = x.shape[1]
    left = lax.broadcasted_iota(jnp.int32, (width, width), 0) // GROUP_SIZE
    right = lax.broadcasted_iota(jnp.int32, (width, width), 1) // GROUP_SIZE
    same = (left == right).astype(F32)
    total = lax.dot_general(
        x, same, (((1,), (0,)), ((), ())), precision=lax.Precision.HIGHEST, preferred_element_type=F32
    )
    return total * (1.0 / GROUP_COUNT)


def moments(sums, images):
    means = group_mean(sums)
    average = means[:images]
    return average, lax.rsqrt(means[images:] - average * average + 1e-05)


def image_of(ref, b):
    rows, _, width, channels = ref.shape
    return ref[:, b].reshape(rows * width, channels)


def put_image(ref, b, value):
    rows, _, width, channels = ref.shape
    ref[:, b] = value.reshape(rows, width, channels).astype(ref.dtype)


def column_sum(x):
    return jnp.sum(x, axis=0, keepdims=True)


def silu(z):
    return z * jax.nn.sigmoid(z)


def silu_slope(z):
    s = jax.nn.sigmoid(z)
    return s * (1.0 + z * (1.0 - s))


def put_sums(sums, b, images, v, w):
    sums[b : b + 1] = column_sum(v)
    sums[images + b : images + b + 1] = column_sum(v * w)


def start_kernel(pixels, sums):
    images = pixels.shape[1]
    for b in range(images):
        v = image_of(pixels, b)
        put_sums(sums, b, images, v, v)


def act_one_kernel(x, sums, vec, o):
    images = x.shape[1]
    average, inverse = moments(sums[...], images)
    for b in range(images):
        xhat = (image_of(x, b) - average[b : b + 1]) * inverse[b : b + 1]
        put_image(o, b, silu(xhat * vec[0:1] + vec[1:2]))


def shaped_of(xhat, mod, vec, b, images):
    scale = 1.0 + (mod[b : b + 1] + vec[12:13])
    shift = mod[images + b : images + b + 1] + vec[13:14]
    return (xhat * vec[3:4] + vec[4:5]) * scale + shift


def act_two_kernel(x, sums, mod, vec, o):
    images = x.shape[1]
    average, inverse = moments(sums[...], images)
    for b in range(images):
        xhat = (image_of(x, b) - average[b : b + 1]) * inverse[b : b + 1]
        put_image(o, b, silu(shaped_of(xhat, mod, vec, b, images)))


def norm_three_kernel(x, sums, vec, o):
    images = x.shape[1]
    average, inverse = moments(sums[...], images)
    for b in range(images):
        xhat = (image_of(x, b) - average[b : b + 1]) * inverse[b : b + 1]
        put_image(o, b, xhat * vec[6:7] + vec[7:8])


def rows_of(z, j, width):
    return pl.ds(pl.multiple_of((z ^ ORDER[j]) * width, width), width)


def shifted(x, by, width):
    length = x.shape[0]
    column = lax.broadcasted_iota(jnp.int32, x.shape, 0) % width
    moved = pltpu.roll(x, by % length, 0)
    return jnp.where(column == (0 if by == 1 else width - 1), 0.0, moved)


def conv_taps(blocks, edges, w, extra, zi, xs, rows, span, width):
    z = zi[0]
    if extra:
        w_far, (w, sems) = w, extra
        copies = begin(sems, (w_far.at[0:9], w), *block_moves(xs, blocks, span))
        put_rims(xs, zi, *edges)
        for copy in copies:
            copy.wait()
    else:
        put_rims(xs, zi, *edges)
        for j, x in enumerate(blocks):
            lanes_of(xs, j, span, x.shape[0])[...] = x[...]
    channels = w.shape[2]
    parts = []
    for dx in range(3):
        total = None
        for dy in range(3):
            at = dy * span
            a = xs[at : at + rows * span, :]
            taps = [w[3 * dy + dx, rows_of(z, j, channels), :] for j in range(4)]
            term = nn(a, jnp.concatenate(taps, axis=0))
            total = term if total is None else total + term
        parts.append(total)
    return parts[1] + shifted(parts[0], 1, width) + shifted(parts[2], -1, width)


def conv_one_kernel(zi, x0, x1, x2, x3, e0, e1, w_far, vec, hidden, sums, xs, *extra):
    rows, images, width, channels = hidden.shape
    blocks = (x0, x1, x2, x3)
    result = conv_taps(
        blocks, (e0, e1), w_far, extra, zi, xs, rows, images * width, width
    ) + vec[2:3]
    hidden[...] = result.reshape(hidden.shape)
    for b in range(images):
        v = image_of(hidden, b)
        put_sums(sums, b, images, v, v)


def conv_two_kernel(zi, x0, x1, x2, x3, e0, e1, w_far, vec, pixels, residual, sums, xs, *extra):
    rows, images, width, channels = residual.shape
    blocks = (x0, x1, x2, x3)
    result = conv_taps(
        blocks, (e0, e1), w_far, extra, zi, xs, rows, images * width, width
    ) + vec[5:6]
    residual[...] = pixels[...] + result.reshape(residual.shape)
    for b in range(images):
        v = image_of(residual, b)
        put_sums(sums, b, images, v, v)


def conv_back_kernel(zi, r, e0, e1, w, own, near, cross, far, xs, *, first):
    rows, images, width, channels = r.shape
    span = images * width
    put_rims(xs, zi, e0, e1)
    xs[span : span + rows * span] = r[...].reshape(rows * span, channels)
    wide = xs[...].astype(F32)
    turned = [shifted(wide, -1, width).astype(BF), xs[...], shifted(wide, 1, width).astype(BF)]
    taps = [(dy, dx) for dy in range(3) for dx in range(3)]
    a = jnp.concatenate(
        [turned[dx][(2 - dy) * span : (2 - dy + rows) * span] for dy, dx in taps], axis=1
    )
    for j, part in enumerate((own, near, far, cross)):
        at = rows_of(zi[0], j, channels)
        b = jnp.concatenate([w[first + 3 * dy + dx, at, :] for dy, dx in taps], axis=1)
        part[...] = nt(a, b).astype(part.dtype).reshape(part.shape)


def total_image(terms, b):
    total = image_of(terms[0], b)
    for term in terms[1:]:
        total = total + image_of(term, b).astype(F32)
    return total


def back_two_sum_kernel(t0, t1, t2, vec, hidden, stats, mod, shaped_grad, sums):
    images = hidden.shape[1]
    average, inverse = moments(stats[...], images)
    for b in range(images):
        xhat = (image_of(hidden, b) - average[b : b + 1]) * inverse[b : b + 1]
        g = total_image((t0, t1, t2), b) * silu_slope(shaped_of(xhat, mod, vec, b, images))
        put_image(shaped_grad, b, g)
        put_sums(sums, b, images, g, xhat)


def back_one_sum_kernel(t0, t1, t2, vec, pixels, stats, residual_grad, partial, sums):
    images = pixels.shape[1]
    average, inverse = moments(stats[0 : 2 * images], images)
    for b in range(images):
        xhat = (image_of(pixels, b) - average[b : b + 1]) * inverse[b : b + 1]
        g = total_image((t0, t1, t2), b) * silu_slope(xhat * vec[0:1] + vec[1:2])
        put_image(partial, b, image_of(residual_grad, b) + g * (inverse[b : b + 1] * vec[0:1]))
        put_sums(sums, b, images, g, xhat)


def put_shares(box, zi, tap, grad, base=0):
    share, channels = box.shape[3:]
    each = channels // share
    for j in range(4):
        for i in range(each):
            at = j * channels + i * share
            row = (zi[0] ^ ORDER[j]) * each + i
            box[(row & 1) ^ zi[4], (row >> 1) ^ base, tap] = grad[at : at + share].astype(box.dtype)


def conv_weights(zi, xs, r, box, base=0):
    rows, images, width, channels = r.shape
    span = images * width
    turned = xs[...].T
    wide = r[...].reshape(rows * span, channels).astype(F32)
    three = jnp.concatenate(
        [shifted(wide, -1, width).astype(BF), wide.astype(BF), shifted(wide, 1, width).astype(BF)],
        axis=1,
    )
    for dy in range(3):
        grad = nn(turned[:, dy * span : (dy + rows) * span], three)
        for dx in range(3):
            put_shares(box, zi, 3 * dy + dx, grad[:, dx * channels : (dx + 1) * channels], base)


def weights_two_kernel(
    zi, x0, x1, x2, x3, e0, e1, r, n0, n1, n2, n3, grads, att, c0, c1, c2, c3, loss, mine, other, xs, ns, cs, box, sems
):
    blocks = begin(
        sems,
        *block_moves(xs, (x0, x1, x2, x3), e0.shape[1]),
        *block_moves(ns, (n0, n1, n2, n3)),
        *block_moves(cs, (c0, c1, c2, c3)),
    )
    put_rims(xs, zi, e0, e1)
    for copy in blocks[:4]:
        copy.wait()
    conv_weights(zi, xs, r, box)
    for copy in blocks[4:]:
        copy.wait()
    rows, images, width, columns = grads.shape
    channels = att.shape[3]
    pixels = rows * images * width
    grad = nn(ns[...].T, grads[...].reshape(pixels, columns))
    for s in range(3):
        put_shares(box, zi, 9 + s, grad[:, s * channels : (s + 1) * channels])
    scale = jnp.concatenate([loss[b : b + 1] for b in range(images)], axis=0)
    scale = jnp.concatenate([scale] * 4, axis=1)[None, :, None, :]
    low = (cs[...].reshape(rows, images, width, 4 * channels).astype(F32) * scale).astype(BF)
    grad = nn(att[...].reshape(pixels, channels).T, low.reshape(pixels, 4 * channels))
    by_output = [grad[:, j * channels : (j + 1) * channels] for j in range(4)]
    put_shares(box, zi, 12, jnp.concatenate(by_output, axis=0))
    mine[...] = box[0]
    other[...] = box[1]


def weights_one_kernel(zi, x0, x1, x2, x3, e0, e1, r, mine, other, xs, box, sems):
    copies = begin(sems, *block_moves(xs, (x0, x1, x2, x3), e0.shape[1]))
    put_rims(xs, zi, e0, e1)
    for copy in copies:
        copy.wait()
    conv_weights(zi, xs, r, box, zi[1])
    mine[...] = box[0]
    other[...] = box[1]


def pair_sum_kernel(mine, other, o):
    o[...] = (mine[...].astype(F32) + other[...].astype(F32)).astype(BF)


def scatter_kernel(mine, other, total, *low):
    total[...] = mine[0].astype(F32) + other[0].astype(F32)
    for k, o in enumerate(low):
        o[...] = (mine[k + 1].astype(F32) + other[k + 1].astype(F32)).astype(BF)


def put_heads(scratch, leading, value, b, heads):
    turned = value.T.astype(scratch.dtype)
    for h in range(heads):
        scratch[b * heads + h, leading] = turned[h * HEAD_DIM : (h + 1) * HEAD_DIM]


def project_kernel(*refs, base):
    zi, w_far, vec, grads, blocks = refs[0], refs[1], refs[2], refs[3], refs[4:8]
    outs, (xs, w, scratch, sems) = refs[8:-4], refs[-4:]
    fetch(sems, (w_far.at[base : base + 3], w), *block_moves(xs, blocks))
    tokens = outs[0].shape[2]
    channels = w.shape[2]
    heads = channels // HEAD_DIM
    images = len(outs) // heads
    rows = xs.shape[0] // (images * IMG_W)
    a = xs[...]
    for s in range(3):
        rows_in = [w[s, rows_of(zi[0], j, channels), :] for j in range(4)]
        value = nn(a, jnp.concatenate(rows_in, axis=0))
        if s != 1:
            at = 8 if s == 0 else 9
            value = value + vec[at : at + 1]
        split = value.reshape(rows, images, IMG_W, channels)
        for b in range(images):
            put_heads(scratch, s, split[:, b].reshape(tokens, channels), b, heads)
    for k, o in enumerate(outs):
        o[0:3] = scratch[zi[1] ^ k]
        o[3] = grads[zi[1] ^ k, 0]


def output_grad_kernel(c0, c1, c2, c3, w0, w1, w2, w3, loss, o, xs, sems):
    fetch(sems, *block_moves(xs, (c0, c1, c2, c3)))
    images, channels = loss.shape
    heads = channels // HEAD_DIM
    tokens = o.shape[3]
    turned = jnp.concatenate([w[...] for w in (w0, w1, w2, w3)], axis=1)
    wide = xs[...].reshape(tokens // IMG_W, images, IMG_W, 4 * channels)
    for b in range(images):
        scale = jnp.concatenate([loss[b : b + 1]] * 4, axis=1)
        low = (wide[:, b].reshape(tokens, 4 * channels).astype(F32) * scale).astype(BF)
        put_heads(o, 0, nt(low, turned), b, heads)


def attention_kernel(*refs, chunk, count, block):
    live, ctx_ref = refs[0], refs[1]
    mine, sibs = (refs[2 + i * count : 2 + (i + 1) * count] for i in range(2))
    oq_ref, own_ref, other_ref = refs[2 + 2 * count : 5 + 2 * count]
    q_s, do_s, kt_s, k_s, v_s, s_s, p_s, acc_s = refs[5 + 2 * count :]
    step = pl.program_id(0)
    last = pl.num_programs(0) - 1
    tokens = mine[0].shape[2]
    depth = HEAD_DIM
    queries = block
    half = count * tokens
    keys = 2 * half
    extra = ctx_ref.shape[2]

    @pl.when(step == 0)
    def _():
        for k in range(count):
            lanes = slice(k * tokens, (k + 1) * tokens)
            q_s[:, lanes] = mine[k][0]
            do_s[:, lanes] = mine[k][3]
            kt_s[:, :, lanes] = mine[k][1:3]
            kt_s[:, :, half + k * tokens : half + (k + 1) * tokens] = sibs[k][1:3]
        kt_s[:, :, keys:] = ctx_ref[...]
        k_s[...] = kt_s[0].T
        v_s[...] = kt_s[1].T
        acc_s[...] = jnp.zeros_like(acc_s)

    here = pl.ds(pl.multiple_of(step * block, block), block)
    q = q_s[:, here]
    do = do_s[:, here]
    spans = [(i * chunk, chunk) for i in range(keys // chunk)] + [(keys, extra)]
    highest = None
    for at, size in spans:
        s = nn(k_s[at : at + size], q)
        if at == keys:
            position = lax.broadcasted_iota(jnp.int32, s.shape, 0)
            s = jnp.where(position < live[0], s, -1e30)
        s_s[at : at + size] = s
        top = jnp.max(s.reshape(size // 8, 8, queries), axis=0)
        highest = top if highest is None else jnp.maximum(highest, top)
    factor = 0.125 * LOG2E
    peak = jnp.max(highest, axis=0, keepdims=True) * factor
    weight_sum = jnp.zeros((8, queries), F32)
    mixture = jnp.zeros((depth, queries), F32)
    for at, size in spans:
        p = jnp.exp2(s_s[at : at + size] * factor - peak)
        weight_sum = weight_sum + jnp.sum(p.reshape(size // 8, 8, queries), axis=0)
        low = p.astype(BF)
        p_s[at : at + size] = low
        mixture = mixture + nn(kt_s[1, :, at : at + size], low)
    inverse = 1.0 / jnp.sum(weight_sum, axis=0, keepdims=True)
    attended = mixture * inverse
    oq_ref[0] = attended.astype(BF)
    delta = jnp.sum(do.astype(F32) * attended, axis=0, keepdims=True)
    do_scaled = (do.astype(F32) * inverse).astype(BF)
    q_scaled = (q.astype(F32) * (inverse * 0.125)).astype(BF)
    query_grad = jnp.zeros((depth, queries), F32)
    for at, size in spans:
        dprob = nn(v_s[at : at + size], do)
        low = p_s[at : at + size]
        dscore = (low.astype(F32) * (dprob - delta)).astype(BF)
        query_grad = query_grad + nn(kt_s[0, :, at : at + size], dscore)
        acc_s[0, :, at : at + size] += nt(q_scaled, dscore)
        acc_s[1, :, at : at + size] += nt(do_scaled, low)
    oq_ref[1] = (query_grad * (inverse * 0.125)).astype(BF)

    @pl.when(step == last)
    def _():
        own_ref[:, :, 0:half] = acc_s[:, :, 0:half].astype(BF)
        own_ref[:, :, half:] = acc_s[:, :, keys:].astype(BF)
        other_ref[...] = acc_s[:, :, half:].astype(BF)


def attention(live, ctx, mine, sibs):
    count = len(mine)
    _, depth, tokens = mine[0].shape
    queries = count * tokens
    total = 2 * queries + ctx.shape[2]
    block = min(512, queries)
    chunk = min(1024, 2 * queries)

    def whole(a):
        return pl.BlockSpec(a.shape, lambda i: (0,) * len(a.shape))

    outs = (
        out((2, depth, queries), BF),
        out((2, depth, queries + ctx.shape[2]), BF),
        out((2, depth, queries + ctx.shape[2]), BF),
    )
    arrays = (ctx, *mine, *sibs)
    return pl.pallas_call(
        functools.partial(attention_kernel, chunk=chunk, count=count, block=block),
        grid=(queries // block,),
        in_specs=[pl.BlockSpec(memory_space=pltpu.SMEM)] + [whole(a) for a in arrays],
        out_specs=(
            pl.BlockSpec((2, depth, block), lambda i: (0, 0, i)),
            whole(outs[1]),
            whole(outs[2]),
        ),
        out_shape=outs,
        scratch_shapes=[
            pltpu.VMEM((depth, queries), BF),
            pltpu.VMEM((depth, queries), BF),
            pltpu.VMEM((2, depth, total), BF),
            pltpu.VMEM((total, depth), BF),
            pltpu.VMEM((total, depth), BF),
            pltpu.VMEM((total, block), F32),
            pltpu.VMEM((total, block), BF),
            pltpu.VMEM((2, depth, total), F32),
        ],
        compiler_params=pltpu.CompilerParams(
            vmem_limit_bytes=56 * 1024 * 1024, dimension_semantics=("arbitrary",)
        ),
        cost_estimate=pl.CostEstimate(
            flops=12 * depth * queries * total, bytes_accessed=8 * depth * total, transcendentals=queries * total
        ),
    )(live, *arrays)


def merge_kernel(oq_far, own_far, other_far, *refs):
    oq, own, other, sems = refs[-4:]
    outs = refs[:-4]
    count = len(outs) // 2
    fetch(sems, (oq_far, oq), (own_far, own), (other_far, other))
    tokens = oq.shape[2] // count
    both = (own[...].astype(F32) + other[...].astype(F32)).astype(BF)
    for k in range(count):
        lanes = slice(k * tokens, (k + 1) * tokens)
        outs[k][0] = oq[1, :, lanes]
        outs[k][1:3] = both[:, :, lanes]
        outs[count + k][:, 0:tokens] = oq[0, :, lanes]
        for s in range(2):
            at = tokens + s * CTX_PAD
            outs[count + k][:, at : at + CTX_PAD] = both[s, :, count * tokens :]


def back_project_kernel(*refs, base, count):
    zi, w_far, pieces = refs[0], refs[1], refs[2 : 2 + count]
    grads, part_own, part_near, part_cross, part_far, biases = refs[2 + count : -3]
    rec, w, sems = refs[-3:]
    fetch(sems, (w_far.at[base : base + 3], w))
    rows, images, width, channels = part_own.shape
    heads = channels // HEAD_DIM
    for k in range(count):
        rec[zi[1] ^ k] = pieces[k][...]
    for b in range(images):
        for s in range(3):
            blocks = [rec[b * heads + h, s] for h in range(heads)]
            value = jnp.concatenate(blocks, axis=0).T.reshape(rows, width, channels)
            grads[:, b, :, s * channels : (s + 1) * channels] = value
    flat = grads[...].reshape(rows * images * width, 3 * channels)
    for j, part in enumerate((part_own, part_near, part_far, part_cross)):
        at = rows_of(zi[0], j, channels)
        taps = jnp.concatenate([w[s, at, :] for s in range(3)], axis=1)
        part[...] = nt(flat, taps).astype(part.dtype).reshape(part.shape)
    wide = flat.astype(F32)
    biases[0:1] = column_sum(wide[:, 0:channels])
    biases[1:2] = column_sum(wide[:, 2 * channels :])


def attended_kernel(*refs):
    zi, pieces = refs[0], refs[1:-3]
    attended, ctx, rec = refs[-3:]
    rows, images, width, channels = attended.shape
    heads = channels // HEAD_DIM
    tokens = rows * width
    for k, piece in enumerate(pieces):
        rec[zi[1] ^ k] = piece[...]
    for b in range(images):
        blocks = [rec[b * heads + h, :, 0:tokens] for h in range(heads)]
        attended[:, b] = jnp.concatenate(blocks, axis=0).T.reshape(rows, width, channels)
    for q in range(len(pieces)):
        for s in range(2):
            at = tokens + s * CTX_PAD
            ctx[q, s] = rec[q, :, at : at + CTX_PAD]


def out_project_kernel(zi, x0, x1, x2, x3, w_far, vec, residual, o, xs, w, sems, *, tap):
    fetch(sems, (w_far.at[tap : tap + 1], w), *block_moves(xs, (x0, x1, x2, x3)))
    channels = w.shape[2]
    rows_in = [w[0, rows_of(zi[0], j, channels), :] for j in range(4)]
    value = nn(xs[...], jnp.concatenate(rows_in, axis=0)) + vec[10:11]
    o[...] = (residual[...] + value.reshape(o.shape)).astype(BF)


def back_three_sum_kernel(t0, t1, t2, residual, stats, g_out, sums):
    images = residual.shape[1]
    average, inverse = moments(stats[...], images)
    for b in range(images):
        g = image_of(t0, b).astype(F32) + image_of(t1, b).astype(F32) + image_of(t2, b).astype(F32)
        xhat = (image_of(residual, b) - average[b : b + 1]) * inverse[b : b + 1]
        put_image(g_out, b, g)
        put_sums(sums, b, images, g, xhat)


def back_three_kernel(g0, x0, c0, stats, sums, vec, loss, residual_grad, low, bias):
    images = x0.shape[1]
    average, inverse = moments(stats[...], images)
    means = group_mean(sums[...] * vec[6:7])
    total = None
    for b in range(images):
        xhat = (image_of(x0, b) - average[b : b + 1]) * inverse[b : b + 1]
        g = image_of(g0, b) * vec[6:7] - means[b : b + 1] - xhat * means[images + b : images + b + 1]
        g = image_of(c0, b).astype(F32) * loss[b : b + 1] + inverse[b : b + 1] * g
        put_image(residual_grad, b, g)
        put_image(low, b, g)
        part = column_sum(g)
        total = part if total is None else total + part
    bias[...] = total


def back_two_kernel(g0, x0, stats, sums, mod, vec, low, bias):
    images = x0.shape[1]
    average, inverse = moments(stats[...], images)
    gains = [vec[3:4] * (1.0 + (mod[b : b + 1] + vec[12:13])) for b in range(images)]
    means = group_mean(sums[0 : 2 * images] * jnp.concatenate(gains + gains, axis=0))
    total = None
    for b in range(images):
        xhat = (image_of(x0, b) - average[b : b + 1]) * inverse[b : b + 1]
        g = image_of(g0, b) * gains[b]
        g = g - means[b : b + 1] - xhat * means[images + b : images + b + 1]
        g = inverse[b : b + 1] * g
        put_image(low, b, g)
        part = column_sum(g)
        total = part if total is None else total + part
    bias[...] = total


def back_one_kernel(partial, pixels, stats, sums, vec, pixel_grad):
    images = pixels.shape[1]
    average, inverse = moments(stats[0 : 2 * images], images)
    means = group_mean(sums[0 : 2 * images] * vec[0:1])
    for b in range(images):
        slope = inverse[b : b + 1] * inverse[b : b + 1] * means[images + b : images + b + 1]
        level = inverse[b : b + 1] * means[b : b + 1] - average[b : b + 1] * slope
        put_image(pixel_grad, b, image_of(partial, b) - (image_of(pixels, b) * slope + level))


RATES = (0.02, 0.02, 0.08, 1.0, 0.02, 0.04, 1.0)


def finish_kernel(*refs):
    terms, (squares, sums, bias, two_sum, qkv_sum, out_sum, one_sum, payload) = refs[:-8], refs[-8:]
    squared = squares[...]
    at = 0
    for o in (two_sum, qkv_sum, out_sum, one_sum):
        if o is one_sum:
            total = terms[1][...]
            for term in terms[2:]:
                total = total + term[...].astype(F32)
        else:
            total = terms[0][at : at + o.shape[0]].astype(F32)
            at += o.shape[0]
        o[...] = total
        squared = squared + column_sum((total * total).reshape(-1, total.shape[-1]))
    count = sums.shape[0]
    payload[0:count] = sums[...]
    payload[count : count + 1] = bias[...]
    payload[count + 1 : count + 2] = squared
    payload[count + 2 :] = jnp.zeros((payload.shape[0] - count - 2, payload.shape[1]), F32)


def vector_kernel(third, second, sums_three, mod, vec, ctx, grad, squares):
    images = sums_three.shape[0] // 2

    def total(ref, at):
        return column_sum(ref[at : at + images])

    scale = 1.0 + (mod[0:images] + vec[12:13])
    shift_grad = second[0:images]
    crossed = second[images : 2 * images]
    scale_grad = crossed * vec[3:4] + shift_grad * vec[4:5]
    at = 2 * images
    rows = (
        total(third, images),
        total(third, 0),
        third[at : at + 1],
        column_sum(scale * crossed),
        column_sum(scale * shift_grad),
        second[at : at + 1],
        total(sums_three, images),
        total(sums_three, 0),
        second[at + 1 : at + 2],
        second[at + 2 : at + 3],
        second[at + 3 : at + 4],
        ctx[...],
        column_sum(scale_grad),
        column_sum(shift_grad),
    )
    squared = third[at + 1 : at + 2]
    for i, row in enumerate(rows):
        grad[i : i + 1] = row
        squared = squared + row * row
    squares[...] = jnp.broadcast_to(squared, squares.shape)


def update_kernel(*refs):
    count = len(RATES)
    squares, given = refs[0:4], refs[4 : 4 + 4 * count]
    made, held, sems = refs[4 + 4 * count : -3 * count - 1], refs[-3 * count - 1 : -1], refs[-1]
    far = [a for i, a in enumerate(given) if i % 4 < 3]
    arriving = begin(sems, *zip(far, held))
    near = squares[0][0:1] + squares[1][0:1]
    total = jnp.sum(near + (squares[2][0:1] + squares[3][0:1]), axis=1, keepdims=True)
    norm = jnp.sqrt(total)
    made[0][...] = jnp.broadcast_to(norm, made[0].shape)
    factor = jnp.minimum(1.0, clip_limit / norm)
    at = 1
    for i, rate in enumerate(RATES):
        for copy in arriving[3 * i : 3 * i + 3]:
            copy.wait()
        weight, moment, square = held[3 * i : 3 * i + 3]
        gradient = given[4 * i + 3]
        decay = 0.0 if i == count - 1 else 0.01
        scale = factor.reshape((1,) * (len(weight.shape) - 2) + factor.shape)
        new = adamw(weight[...], moment[...], square[...], gradient[...] * scale, rate, decay)
        for value in new:
            made[at][...] = value
            at += 1
        if i < count - 1:
            made[at][...] = new[0].astype(BF)
            at += 1


def adamw(weight, moment, square, gradient, step_rate, weight_decay):
    moment_new = 0.9 * moment + 0.1 * gradient
    square_new = 0.999 * square + 0.001 * gradient * gradient
    corrected = moment_new / (1.0 - 0.9**STEP)
    scaled = square_new / (1.0 - 0.999**STEP)
    weight_new = weight - step_rate * (
        corrected / (jnp.sqrt(scaled) + 1e-08) + weight_decay * weight
    )
    return (weight_new, moment_new, square_new)


def turn_moves(row_count, chan_count):
    share = row_count // chan_count
    return [
        (r * chan_count + z, (z * share + r % share) * chan_count + r // share)
        for r in range(row_count)
        for z in range(chan_count)
    ]


def turn_back(x, row_count, chan_count):
    moves = [(j, i) for i, j in turn_moves(row_count, chan_count)]
    return lax.ppermute(x, ("rows", "chan"), moves)


def body(
    pixels,
    cotangent,
    loss_weight,
    timesteps,
    clip_embed,
    context,
    text_len,
    conv_first,
    conv_first_moment,
    conv_first_square,
    conv_second,
    conv_second_moment,
    conv_second_square,
    qkv_weight,
    qkv_weight_moment,
    qkv_weight_square,
    out_weight,
    out_weight_moment,
    out_weight_square,
    embed_weight,
    embed_weight_moment,
    embed_weight_square,
    context_weight,
    context_weight_moment,
    context_weight_square,
    vectors,
    vectors_moment,
    vectors_square,
):
    row_count = lax.axis_size("rows")
    chan_count = lax.axis_size("chan")
    row = lax.axis_index("rows")
    chan = lax.axis_index("chan")
    local_rows, images, width, channels = pixels.shape
    heads = channels // HEAD_DIM
    pairs = images * heads
    assert chan_count == 4 and row_count == 2 * pairs
    pair = row // 2
    zi = jnp.stack(
        [chan, pair, row, row_count - 1 - row, row % 2]
    ).astype(jnp.int32)
    act = (local_rows, images, width, channels)
    edge_rows = (local_rows + 2) * images * width
    xs = pltpu.VMEM((edge_rows, C), BF)
    flat = pltpu.VMEM((local_rows * images * width, C), BF)
    taps = pltpu.VMEM((9, C, channels), BF)
    conv_flops = 2 * local_rows * images * width * 9 * C * channels

    (sums,) = local_call(start_kernel, [out((2 * images, channels), F32)], pixels)
    loss = jnp.broadcast_to(loss_weight[:, None], (images, channels))
    cot = after(cotangent, sums)
    cot_near, cot_far = swap(cot, "chan", 1), swap(cot, "chan", 3)

    sums_shape = out((2 * images, channels), F32)
    by_chip = sums + swap(sums, "rows", 1)
    stats_one = rows_sum(sums, by_chip)

    one_full = lax.all_gather(after(conv_first, by_chip).astype(BF), "rows", axis=1, tiled=True)
    (active_one,) = local_call(
        act_one_kernel, [out(act, BF)], pixels, after(stats_one, cot_near, cot_far), vectors
    )
    blocks_one = chan_blocks(active_one)
    arrived = blocks_one[1:3]
    two_low = after(conv_second, *arrived).astype(BF)
    qkv_low = jnp.transpose(after(qkv_weight, *arrived), (1, 0, 2)).astype(BF)
    out_low = after(out_weight, *arrived).astype(BF)[None]
    two_full = lax.all_gather(
        jnp.concatenate([two_low, qkv_low, out_low], axis=0), "rows", axis=1, tiled=True
    )
    ctx_full = lax.all_gather(
        after(context_weight, *arrived).astype(BF), "rows", axis=0, tiled=True
    )

    share = EMB // row_count
    index = row * share + jnp.arange(share, dtype=jnp.int32)
    half_width = EMB // 2
    frequency = jnp.exp(-math.log(10000.0) * (index % half_width).astype(F32) / half_width)
    phases = after(timesteps, active_one).astype(F32)[:, None] * frequency[None, :]
    features = jnp.where(index[None, :] < half_width, jnp.cos(phases), jnp.sin(phases))
    clip_share = lax.dynamic_slice_in_dim(clip_embed, row * share, share, 1)
    embedding = jax.nn.silu(features + clip_share).astype(BF)
    both = jnp.eye(2, dtype=F32)[None, :, :, None]
    embed_rows = (embedding.astype(F32).T[:, None, None, :] * both).reshape(2 * share, 2 * images)
    modulation = jnp.einsum(
        "be,esc->sbc",
        embedding,
        after(embed_weight, active_one).astype(BF),
        preferred_element_type=F32,
    ).reshape(2 * images, channels)

    cot_cross = swap(after(cot_far, *blocks_one), "chan", 1)
    rims_one = rims(blocks_one)
    hidden, sums = local_call(
        conv_one_kernel,
        [out(act, F32), sums_shape],
        zi,
        *near_rows(*blocks_one),
        *rims_one,
        one_full,
        vectors,
        scratch=[xs],
        flops=conv_flops,
    )
    stats_two = rows_sum(jnp.concatenate([after(sums, cot_cross), modulation], axis=0))
    stats_two, mod = stats_two[: 2 * images], stats_two[2 * images :]
    (active_two,) = local_call(
        act_two_kernel, [out(act, BF)], hidden, stats_two, mod, vectors
    )

    blocks_two = chan_blocks(active_two)

    def out_rows(owner):
        return lax.dynamic_slice_in_dim(two_full[12], owner * channels, channels, 0)

    out_part = [out_rows(chan)] + [swap(out_rows(chan ^ k), "chan", k) for k in ORDER[1:]]
    tokens = local_rows * width
    cots = (cotangent, cot_near, cot_far, cot_cross)
    (attended_grad,) = local_call(
        output_grad_kernel,
        [out((pairs, 1, HEAD_DIM, tokens), BF)],
        *far_rows(*(after(a, active_two) for a in cots)),
        *out_part,
        loss,
        scratch=[flat],
        copies=4,
    )
    ctx_share = DCTX // row_count
    ctx_rows = lax.dynamic_slice_in_dim(context, row * ctx_share, ctx_share, 2)
    ctx_rows = jnp.transpose(ctx_rows, (2, 0, 1)).reshape(ctx_share, 1, 1, -1)
    ctx_rows = (ctx_rows * jnp.eye(2, dtype=BF)[None, :, :, None]).reshape(2 * ctx_share, -1)
    rims_two = rims((after(blocks_two[0], attended_grad), *blocks_two[1:]))
    residual, sums = local_call(
        conv_two_kernel,
        [out(act, F32), sums_shape],
        zi,
        *far_rows(*blocks_two),
        *rims_two,
        Far(two_full),
        after(vectors, ctx_rows, embed_rows),
        pixels,
        scratch=[xs, taps],
        copies=5,
        flops=conv_flops,
    )
    stats_three = rows_sum(sums)
    (normed,) = local_call(norm_three_kernel, [out(act, BF)], residual, stats_three, vectors)
    blocks_three = chan_blocks(normed)

    image, head = pair // heads, pair % heads
    ctx_low = pick(context, image)
    ctx_projected = jnp.einsum("te,esc->sct", ctx_low, ctx_full, preferred_element_type=F32)
    ctx_bias = jnp.stack([jnp.zeros_like(vectors[11]), vectors[11]])[:, :, None]
    ctx_heads = lax.dynamic_slice_in_dim(ctx_projected + ctx_bias, head * HEAD_DIM, HEAD_DIM, 1)
    ctx_heads = jnp.pad(ctx_heads.astype(BF), ((0, 0), (0, 0), (0, CTX_PAD - CTX)))
    live = (CLIP_TOK + pick(text_len, image))[None].astype(jnp.int32)

    pieces = local_call(
        functools.partial(project_kernel, base=9),
        [out((4, HEAD_DIM, tokens), BF)] * pairs,
        zi,
        Far(two_full),
        after(vectors, ctx_heads),
        attended_grad,
        *far_rows(*blocks_three),
        scratch=[
            flat,
            pltpu.VMEM((3, C, channels), BF),
            pltpu.VMEM((pairs, 3, HEAD_DIM, tokens), BF),
        ],
        copies=5,
        flops=conv_flops // 3,
    )
    pieces = [pieces[0]] + [swap(pieces[k], "rows", 2 * k) for k in range(1, pairs)]
    siblings = [swap(piece, "rows", 1) for piece in pieces]

    out_query, own, other = attention(live, ctx_heads, pieces, siblings)
    merged = local_call(
        merge_kernel,
        [out((3, HEAD_DIM, tokens), BF)] * pairs
        + [out((HEAD_DIM, tokens + 2 * CTX_PAD), BF)] * pairs,
        Far(out_query),
        Far(own),
        Far(swap(other, "rows", 1)),
        scratch=[
            pltpu.VMEM(out_query.shape, BF),
            pltpu.VMEM(own.shape, BF),
            pltpu.VMEM(own.shape, BF),
        ],
        copies=3,
    )
    received = [merged[0]] + [swap(merged[k], "rows", 2 * k) for k in range(1, pairs)]

    grads, part_own, part_near, part_cross, part_far, qv_bias = local_call(
        functools.partial(back_project_kernel, base=9, count=pairs),
        [
            out((local_rows, images, width, 3 * channels), BF),
            out(act, F32),
            out(act, BF),
            out(act, BF),
            out(act, F32),
            out((2, channels), F32),
        ],
        zi,
        Far(two_full),
        *received,
        scratch=[
            pltpu.VMEM((pairs, 3, HEAD_DIM, tokens), BF),
            pltpu.VMEM((3, C, channels), BF),
        ],
        copies=1,
        flops=conv_flops // 3,
    )
    normed_terms = chan_scatter(part_own, part_near, part_cross, part_far)
    late = [after(piece, part_cross) for piece in merged[pairs:]]
    late = [late[0]] + [swap(late[k], "rows", 2 * k) for k in range(1, pairs)]
    normed_grad, sums = local_call(
        back_three_sum_kernel,
        [out(act, F32), sums_shape],
        *normed_terms,
        residual,
        after(stats_three, *late),
    )
    sums_three = rows_sum(sums)
    residual_grad, residual_low, conv_two_bias = local_call(
        back_three_kernel,
        [out(act, F32), out(act, BF), out((1, channels), F32)],
        normed_grad,
        residual,
        cotangent,
        stats_three,
        sums_three,
        vectors,
        loss,
    )
    attended, ctx_all = local_call(
        attended_kernel,
        [out(act, BF), out((pairs, 2, HEAD_DIM, CTX_PAD), BF)],
        zi,
        *late,
        scratch=[pltpu.VMEM((pairs, HEAD_DIM, tokens + 2 * CTX_PAD), BF)],
    )
    weights_scratch = [
        xs,
        flat,
        flat,
        pltpu.VMEM((2, pairs, 13, C // row_count, channels), BF),
    ]
    two_grads = local_call(
        weights_two_kernel,
        [out((pairs, 13, C // row_count, channels), BF)] * 2,
        zi,
        *far_rows(*blocks_two),
        *rims_two,
        residual_low,
        *far_rows(*blocks_three),
        grads,
        attended,
        *far_rows(*cots),
        loss,
        scratch=weights_scratch,
        copies=12,
        flops=conv_flops,
    )
    one_edge = pltpu.VMEM((edge_rows, channels), BF)
    back_parts = [out(act, F32), out(act, BF), out(act, BF), out(act, F32)]
    (two_pairs,) = local_call(
        pair_sum_kernel,
        [out((pairs, 13, C // row_count, channels), BF)],
        two_grads[0],
        swap(two_grads[1], "rows", 1),
    )
    groups = [[2 * p + c for p in range(pairs)] for c in range(2)]
    two_total = lax.psum_scatter(two_pairs, "rows", axis_index_groups=groups)
    parts = local_call(
        functools.partial(conv_back_kernel, first=0),
        back_parts,
        zi,
        residual_low,
        *rims((residual_low,)),
        two_full,
        scratch=[one_edge],
    )
    shaped_grad, sums = local_call(
        back_two_sum_kernel,
        [out(act, F32), sums_shape],
        *chan_scatter(*parts),
        vectors,
        hidden,
        stats_two,
        mod,
    )
    att = after(attended, sums)
    att_near, att_far = swap(att, "chan", 1), swap(att, "chan", 3)
    out_bias = jnp.sum(
        cotangent.astype(F32) * loss_weight[None, :, None, None], axis=(0, 1, 2)
    )[None]
    second = rows_sum(jnp.concatenate([sums, conv_two_bias, qv_bias, out_bias], axis=0))
    sums_two = second[: 2 * images]
    hidden_low, conv_one_bias = local_call(
        back_two_kernel,
        [out(act, BF), out((1, channels), F32)],
        shaped_grad,
        hidden,
        after(stats_two, two_pairs),
        sums_two,
        mod,
        vectors,
    )
    one_grads = local_call(
        weights_one_kernel,
        [out((pairs, 9, C // row_count, channels), BF)] * 2,
        zi,
        *far_rows(*blocks_one),
        *rims_one,
        hidden_low,
        scratch=[xs, pltpu.VMEM((2, pairs, 9, C // row_count, channels), BF)],
        copies=4,
        flops=conv_flops,
    )
    one_terms = weight_scatter(one_grads[0], swap(one_grads[1], "rows", 1))
    parts = local_call(
        functools.partial(conv_back_kernel, first=0),
        back_parts,
        zi,
        after(hidden_low, att_near, att_far),
        *rims((hidden_low,)),
        one_full,
        scratch=[one_edge],
    )
    partial, sums = local_call(
        back_one_sum_kernel,
        [out(act, F32), sums_shape],
        *chan_scatter(*parts),
        after(vectors, *one_terms),
        pixels,
        stats_one,
        residual_grad,
    )

    att_far = after(att_far, sums)
    attended_blocks = (attended, att_near, att_far, swap(att_far, "chan", 1))
    (activations,) = local_call(
        functools.partial(out_project_kernel, tap=12),
        [out(act, BF)],
        zi,
        *far_rows(*attended_blocks),
        Far(two_full),
        vectors,
        residual,
        scratch=[flat, pltpu.VMEM((1, C, channels), BF)],
        copies=5,
    )

    shift_grad, crossed = sums_two[:images], sums_two[images : 2 * images]
    scale_grad = crossed * vectors[3] + shift_grad * vectors[4]
    embed_grad = jnp.dot(
        embed_rows,
        jnp.concatenate((scale_grad, shift_grad), axis=0),
        precision=lax.Precision.HIGHEST,
    )
    ctx_all = ctx_all[:, :, :, :CTX].reshape(images, heads, 2, HEAD_DIM, CTX)
    context_grad = jnp.dot(
        ctx_rows,
        jnp.transpose(ctx_all, (2, 0, 4, 1, 3)).reshape(-1, channels),
        preferred_element_type=F32,
    )
    ctx_value_bias = jnp.sum(ctx_all[:, :, 1].astype(F32), axis=(0, 3)).reshape(1, channels)

    squared = jnp.zeros((1, channels), F32)
    for member in (embed_grad, context_grad):
        squared = squared + jnp.sum((member * member).reshape(-1, channels), axis=0)[None]
    conv_share = (9, C // row_count, channels)
    two_sum, qkv_sum, out_sum, one_sum, payload = local_call(
        finish_kernel,
        [
            out(conv_share, F32),
            out((3,) + conv_share[1:], F32),
            out((1,) + conv_share[1:], F32),
            out(conv_share, F32),
            out((-(-(2 * images + 2) // 8) * 8, channels), F32),
        ],
        two_total,
        *one_terms,
        squared,
        sums,
        conv_one_bias,
    )
    out_sum = turn_back(out_sum, row_count, chan_count)[0]
    third = rows_sum(payload)
    (pixel_grad,) = local_call(
        back_one_kernel,
        [out(act, F32)],
        partial,
        pixels,
        stats_one,
        third,
        vectors,
    )
    vector_grad, squares = local_call(
        vector_kernel,
        [out((14, channels), F32), out((8, channels), F32)],
        third,
        second,
        sums_three,
        mod,
        vectors,
        ctx_value_bias,
    )
    squares = [squares] + [swap(squares, "chan", k) for k in (1, 2, 3)]
    squares[0] = after(squares[0], activations, pixel_grad)

    def turn(x):
        return jnp.transpose(x, (1, 0, 2))

    def flat_rows(x):
        return x.reshape(-1, x.shape[2])

    weights = (
        (conv_first, conv_first_moment, conv_first_square, one_sum),
        (conv_second, conv_second_moment, conv_second_square, two_sum),
        (turn(qkv_weight), turn(qkv_weight_moment), turn(qkv_weight_square), qkv_sum),
        (out_weight, out_weight_moment, out_weight_square, out_sum),
        (flat_rows(embed_weight), flat_rows(embed_weight_moment), flat_rows(embed_weight_square), embed_grad),
        (
            flat_rows(context_weight),
            flat_rows(context_weight_moment),
            flat_rows(context_weight_square),
            context_grad,
        ),
        (vectors, vectors_moment, vectors_square, vector_grad),
    )
    outs = [out((1, channels), F32)]
    for weight, *_ in weights:
        outs += [out(weight.shape, F32)] * 3 + [out(weight.shape, BF)]
    operands = [a for group in weights for a in group]
    norm, *updated = local_call(
        update_kernel,
        outs[:-1],
        *squares,
        *(a if i % 4 == 3 else Far(a) for i, a in enumerate(operands)),
        scratch=[pltpu.VMEM(a.shape, F32) for i, a in enumerate(operands) if i % 4 < 3],
        copies=3 * len(weights),
        limit=24,
    )
    for i in (8, 9, 10, 11):
        updated[i] = turn(updated[i])
    for i in range(16, 24):
        updated[i] = updated[i].reshape(-1, 2, channels)
    return (activations, pixel_grad, norm[0, 0], *updated)


def solution(mesh):
    act = P("rows", None, None, "chan")
    conv = P(None, "rows", "chan")
    wide = P("rows", None, "chan")
    flat = P("rows", "chan")
    vec = P(None, "chan")
    weights = (conv, conv, wide, flat, wide, wide)
    in_specs = (act, act) + (P(),) * 5 + tuple(s for w in weights for s in (w,) * 3) + (vec,) * 3
    out_specs = (act, act, P()) + tuple(s for w in weights for s in (w,) * 4) + (vec,) * 3
    return jax.shard_map(body, mesh=mesh, in_specs=in_specs, out_specs=out_specs, check_vma=False)
```

```python
import functools
import math

import jax
import jax.numpy as jnp
from jax import lax
from jax.experimental import pallas as pl
from jax.experimental.pallas import tpu as pltpu
from jax.sharding import PartitionSpec as P

C = 512
GROUPS = 32
HEAD_DIM = 64
EMB = 2048
DCTX = 2048
IMG_H = 64
IMG_W = 64
CLIP_TOK = 4
STEP = 10
CTX = 81
CTX_PAD = 128
GROUP_SIZE = C // GROUPS
GROUP_COUNT = IMG_H * IMG_W * GROUP_SIZE
LOG2E = 1.4426950408889634
BF = jnp.bfloat16
F32 = jnp.float32
ORDER = (0, 1, 3, 2)

clip_limit = 1.0


def swap(x, axis, distance):
    size = lax.axis_size(axis)
    return lax.ppermute(x, axis, [(i, i ^ distance) for i in range(size)])


def rows_sum(x, first=None):
    size = lax.axis_size("rows")
    x = x + swap(x, "rows", 1) if first is None else first
    step = 2
    while step < size:
        if step * 4 <= size:
            one, two, three = (swap(x, "rows", step * k) for k in (1, 2, 3))
            x = (x + one) + (two + three)
            step *= 4
        else:
            x = x + swap(x, "rows", step)
            step *= 2
    return x


def chan_blocks(x, *beside):
    far = swap(x, "chan", 3)
    near = swap(x, "chan", 1)
    return (x, near, far, swap(after(far, *beside), "chan", 1))


def chan_scatter(own, near, cross, far):
    cross = swap(cross, "chan", 1)
    near = swap(near, "chan", 1)
    return own, near, swap((far + cross.astype(F32)).astype(BF), "chan", 3)


def rims(blocks):
    size = lax.axis_size("rows")
    even = lax.axis_index("rows") % 2 == 0
    top = jnp.stack([x[0] for x in blocks])
    bottom = jnp.stack([x[-1] for x in blocks])
    inside = swap(jnp.where(even, bottom, top), "rows", 1)
    pairs = [(i, i + 1) for i in range(1, size - 1, 2)]
    outside = jnp.where(even, top, bottom)
    outside = lax.ppermute(outside, "rows", pairs + [(j, i) for i, j in pairs])
    shape = (len(blocks), -1, inside.shape[-1])
    return inside.reshape(shape), outside.reshape(shape)


def after(x, *earlier):
    return lax.optimization_barrier((x, *earlier))[0]


def pick(x, index, axis=0):
    return lax.dynamic_index_in_dim(x, index, axis, keepdims=False)


def weight_scatter(mine, other):
    count = mine.shape[0]
    shape = mine.shape[1:]
    total, *low = local_call(
        scatter_kernel, [out(shape, F32)] + [out(shape, BF)] * (count - 1), mine, other
    )
    return [total] + [swap(low[k - 1], "rows", 2 * k) for k in range(1, count)]


class Far:
    def __init__(self, array):
        self.array = array


def near_rows(*arrays):
    return tuple(a.reshape(math.prod(a.shape[:-1]), a.shape[-1]) for a in arrays)


def far_rows(*arrays):
    return tuple(Far(a.reshape(math.prod(a.shape[:-1]), a.shape[-1])) for a in arrays)


def local_call(kernel, outs, *args, scratch=(), copies=0, flops=0, limit=0):
    arrays = [a.array if isinstance(a, Far) else a for a in args]

    def spec(a):
        if isinstance(a, Far):
            return pl.BlockSpec(memory_space=pl.ANY)
        return pl.BlockSpec(memory_space=pltpu.SMEM if a.dtype == jnp.int32 else pltpu.VMEM)

    size = sum(math.prod(a.shape) * a.dtype.itemsize for a in (*arrays, *outs))
    scratch = list(scratch)
    if copies:
        scratch.append(pltpu.SemaphoreType.DMA((copies,)))
    return pl.pallas_call(
        kernel,
        out_shape=tuple(outs),
        in_specs=[spec(a) for a in args],
        out_specs=tuple(pl.BlockSpec(memory_space=pltpu.VMEM) for _ in outs),
        scratch_shapes=scratch,
        compiler_params=pltpu.CompilerParams(vmem_limit_bytes=(limit or (56 if copies else 50)) * 1024 * 1024),
        cost_estimate=pl.CostEstimate(flops=1, bytes_accessed=1, transcendentals=0),
    )(*arrays)


def begin(sems, *moves):
    started = []
    for i, (source, place) in enumerate(moves):
        copy = pltpu.make_async_copy(source, place, sems.at[i])
        copy.start()
        started.append(copy)
    return started


def fetch(sems, *moves):
    for copy in begin(sems, *moves):
        copy.wait()


def lanes_of(xs, j, start=0, size=None):
    width = xs.shape[1] // 4
    size = xs.shape[0] if size is None else size
    return xs.at[start : start + size, j * width : (j + 1) * width]


def block_moves(xs, blocks, start=0):
    return [(x, lanes_of(xs, j, start, x.shape[0])) for j, x in enumerate(blocks)]


def put_rims(xs, zi, inside, outside):
    count, span, width = inside.shape
    last = xs.shape[0] - span
    for j in range(count):
        lanes = slice(j * width, (j + 1) * width)
        xs[pl.ds(pl.multiple_of((1 - zi[4]) * last, span), span), lanes] = inside[j]
        xs[pl.ds(pl.multiple_of(zi[4] * last, span), span), lanes] = outside[j]


def out(shape, dtype):
    return jax.ShapeDtypeStruct(shape, dtype)


def nn(a, b):
    return lax.dot_general(a, b, (((1,), (0,)), ((), ())), preferred_element_type=F32)


def nt(a, b):
    return lax.dot_general(a, b, (((1,), (1,)), ((), ())), preferred_element_type=F32)


def group_mean(x):
    width = x.shape[1]
    left = lax.broadcasted_iota(jnp.int32, (width, width), 0) // GROUP_SIZE
    right = lax.broadcasted_iota(jnp.int32, (width, width), 1) // GROUP_SIZE
    same = (left == right).astype(F32)
    total = lax.dot_general(
        x, same, (((1,), (0,)), ((), ())), precision=lax.Precision.HIGHEST, preferred_element_type=F32
    )
    return total * (1.0 / GROUP_COUNT)


def moments(sums, images):
    means = group_mean(sums)
    average = means[:images]
    return average, lax.rsqrt(means[images:] - average * average + 1e-05)


def image_of(ref, b):
    rows, _, width, channels = ref.shape
    return ref[:, b].reshape(rows * width, channels)


def put_image(ref, b, value):
    rows, _, width, channels = ref.shape
    ref[:, b] = value.reshape(rows, width, channels).astype(ref.dtype)


def column_sum(x):
    return jnp.sum(x, axis=0, keepdims=True)


def silu(z):
    return z * jax.nn.sigmoid(z)


def silu_slope(z):
    s = jax.nn.sigmoid(z)
    return s * (1.0 + z * (1.0 - s))


def put_sums(sums, b, images, v, w):
    sums[b : b + 1] = column_sum(v)
    sums[images + b : images + b + 1] = column_sum(v * w)


def start_kernel(pixels, sums):
    images = pixels.shape[1]
    for b in range(images):
        v = image_of(pixels, b)
        put_sums(sums, b, images, v, v)


def act_one_kernel(x, sums, vec, o):
    images = x.shape[1]
    average, inverse = moments(sums[...], images)
    for b in range(images):
        xhat = (image_of(x, b) - average[b : b + 1]) * inverse[b : b + 1]
        put_image(o, b, silu(xhat * vec[0:1] + vec[1:2]))


def shaped_of(xhat, mod, vec, b, images):
    scale = 1.0 + (mod[b : b + 1] + vec[12:13])
    shift = mod[images + b : images + b + 1] + vec[13:14]
    return (xhat * vec[3:4] + vec[4:5]) * scale + shift


def act_two_kernel(x, sums, mod, vec, o):
    images = x.shape[1]
    average, inverse = moments(sums[...], images)
    for b in range(images):
        xhat = (image_of(x, b) - average[b : b + 1]) * inverse[b : b + 1]
        put_image(o, b, silu(shaped_of(xhat, mod, vec, b, images)))


def norm_three_kernel(x, sums, vec, o):
    images = x.shape[1]
    average, inverse = moments(sums[...], images)
    for b in range(images):
        xhat = (image_of(x, b) - average[b : b + 1]) * inverse[b : b + 1]
        put_image(o, b, xhat * vec[6:7] + vec[7:8])


def rows_of(z, j, width):
    return pl.ds(pl.multiple_of((z ^ ORDER[j]) * width, width), width)


def shifted(x, by, width):
    length = x.shape[0]
    column = lax.broadcasted_iota(jnp.int32, x.shape, 0) % width
    moved = pltpu.roll(x, by % length, 0)
    return jnp.where(column == (0 if by == 1 else width - 1), 0.0, moved)


def conv_taps(blocks, edges, w, extra, zi, xs, rows, span, width):
    z = zi[0]
    if extra:
        w_far, (w, sems) = w, extra
        copies = begin(sems, (w_far.at[0:9], w), *block_moves(xs, blocks, span))
        put_rims(xs, zi, *edges)
        for copy in copies:
            copy.wait()
    else:
        put_rims(xs, zi, *edges)
        for j, x in enumerate(blocks):
            lanes_of(xs, j, span, x.shape[0])[...] = x[...]
    channels = w.shape[2]
    parts = []
    for dx in range(3):
        total = None
        for dy in range(3):
            at = dy * span
            a = xs[at : at + rows * span, :]
            taps = [w[3 * dy + dx, rows_of(z, j, channels), :] for j in range(4)]
            term = nn(a, jnp.concatenate(taps, axis=0))
            total = term if total is None else total + term
        parts.append(total)
    return parts[1] + shifted(parts[0], 1, width) + shifted(parts[2], -1, width)


def conv_one_kernel(zi, x0, x1, x2, x3, e0, e1, w_far, vec, hidden, sums, xs, *extra):
    rows, images, width, channels = hidden.shape
    blocks = (x0, x1, x2, x3)
    result = conv_taps(
        blocks, (e0, e1), w_far, extra, zi, xs, rows, images * width, width
    ) + vec[2:3]
    hidden[...] = result.reshape(hidden.shape)
    for b in range(images):
        v = image_of(hidden, b)
        put_sums(sums, b, images, v, v)


def conv_two_kernel(zi, x0, x1, x2, x3, e0, e1, w_far, vec, pixels, residual, sums, xs, *extra):
    rows, images, width, channels = residual.shape
    blocks = (x0, x1, x2, x3)
    result = conv_taps(
        blocks, (e0, e1), w_far, extra, zi, xs, rows, images * width, width
    ) + vec[5:6]
    residual[...] = pixels[...] + result.reshape(residual.shape)
    for b in range(images):
        v = image_of(residual, b)
        put_sums(sums, b, images, v, v)


def conv_back_kernel(zi, r, e0, e1, w, own, near, cross, far, xs, *, first):
    rows, images, width, channels = r.shape
    span = images * width
    put_rims(xs, zi, e0, e1)
    xs[span : span + rows * span] = r[...].reshape(rows * span, channels)
    wide = xs[...].astype(F32)
    turned = [shifted(wide, -1, width).astype(BF), xs[...], shifted(wide, 1, width).astype(BF)]
    taps = [(dy, dx) for dy in range(3) for dx in range(3)]
    a = jnp.concatenate(
        [turned[dx][(2 - dy) * span : (2 - dy + rows) * span] for dy, dx in taps], axis=1
    )
    for j, part in enumerate((own, near, far, cross)):
        at = rows_of(zi[0], j, channels)
        b = jnp.concatenate([w[first + 3 * dy + dx, at, :] for dy, dx in taps], axis=1)
        part[...] = nt(a, b).astype(part.dtype).reshape(part.shape)


def total_image(terms, b):
    total = image_of(terms[0], b)
    for term in terms[1:]:
        total = total + image_of(term, b).astype(F32)
    return total


def back_two_sum_kernel(t0, t1, t2, vec, hidden, stats, mod, shaped_grad, sums):
    images = hidden.shape[1]
    average, inverse = moments(stats[...], images)
    for b in range(images):
        xhat = (image_of(hidden, b) - average[b : b + 1]) * inverse[b : b + 1]
        g = total_image((t0, t1, t2), b) * silu_slope(shaped_of(xhat, mod, vec, b, images))
        put_image(shaped_grad, b, g)
        put_sums(sums, b, images, g, xhat)


def back_one_sum_kernel(t0, t1, t2, vec, pixels, stats, residual_grad, partial, sums):
    images = pixels.shape[1]
    average, inverse = moments(stats[0 : 2 * images], images)
    for b in range(images):
        xhat = (image_of(pixels, b) - average[b : b + 1]) * inverse[b : b + 1]
        g = total_image((t0, t1, t2), b) * silu_slope(xhat * vec[0:1] + vec[1:2])
        put_image(partial, b, image_of(residual_grad, b) + g * (inverse[b : b + 1] * vec[0:1]))
        put_sums(sums, b, images, g, xhat)


def put_shares(box, zi, tap, grad, base=0):
    share, channels = box.shape[3:]
    each = channels // share
    for j in range(4):
        for i in range(each):
            at = j * channels + i * share
            row = (zi[0] ^ ORDER[j]) * each + i
            box[(row & 1) ^ zi[4], (row >> 1) ^ base, tap] = grad[at : at + share].astype(box.dtype)


def conv_weights(zi, xs, r, box, base=0):
    rows, images, width, channels = r.shape
    span = images * width
    turned = xs[...].T
    wide = r[...].reshape(rows * span, channels).astype(F32)
    three = jnp.concatenate(
        [shifted(wide, -1, width).astype(BF), wide.astype(BF), shifted(wide, 1, width).astype(BF)],
        axis=1,
    )
    for dy in range(3):
        grad = nn(turned[:, dy * span : (dy + rows) * span], three)
        for dx in range(3):
            put_shares(box, zi, 3 * dy + dx, grad[:, dx * channels : (dx + 1) * channels], base)


def weights_two_kernel(
    zi, x0, x1, x2, x3, e0, e1, r, n0, n1, n2, n3, grads, att, c0, c1, c2, c3, loss, mine, other, xs, ns, cs, box, sems
):
    blocks = begin(
        sems,
        *block_moves(xs, (x0, x1, x2, x3), e0.shape[1]),
        *block_moves(ns, (n0, n1, n2, n3)),
        *block_moves(cs, (c0, c1, c2, c3)),
    )
    put_rims(xs, zi, e0, e1)
    for copy in blocks[:4]:
        copy.wait()
    conv_weights(zi, xs, r, box)
    for copy in blocks[4:]:
        copy.wait()
    rows, images, width, columns = grads.shape
    channels = att.shape[3]
    pixels = rows * images * width
    grad = nn(ns[...].T, grads[...].reshape(pixels, columns))
    for s in range(3):
        put_shares(box, zi, 9 + s, grad[:, s * channels : (s + 1) * channels])
    scale = jnp.concatenate([loss[b : b + 1] for b in range(images)], axis=0)
    scale = jnp.concatenate([scale] * 4, axis=1)[None, :, None, :]
    low = (cs[...].reshape(rows, images, width, 4 * channels).astype(F32) * scale).astype(BF)
    grad = nn(att[...].reshape(pixels, channels).T, low.reshape(pixels, 4 * channels))
    by_output = [grad[:, j * channels : (j + 1) * channels] for j in range(4)]
    put_shares(box, zi, 12, jnp.concatenate(by_output, axis=0))
    mine[...] = box[0]
    other[...] = box[1]


def weights_one_kernel(zi, x0, x1, x2, x3, e0, e1, r, mine, other, xs, box, sems):
    copies = begin(sems, *block_moves(xs, (x0, x1, x2, x3), e0.shape[1]))
    put_rims(xs, zi, e0, e1)
    for copy in copies:
        copy.wait()
    conv_weights(zi, xs, r, box, zi[1])
    mine[...] = box[0]
    other[...] = box[1]


def pair_sum_kernel(mine, other, o):
    o[...] = (mine[...].astype(F32) + other[...].astype(F32)).astype(BF)


def scatter_kernel(mine, other, total, *low):
    total[...] = mine[0].astype(F32) + other[0].astype(F32)
    for k, o in enumerate(low):
        o[...] = (mine[k + 1].astype(F32) + other[k + 1].astype(F32)).astype(BF)


def put_heads(scratch, leading, value, b, heads):
    turned = value.T.astype(scratch.dtype)
    for h in range(heads):
        scratch[b * heads + h, leading] = turned[h * HEAD_DIM : (h + 1) * HEAD_DIM]


def project_kernel(*refs, base):
    zi, w_far, vec, grads, blocks = refs[0], refs[1], refs[2], refs[3], refs[4:8]
    outs, (xs, w, scratch, sems) = refs[8:-4], refs[-4:]
    fetch(sems, (w_far.at[base : base + 3], w), *block_moves(xs, blocks))
    tokens = outs[0].shape[2]
    channels = w.shape[2]
    heads = channels // HEAD_DIM
    images = len(outs) // heads
    rows = xs.shape[0] // (images * IMG_W)
    a = xs[...]
    for s in range(3):
        rows_in = [w[s, rows_of(zi[0], j, channels), :] for j in range(4)]
        value = nn(a, jnp.concatenate(rows_in, axis=0))
        if s != 1:
            at = 8 if s == 0 else 9
            value = value + vec[at : at + 1]
        split = value.reshape(rows, images, IMG_W, channels)
        for b in range(images):
            put_heads(scratch, s, split[:, b].reshape(tokens, channels), b, heads)
    for k, o in enumerate(outs):
        o[0:3] = scratch[zi[1] ^ k]
        o[3] = grads[zi[1] ^ k, 0]


def output_grad_kernel(c0, c1, c2, c3, w0, w1, w2, w3, loss, o, xs, sems):
    fetch(sems, *block_moves(xs, (c0, c1, c2, c3)))
    images, channels = loss.shape
    heads = channels // HEAD_DIM
    tokens = o.shape[3]
    turned = jnp.concatenate([w[...] for w in (w0, w1, w2, w3)], axis=1)
    wide = xs[...].reshape(tokens // IMG_W, images, IMG_W, 4 * channels)
    for b in range(images):
        scale = jnp.concatenate([loss[b : b + 1]] * 4, axis=1)
        low = (wide[:, b].reshape(tokens, 4 * channels).astype(F32) * scale).astype(BF)
        put_heads(o, 0, nt(low, turned), b, heads)


def attention_kernel(*refs, chunk, count, block):
    live, ctx_ref = refs[0], refs[1]
    mine, sibs = (refs[2 + i * count : 2 + (i + 1) * count] for i in range(2))
    oq_ref, own_ref, other_ref = refs[2 + 2 * count : 5 + 2 * count]
    q_s, do_s, kt_s, k_s, v_s, s_s, p_s, acc_s = refs[5 + 2 * count :]
    step = pl.program_id(0)
    last = pl.num_programs(0) - 1
    tokens = mine[0].shape[2]
    depth = HEAD_DIM
    queries = block
    half = count * tokens
    keys = 2 * half
    extra = ctx_ref.shape[2]

    @pl.when(step == 0)
    def _():
        for k in range(count):
            lanes = slice(k * tokens, (k + 1) * tokens)
            q_s[:, lanes] = mine[k][0]
            do_s[:, lanes] = mine[k][3]
            kt_s[:, :, lanes] = mine[k][1:3]
            kt_s[:, :, half + k * tokens : half + (k + 1) * tokens] = sibs[k][1:3]
        kt_s[:, :, keys:] = ctx_ref[...]
        k_s[...] = kt_s[0].T
        v_s[...] = kt_s[1].T
        acc_s[...] = jnp.zeros_like(acc_s)

    here = pl.ds(pl.multiple_of(step * block, block), block)
    q = q_s[:, here]
    do = do_s[:, here]
    spans = [(i * chunk, chunk) for i in range(keys // chunk)] + [(keys, extra)]
    highest = None
    for at, size in spans:
        s = nn(k_s[at : at + size], q)
        if at == keys:
            position = lax.broadcasted_iota(jnp.int32, s.shape, 0)
            s = jnp.where(position < live[0], s, -1e30)
        s_s[at : at + size] = s
        top = jnp.max(s.reshape(size // 8, 8, queries), axis=0)
        highest = top if highest is None else jnp.maximum(highest, top)
    factor = 0.125 * LOG2E
    peak = jnp.max(highest, axis=0, keepdims=True) * factor
    weight_sum = jnp.zeros((8, queries), F32)
    mixture = jnp.zeros((depth, queries), F32)
    for at, size in spans:
        p = jnp.exp2(s_s[at : at + size] * factor - peak)
        weight_sum = weight_sum + jnp.sum(p.reshape(size // 8, 8, queries), axis=0)
        low = p.astype(BF)
        p_s[at : at + size] = low
        mixture = mixture + nn(kt_s[1, :, at : at + size], low)
    inverse = 1.0 / jnp.sum(weight_sum, axis=0, keepdims=True)
    attended = mixture * inverse
    oq_ref[0] = attended.astype(BF)
    delta = jnp.sum(do.astype(F32) * attended, axis=0, keepdims=True)
    do_scaled = (do.astype(F32) * inverse).astype(BF)
    q_scaled = (q.astype(F32) * (inverse * 0.125)).astype(BF)
    query_grad = jnp.zeros((depth, queries), F32)
    for at, size in spans:
        dprob = nn(v_s[at : at + size], do)
        low = p_s[at : at + size]
        dscore = (low.astype(F32) * (dprob - delta)).astype(BF)
        query_grad = query_grad + nn(kt_s[0, :, at : at + size], dscore)
        acc_s[0, :, at : at + size] += nt(q_scaled, dscore)
        acc_s[1, :, at : at + size] += nt(do_scaled, low)
    oq_ref[1] = (query_grad * (inverse * 0.125)).astype(BF)

    @pl.when(step == last)
    def _():
        own_ref[:, :, 0:half] = acc_s[:, :, 0:half].astype(BF)
        own_ref[:, :, half:] = acc_s[:, :, keys:].astype(BF)
        other_ref[...] = acc_s[:, :, half:].astype(BF)


def attention(live, ctx, mine, sibs):
    count = len(mine)
    _, depth, tokens = mine[0].shape
    queries = count * tokens
    total = 2 * queries + ctx.shape[2]
    block = min(1024, queries)
    chunk = min(256, 2 * queries)

    def whole(a):
        return pl.BlockSpec(a.shape, lambda i: (0,) * len(a.shape))

    outs = (
        out((2, depth, queries), BF),
        out((2, depth, queries + ctx.shape[2]), BF),
        out((2, depth, queries + ctx.shape[2]), BF),
    )
    arrays = (ctx, *mine, *sibs)
    return pl.pallas_call(
        functools.partial(attention_kernel, chunk=chunk, count=count, block=block),
        grid=(queries // block,),
        in_specs=[pl.BlockSpec(memory_space=pltpu.SMEM)] + [whole(a) for a in arrays],
        out_specs=(
            pl.BlockSpec((2, depth, block), lambda i: (0, 0, i)),
            whole(outs[1]),
            whole(outs[2]),
        ),
        out_shape=outs,
        scratch_shapes=[
            pltpu.VMEM((depth, queries), BF),
            pltpu.VMEM((depth, queries), BF),
            pltpu.VMEM((2, depth, total), BF),
            pltpu.VMEM((total, depth), BF),
            pltpu.VMEM((total, depth), BF),
            pltpu.VMEM((total, block), F32),
            pltpu.VMEM((total, block), BF),
            pltpu.VMEM((2, depth, total), F32),
        ],
        compiler_params=pltpu.CompilerParams(
            vmem_limit_bytes=56 * 1024 * 1024, dimension_semantics=("arbitrary",)
        ),
        cost_estimate=pl.CostEstimate(
            flops=12 * depth * queries * total, bytes_accessed=8 * depth * total, transcendentals=queries * total
        ),
    )(live, *arrays)


def merge_kernel(oq_far, own_far, other_far, *refs):
    oq, own, other, sems = refs[-4:]
    outs = refs[:-4]
    count = len(outs) // 2
    fetch(sems, (oq_far, oq), (own_far, own), (other_far, other))
    tokens = oq.shape[2] // count
    both = (own[...].astype(F32) + other[...].astype(F32)).astype(BF)
    for k in range(count):
        lanes = slice(k * tokens, (k + 1) * tokens)
        outs[k][0] = oq[1, :, lanes]
        outs[k][1:3] = both[:, :, lanes]
        outs[count + k][:, 0:tokens] = oq[0, :, lanes]
        for s in range(2):
            at = tokens + s * CTX_PAD
            outs[count + k][:, at : at + CTX_PAD] = both[s, :, count * tokens :]


def back_project_kernel(*refs, base, count):
    zi, w_far, pieces = refs[0], refs[1], refs[2 : 2 + count]
    grads, part_own, part_near, part_cross, part_far, biases = refs[2 + count : -3]
    rec, w, sems = refs[-3:]
    fetch(sems, (w_far.at[base : base + 3], w))
    rows, images, width, channels = part_own.shape
    heads = channels // HEAD_DIM
    for k in range(count):
        rec[zi[1] ^ k] = pieces[k][...]
    for b in range(images):
        for s in range(3):
            blocks = [rec[b * heads + h, s] for h in range(heads)]
            value = jnp.concatenate(blocks, axis=0).T.reshape(rows, width, channels)
            grads[:, b, :, s * channels : (s + 1) * channels] = value
    flat = grads[...].reshape(rows * images * width, 3 * channels)
    for j, part in enumerate((part_own, part_near, part_far, part_cross)):
        at = rows_of(zi[0], j, channels)
        taps = jnp.concatenate([w[s, at, :] for s in range(3)], axis=1)
        part[...] = nt(flat, taps).astype(part.dtype).reshape(part.shape)
    wide = flat.astype(F32)
    biases[0:1] = column_sum(wide[:, 0:channels])
    biases[1:2] = column_sum(wide[:, 2 * channels :])


def attended_kernel(*refs):
    zi, pieces = refs[0], refs[1:-3]
    attended, ctx, rec = refs[-3:]
    rows, images, width, channels = attended.shape
    heads = channels // HEAD_DIM
    tokens = rows * width
    for k, piece in enumerate(pieces):
        rec[zi[1] ^ k] = piece[...]
    for b in range(images):
        blocks = [rec[b * heads + h, :, 0:tokens] for h in range(heads)]
        attended[:, b] = jnp.concatenate(blocks, axis=0).T.reshape(rows, width, channels)
    for q in range(len(pieces)):
        for s in range(2):
            at = tokens + s * CTX_PAD
            ctx[q, s] = rec[q, :, at : at + CTX_PAD]


def out_project_kernel(zi, x0, x1, x2, x3, w_far, vec, residual, o, xs, w, sems, *, tap):
    fetch(sems, (w_far.at[tap : tap + 1], w), *block_moves(xs, (x0, x1, x2, x3)))
    channels = w.shape[2]
    rows_in = [w[0, rows_of(zi[0], j, channels), :] for j in range(4)]
    value = nn(xs[...], jnp.concatenate(rows_in, axis=0)) + vec[10:11]
    o[...] = (residual[...] + value.reshape(o.shape)).astype(BF)


def back_three_sum_kernel(t0, t1, t2, residual, stats, g_out, sums):
    images = residual.shape[1]
    average, inverse = moments(stats[...], images)
    for b in range(images):
        g = image_of(t0, b).astype(F32) + image_of(t1, b).astype(F32) + image_of(t2, b).astype(F32)
        xhat = (image_of(residual, b) - average[b : b + 1]) * inverse[b : b + 1]
        put_image(g_out, b, g)
        put_sums(sums, b, images, g, xhat)


def back_three_kernel(g0, x0, c0, stats, sums, vec, loss, residual_grad, low, bias):
    images = x0.shape[1]
    average, inverse = moments(stats[...], images)
    means = group_mean(sums[...] * vec[6:7])
    total = None
    for b in range(images):
        xhat = (image_of(x0, b) - average[b : b + 1]) * inverse[b : b + 1]
        g = image_of(g0, b) * vec[6:7] - means[b : b + 1] - xhat * means[images + b : images + b + 1]
        g = image_of(c0, b).astype(F32) * loss[b : b + 1] + inverse[b : b + 1] * g
        put_image(residual_grad, b, g)
        put_image(low, b, g)
        part = column_sum(g)
        total = part if total is None else total + part
    bias[...] = total


def back_two_kernel(g0, x0, stats, sums, mod, vec, low, bias):
    images = x0.shape[1]
    average, inverse = moments(stats[...], images)
    gains = [vec[3:4] * (1.0 + (mod[b : b + 1] + vec[12:13])) for b in range(images)]
    means = group_mean(sums[0 : 2 * images] * jnp.concatenate(gains + gains, axis=0))
    total = None
    for b in range(images):
        xhat = (image_of(x0, b) - average[b : b + 1]) * inverse[b : b + 1]
        g = image_of(g0, b) * gains[b]
        g = g - means[b : b + 1] - xhat * means[images + b : images + b + 1]
        g = inverse[b : b + 1] * g
        put_image(low, b, g)
        part = column_sum(g)
        total = part if total is None else total + part
    bias[...] = total


def back_one_kernel(partial, pixels, stats, sums, vec, pixel_grad):
    images = pixels.shape[1]
    average, inverse = moments(stats[0 : 2 * images], images)
    means = group_mean(sums[0 : 2 * images] * vec[0:1])
    for b in range(images):
        slope = inverse[b : b + 1] * inverse[b : b + 1] * means[images + b : images + b + 1]
        level = inverse[b : b + 1] * means[b : b + 1] - average[b : b + 1] * slope
        put_image(pixel_grad, b, image_of(partial, b) - (image_of(pixels, b) * slope + level))


RATES = (0.02, 0.02, 0.08, 1.0, 0.02, 0.04, 1.0)


def finish_kernel(*refs):
    terms, (squares, sums, bias, two_sum, qkv_sum, out_sum, one_sum, payload) = refs[:-8], refs[-8:]
    squared = squares[...]
    at = 0
    for o in (two_sum, qkv_sum, out_sum, one_sum):
        if o is one_sum:
            total = terms[1][...]
            for term in terms[2:]:
                total = total + term[...].astype(F32)
        else:
            total = terms[0][at : at + o.shape[0]].astype(F32)
            at += o.shape[0]
        o[...] = total
        squared = squared + column_sum((total * total).reshape(-1, total.shape[-1]))
    count = sums.shape[0]
    payload[0:count] = sums[...]
    payload[count : count + 1] = bias[...]
    payload[count + 1 : count + 2] = squared
    payload[count + 2 :] = jnp.zeros((payload.shape[0] - count - 2, payload.shape[1]), F32)


def vector_kernel(third, second, sums_three, mod, vec, ctx, grad, squares):
    images = sums_three.shape[0] // 2

    def total(ref, at):
        return column_sum(ref[at : at + images])

    scale = 1.0 + (mod[0:images] + vec[12:13])
    shift_grad = second[0:images]
    crossed = second[images : 2 * images]
    scale_grad = crossed * vec[3:4] + shift_grad * vec[4:5]
    at = 2 * images
    rows = (
        total(third, images),
        total(third, 0),
        third[at : at + 1],
        column_sum(scale * crossed),
        column_sum(scale * shift_grad),
        second[at : at + 1],
        total(sums_three, images),
        total(sums_three, 0),
        second[at + 1 : at + 2],
        second[at + 2 : at + 3],
        second[at + 3 : at + 4],
        ctx[...],
        column_sum(scale_grad),
        column_sum(shift_grad),
    )
    squared = third[at + 1 : at + 2]
    for i, row in enumerate(rows):
        grad[i : i + 1] = row
        squared = squared + row * row
    squares[...] = jnp.broadcast_to(squared, squares.shape)


def update_kernel(*refs):
    count = len(RATES)
    squares, given = refs[0:4], refs[4 : 4 + 4 * count]
    made, held, sems = refs[4 + 4 * count : -3 * count - 1], refs[-3 * count - 1 : -1], refs[-1]
    far = [a for i, a in enumerate(given) if i % 4 < 3]
    arriving = begin(sems, *zip(far, held))
    near = squares[0][0:1] + squares[1][0:1]
    total = jnp.sum(near + (squares[2][0:1] + squares[3][0:1]), axis=1, keepdims=True)
    norm = jnp.sqrt(total)
    made[0][...] = jnp.broadcast_to(norm, made[0].shape)
    factor = jnp.minimum(1.0, clip_limit / norm)
    at = 1
    for i, rate in enumerate(RATES):
        for copy in arriving[3 * i : 3 * i + 3]:
            copy.wait()
        weight, moment, square = held[3 * i : 3 * i + 3]
        gradient = given[4 * i + 3]
        decay = 0.0 if i == count - 1 else 0.01
        scale = factor.reshape((1,) * (len(weight.shape) - 2) + factor.shape)
        new = adamw(weight[...], moment[...], square[...], gradient[...] * scale, rate, decay)
        for value in new:
            made[at][...] = value
            at += 1
        if i < count - 1:
            made[at][...] = new[0].astype(BF)
            at += 1


def adamw(weight, moment, square, gradient, step_rate, weight_decay):
    moment_new = 0.9 * moment + 0.1 * gradient
    square_new = 0.999 * square + 0.001 * gradient * gradient
    corrected = moment_new / (1.0 - 0.9**STEP)
    scaled = square_new / (1.0 - 0.999**STEP)
    weight_new = weight - step_rate * (
        corrected / (jnp.sqrt(scaled) + 1e-08) + weight_decay * weight
    )
    return (weight_new, moment_new, square_new)


def turn_moves(row_count, chan_count):
    share = row_count // chan_count
    return [
        (r * chan_count + z, (z * share + r % share) * chan_count + r // share)
        for r in range(row_count)
        for z in range(chan_count)
    ]


def turn_back(x, row_count, chan_count):
    moves = [(j, i) for i, j in turn_moves(row_count, chan_count)]
    return lax.ppermute(x, ("rows", "chan"), moves)


def body(
    pixels,
    cotangent,
    loss_weight,
    timesteps,
    clip_embed,
    context,
    text_len,
    conv_first,
    conv_first_moment,
    conv_first_square,
    conv_second,
    conv_second_moment,
    conv_second_square,
    qkv_weight,
    qkv_weight_moment,
    qkv_weight_square,
    out_weight,
    out_weight_moment,
    out_weight_square,
    embed_weight,
    embed_weight_moment,
    embed_weight_square,
    context_weight,
    context_weight_moment,
    context_weight_square,
    vectors,
    vectors_moment,
    vectors_square,
):
    row_count = lax.axis_size("rows")
    chan_count = lax.axis_size("chan")
    row = lax.axis_index("rows")
    chan = lax.axis_index("chan")
    local_rows, images, width, channels = pixels.shape
    heads = channels // HEAD_DIM
    pairs = images * heads
    assert chan_count == 4 and row_count == 2 * pairs
    pair = row // 2
    zi = jnp.stack(
        [chan, pair, row, row_count - 1 - row, row % 2]
    ).astype(jnp.int32)
    act = (local_rows, images, width, channels)
    edge_rows = (local_rows + 2) * images * width
    xs = pltpu.VMEM((edge_rows, C), BF)
    flat = pltpu.VMEM((local_rows * images * width, C), BF)
    taps = pltpu.VMEM((9, C, channels), BF)
    conv_flops = 2 * local_rows * images * width * 9 * C * channels

    (sums,) = local_call(start_kernel, [out((2 * images, channels), F32)], pixels)
    loss = jnp.broadcast_to(loss_weight[:, None], (images, channels))
    cot = after(cotangent, sums)
    cot_near, cot_far = swap(cot, "chan", 1), swap(cot, "chan", 3)

    sums_shape = out((2 * images, channels), F32)
    by_chip = sums + swap(sums, "rows", 1)
    stats_one = rows_sum(sums, by_chip)

    one_full = lax.all_gather(after(conv_first, by_chip).astype(BF), "rows", axis=1, tiled=True)
    (active_one,) = local_call(
        act_one_kernel, [out(act, BF)], pixels, after(stats_one, cot_near, cot_far), vectors
    )
    blocks_one = chan_blocks(active_one)
    arrived = blocks_one[1:3]
    two_low = after(conv_second, *arrived).astype(BF)
    qkv_low = jnp.transpose(after(qkv_weight, *arrived), (1, 0, 2)).astype(BF)
    out_low = after(out_weight, *arrived).astype(BF)[None]
    two_full = lax.all_gather(
        jnp.concatenate([two_low, qkv_low, out_low], axis=0), "rows", axis=1, tiled=True
    )
    ctx_full = lax.all_gather(
        after(context_weight, *arrived).astype(BF), "rows", axis=0, tiled=True
    )

    share = EMB // row_count
    index = row * share + jnp.arange(share, dtype=jnp.int32)
    half_width = EMB // 2
    frequency = jnp.exp(-math.log(10000.0) * (index % half_width).astype(F32) / half_width)
    phases = after(timesteps, active_one).astype(F32)[:, None] * frequency[None, :]
    features = jnp.where(index[None, :] < half_width, jnp.cos(phases), jnp.sin(phases))
    clip_share = lax.dynamic_slice_in_dim(clip_embed, row * share, share, 1)
    embedding = jax.nn.silu(features + clip_share).astype(BF)
    both = jnp.eye(2, dtype=F32)[None, :, :, None]
    embed_rows = (embedding.astype(F32).T[:, None, None, :] * both).reshape(2 * share, 2 * images)
    modulation = jnp.einsum(
        "be,esc->sbc",
        embedding,
        after(embed_weight, active_one).astype(BF),
        preferred_element_type=F32,
    ).reshape(2 * images, channels)

    cot_cross = swap(after(cot_far, *blocks_one), "chan", 1)
    rims_one = rims(blocks_one)
    hidden, sums = local_call(
        conv_one_kernel,
        [out(act, F32), sums_shape],
        zi,
        *near_rows(*blocks_one),
        *rims_one,
        one_full,
        vectors,
        scratch=[xs],
        flops=conv_flops,
    )
    stats_two = rows_sum(jnp.concatenate([after(sums, cot_cross), modulation], axis=0))
    stats_two, mod = stats_two[: 2 * images], stats_two[2 * images :]
    (active_two,) = local_call(
        act_two_kernel, [out(act, BF)], hidden, stats_two, mod, vectors
    )

    blocks_two = chan_blocks(active_two)

    def out_rows(owner):
        return lax.dynamic_slice_in_dim(two_full[12], owner * channels, channels, 0)

    out_part = [out_rows(chan)] + [swap(out_rows(chan ^ k), "chan", k) for k in ORDER[1:]]
    tokens = local_rows * width
    cots = (cotangent, cot_near, cot_far, cot_cross)
    (attended_grad,) = local_call(
        output_grad_kernel,
        [out((pairs, 1, HEAD_DIM, tokens), BF)],
        *far_rows(*(after(a, active_two) for a in cots)),
        *out_part,
        loss,
        scratch=[flat],
        copies=4,
    )
    ctx_share = DCTX // row_count
    ctx_rows = lax.dynamic_slice_in_dim(context, row * ctx_share, ctx_share, 2)
    ctx_rows = jnp.transpose(ctx_rows, (2, 0, 1)).reshape(ctx_share, 1, 1, -1)
    ctx_rows = (ctx_rows * jnp.eye(2, dtype=BF)[None, :, :, None]).reshape(2 * ctx_share, -1)
    rims_two = rims((after(blocks_two[0], attended_grad), *blocks_two[1:]))
    residual, sums = local_call(
        conv_two_kernel,
        [out(act, F32), sums_shape],
        zi,
        *far_rows(*blocks_two),
        *rims_two,
        Far(two_full),
        after(vectors, ctx_rows, embed_rows),
        pixels,
        scratch=[xs, taps],
        copies=5,
        flops=conv_flops,
    )
    stats_three = rows_sum(sums)
    (normed,) = local_call(norm_three_kernel, [out(act, BF)], residual, stats_three, vectors)
    blocks_three = chan_blocks(normed)

    image, head = pair // heads, pair % heads
    ctx_low = pick(context, image)
    ctx_projected = jnp.einsum("te,esc->sct", ctx_low, ctx_full, preferred_element_type=F32)
    ctx_bias = jnp.stack([jnp.zeros_like(vectors[11]), vectors[11]])[:, :, None]
    ctx_heads = lax.dynamic_slice_in_dim(ctx_projected + ctx_bias, head * HEAD_DIM, HEAD_DIM, 1)
    ctx_heads = jnp.pad(ctx_heads.astype(BF), ((0, 0), (0, 0), (0, CTX_PAD - CTX)))
    live = (CLIP_TOK + pick(text_len, image))[None].astype(jnp.int32)

    pieces = local_call(
        functools.partial(project_kernel, base=9),
        [out((4, HEAD_DIM, tokens), BF)] * pairs,
        zi,
        Far(two_full),
        after(vectors, ctx_heads),
        attended_grad,
        *far_rows(*blocks_three),
        scratch=[
            flat,
            pltpu.VMEM((3, C, channels), BF),
            pltpu.VMEM((pairs, 3, HEAD_DIM, tokens), BF),
        ],
        copies=5,
        flops=conv_flops // 3,
    )
    pieces = [pieces[0]] + [swap(pieces[k], "rows", 2 * k) for k in range(1, pairs)]
    siblings = [swap(piece, "rows", 1) for piece in pieces]

    out_query, own, other = attention(live, ctx_heads, pieces, siblings)
    merged = local_call(
        merge_kernel,
        [out((3, HEAD_DIM, tokens), BF)] * pairs
        + [out((HEAD_DIM, tokens + 2 * CTX_PAD), BF)] * pairs,
        Far(out_query),
        Far(own),
        Far(swap(other, "rows", 1)),
        scratch=[
            pltpu.VMEM(out_query.shape, BF),
            pltpu.VMEM(own.shape, BF),
            pltpu.VMEM(own.shape, BF),
        ],
        copies=3,
    )
    received = [merged[0]] + [swap(merged[k], "rows", 2 * k) for k in range(1, pairs)]

    grads, part_own, part_near, part_cross, part_far, qv_bias = local_call(
        functools.partial(back_project_kernel, base=9, count=pairs),
        [
            out((local_rows, images, width, 3 * channels), BF),
            out(act, F32),
            out(act, BF),
            out(act, BF),
            out(act, F32),
            out((2, channels), F32),
        ],
        zi,
        Far(two_full),
        *received,
        scratch=[
            pltpu.VMEM((pairs, 3, HEAD_DIM, tokens), BF),
            pltpu.VMEM((3, C, channels), BF),
        ],
        copies=1,
        flops=conv_flops // 3,
    )
    normed_terms = chan_scatter(part_own, part_near, part_cross, part_far)
    late = [after(piece, part_cross) for piece in merged[pairs:]]
    late = [late[0]] + [swap(late[k], "rows", 2 * k) for k in range(1, pairs)]
    normed_grad, sums = local_call(
        back_three_sum_kernel,
        [out(act, F32), sums_shape],
        *normed_terms,
        residual,
        after(stats_three, *late),
    )
    sums_three = rows_sum(sums)
    residual_grad, residual_low, conv_two_bias = local_call(
        back_three_kernel,
        [out(act, F32), out(act, BF), out((1, channels), F32)],
        normed_grad,
        residual,
        cotangent,
        stats_three,
        sums_three,
        vectors,
        loss,
    )
    attended, ctx_all = local_call(
        attended_kernel,
        [out(act, BF), out((pairs, 2, HEAD_DIM, CTX_PAD), BF)],
        zi,
        *late,
        scratch=[pltpu.VMEM((pairs, HEAD_DIM, tokens + 2 * CTX_PAD), BF)],
    )
    weights_scratch = [
        xs,
        flat,
        flat,
        pltpu.VMEM((2, pairs, 13, C // row_count, channels), BF),
    ]
    two_grads = local_call(
        weights_two_kernel,
        [out((pairs, 13, C // row_count, channels), BF)] * 2,
        zi,
        *far_rows(*blocks_two),
        *rims_two,
        residual_low,
        *far_rows(*blocks_three),
        grads,
        attended,
        *far_rows(*cots),
        loss,
        scratch=weights_scratch,
        copies=12,
        flops=conv_flops,
    )
    one_edge = pltpu.VMEM((edge_rows, channels), BF)
    back_parts = [out(act, F32), out(act, BF), out(act, BF), out(act, F32)]
    (two_pairs,) = local_call(
        pair_sum_kernel,
        [out((pairs, 13, C // row_count, channels), BF)],
        two_grads[0],
        swap(two_grads[1], "rows", 1),
    )
    groups = [[2 * p + c for p in range(pairs)] for c in range(2)]
    two_total = lax.psum_scatter(two_pairs, "rows", axis_index_groups=groups)
    parts = local_call(
        functools.partial(conv_back_kernel, first=0),
        back_parts,
        zi,
        residual_low,
        *rims((residual_low,)),
        two_full,
        scratch=[one_edge],
    )
    shaped_grad, sums = local_call(
        back_two_sum_kernel,
        [out(act, F32), sums_shape],
        *chan_scatter(*parts),
        vectors,
        hidden,
        stats_two,
        mod,
    )
    att = after(attended, sums)
    att_near, att_far = swap(att, "chan", 1), swap(att, "chan", 3)
    out_bias = jnp.sum(
        cotangent.astype(F32) * loss_weight[None, :, None, None], axis=(0, 1, 2)
    )[None]
    second = rows_sum(jnp.concatenate([sums, conv_two_bias, qv_bias, out_bias], axis=0))
    sums_two = second[: 2 * images]
    hidden_low, conv_one_bias = local_call(
        back_two_kernel,
        [out(act, BF), out((1, channels), F32)],
        shaped_grad,
        hidden,
        after(stats_two, two_pairs),
        sums_two,
        mod,
        vectors,
    )
    one_grads = local_call(
        weights_one_kernel,
        [out((pairs, 9, C // row_count, channels), BF)] * 2,
        zi,
        *far_rows(*blocks_one),
        *rims_one,
        hidden_low,
        scratch=[xs, pltpu.VMEM((2, pairs, 9, C // row_count, channels), BF)],
        copies=4,
        flops=conv_flops,
    )
    one_terms = weight_scatter(one_grads[0], swap(one_grads[1], "rows", 1))
    parts = local_call(
        functools.partial(conv_back_kernel, first=0),
        back_parts,
        zi,
        after(hidden_low, att_near, att_far),
        *rims((hidden_low,)),
        one_full,
        scratch=[one_edge],
    )
    partial, sums = local_call(
        back_one_sum_kernel,
        [out(act, F32), sums_shape],
        *chan_scatter(*parts),
        after(vectors, *one_terms),
        pixels,
        stats_one,
        residual_grad,
    )

    att_far = after(att_far, sums)
    attended_blocks = (attended, att_near, att_far, swap(att_far, "chan", 1))
    (activations,) = local_call(
        functools.partial(out_project_kernel, tap=12),
        [out(act, BF)],
        zi,
        *far_rows(*attended_blocks),
        Far(two_full),
        vectors,
        residual,
        scratch=[flat, pltpu.VMEM((1, C, channels), BF)],
        copies=5,
    )

    shift_grad, crossed = sums_two[:images], sums_two[images : 2 * images]
    scale_grad = crossed * vectors[3] + shift_grad * vectors[4]
    embed_grad = jnp.dot(
        embed_rows,
        jnp.concatenate((scale_grad, shift_grad), axis=0),
        precision=lax.Precision.HIGHEST,
    )
    ctx_all = ctx_all[:, :, :, :CTX].reshape(images, heads, 2, HEAD_DIM, CTX)
    context_grad = jnp.dot(
        ctx_rows,
        jnp.transpose(ctx_all, (2, 0, 4, 1, 3)).reshape(-1, channels),
        preferred_element_type=F32,
    )
    ctx_value_bias = jnp.sum(ctx_all[:, :, 1].astype(F32), axis=(0, 3)).reshape(1, channels)

    squared = jnp.zeros((1, channels), F32)
    for member in (embed_grad, context_grad):
        squared = squared + jnp.sum((member * member).reshape(-1, channels), axis=0)[None]
    conv_share = (9, C // row_count, channels)
    two_sum, qkv_sum, out_sum, one_sum, payload = local_call(
        finish_kernel,
        [
            out(conv_share, F32),
            out((3,) + conv_share[1:], F32),
            out((1,) + conv_share[1:], F32),
            out(conv_share, F32),
            out((-(-(2 * images + 2) // 8) * 8, channels), F32),
        ],
        two_total,
        *one_terms,
        squared,
        sums,
        conv_one_bias,
    )
    out_sum = turn_back(out_sum, row_count, chan_count)[0]
    third = rows_sum(payload)
    (pixel_grad,) = local_call(
        back_one_kernel,
        [out(act, F32)],
        partial,
        pixels,
        stats_one,
        third,
        vectors,
    )
    vector_grad, squares = local_call(
        vector_kernel,
        [out((14, channels), F32), out((8, channels), F32)],
        third,
        second,
        sums_three,
        mod,
        vectors,
        ctx_value_bias,
    )
    squares = [squares] + [swap(squares, "chan", k) for k in (1, 2, 3)]
    squares[0] = after(squares[0], pixel_grad)

    def turn(x):
        return jnp.transpose(x, (1, 0, 2))

    def flat_rows(x):
        return x.reshape(-1, x.shape[2])

    weights = (
        (conv_first, conv_first_moment, conv_first_square, one_sum),
        (conv_second, conv_second_moment, conv_second_square, two_sum),
        (turn(qkv_weight), turn(qkv_weight_moment), turn(qkv_weight_square), qkv_sum),
        (out_weight, out_weight_moment, out_weight_square, out_sum),
        (flat_rows(embed_weight), flat_rows(embed_weight_moment), flat_rows(embed_weight_square), embed_grad),
        (
            flat_rows(context_weight),
            flat_rows(context_weight_moment),
            flat_rows(context_weight_square),
            context_grad,
        ),
        (vectors, vectors_moment, vectors_square, vector_grad),
    )
    outs = [out((1, channels), F32)]
    for weight, *_ in weights:
        outs += [out(weight.shape, F32)] * 3 + [out(weight.shape, BF)]
    operands = [a for group in weights for a in group]
    norm, *updated = local_call(
        update_kernel,
        outs[:-1],
        *squares,
        *(a if i % 4 == 3 else Far(a) for i, a in enumerate(operands)),
        scratch=[pltpu.VMEM(a.shape, F32) for i, a in enumerate(operands) if i % 4 < 3],
        copies=3 * len(weights),
        limit=24,
    )
    for i in (8, 9, 10, 11):
        updated[i] = turn(updated[i])
    for i in range(16, 24):
        updated[i] = updated[i].reshape(-1, 2, channels)
    return (activations, pixel_grad, norm[0, 0], *updated)


def solution(mesh):
    act = P("rows", None, None, "chan")
    conv = P(None, "rows", "chan")
    wide = P("rows", None, "chan")
    flat = P("rows", "chan")
    vec = P(None, "chan")
    weights = (conv, conv, wide, flat, wide, wide)
    in_specs = (act, act) + (P(),) * 5 + tuple(s for w in weights for s in (w,) * 3) + (vec,) * 3
    out_specs = (act, act, P()) + tuple(s for w in weights for s in (w,) * 4) + (vec,) * 3
    return jax.shard_map(body, mesh=mesh, in_specs=in_specs, out_specs=out_specs, check_vma=False)
```
